128 devices in a mesh: grp: 8 (over y, z_hi), lm: 16 (over x, z_lo, core).
Axes of the slice: x: 4, y: 4, z: 4 (z_hi: 2, z_lo: 2; z = z_hi * 2 + z_lo), core: 2. Of those that a mesh axis runs over, the one named last changes fastest.
Arguments:
- embeddings: bfloat16 [32768, 512], P(('grp', 'lm')), may hold values from -14 to 14
- landmarks: bfloat16 [32768, 512], P('lm'), may hold values from -14 to 14
- start_vectors: float32 [32768, 128], P(('grp', 'lm')), may hold values from -10 to 10
- row_weight: float32 [32768], P(('grp', 'lm')), may hold values from 0.1 to 9
- spread: float32 [1], replicated, may hold values from 11.313708 to 33.941124
Outputs:
- subspace: float32 [32768, 128], P(('grp', 'lm'))
The draws below stay inside these ranges and needn't reach their ends.
All inputs are finite; a program needn't handle non-finite values.
Results may differ from the reference program's by a relative error of at most 0.019.
Values may be sent and summed in bfloat16 or wider, within the bound.
No kernel may reach another device: no remote copies, remote signals or barrier semaphores. Data moves between devices by JAX's collectives and lax.ppermute only.
A program may use at most 128 MiB of HBM per device.

```python
import math
import jax
import jax.numpy as jnp
from jax import lax

D = 512
VECS = 128
ITERS = 2
ROWS = 32768
LANDMARKS = 32768


def draw_row_weight(key, part):
    position = jnp.arange(ROWS, dtype=jnp.float32) / ROWS
    base = jnp.exp(jax.random.uniform(key, (ROWS,), jnp.float32, math.log(0.1), 0.0))
    ramp = jnp.exp(position * math.log(3.0))
    return base * ramp


def feature_rows(key, count, salt):
    inner = jax.random.fold_in(key, salt)
    return jnp.clip(jax.random.normal(inner, (count, D), jnp.float32), -6.0, 6.0)


def draw_embeddings(key, part):
    return feature_rows(key, ROWS, 101).astype(jnp.bfloat16)


def draw_landmarks(key, part):
    return feature_rows(key, LANDMARKS, 202).astype(jnp.bfloat16)


def draw_start_vectors(key, part):
    first, second, third = jax.random.split(jax.random.fold_in(key, 17), 3)
    position = jnp.arange(ROWS, dtype=jnp.float32) / ROWS
    magnitude = jax.random.uniform(second, (1, VECS), jnp.float32, 1.0, 2.0)
    sign = 2.0 * jax.random.randint(third, (1, VECS), 0, 2).astype(jnp.float32) - 1.0
    column_factor = magnitude * sign
    noise = jnp.clip(jax.random.normal(first, (ROWS, VECS), jnp.float32), -6.0, 6.0)
    ramp = 0.5 * jnp.exp(position * math.log(3.0))
    return noise + ramp[:, None] * column_factor


def setup_inputs(seed: int = 0) -> dict:
    key_list = jax.random.split(jax.random.key(seed), 6)
    return {
        "embeddings": draw_embeddings(jax.random.fold_in(key_list[5], 71), 0),
        "landmarks": draw_landmarks(jax.random.fold_in(key_list[5], 71), 0),
        "start_vectors": draw_start_vectors(jax.random.fold_in(key_list[5], 71), 0),
        "row_weight": draw_row_weight(jax.random.fold_in(key_list[5], 71), 0),
        "spread": jnp.clip(jnp.exp(jax.random.uniform(key_list[4], (1,), jnp.float32, math.log(11.313708), math.log(33.941124))), 11.313708, 33.941124),
    }


def unit_rows(values):
    values = values.astype(jnp.float32)
    scale = lax.rsqrt(lax.optimization_barrier(jnp.sum(values * values, axis=1, keepdims=True)) + 1e-06)
    return (values * scale).astype(jnp.bfloat16)

def round_trip(values):
    rounded = lax.optimization_barrier(values.astype(jnp.bfloat16))
    return rounded.astype(jnp.float32)

def reference(embeddings, landmarks, start_vectors, row_weight, spread):
    highest = lax.Precision.HIGHEST
    rows_unit = unit_rows(embeddings).astype(jnp.float32)
    marks_unit = unit_rows(landmarks).astype(jnp.float32)
    total_rows = embeddings.shape[0]
    block = math.gcd(LANDMARKS, 1024)
    marks_blocks = marks_unit.reshape(LANDMARKS // block, block, D)
    gamma = spread[0]
    weight = row_weight.astype(jnp.float32)
    weight_sum = jnp.sum(weight)
    vectors = start_vectors.astype(jnp.float32)
    for step in range(ITERS):
        weighted_full = weight[:, None] * vectors
        weighted = round_trip(weighted_full)
        totals = lax.optimization_barrier(jnp.sum(weighted_full, axis=0))

        def visit(carry, marks):
            raw, shift = carry
            cosine = jnp.dot(rows_unit, marks.T, precision=highest)
            values = jnp.exp(gamma * cosine)
            kernel = round_trip(values)
            means = jnp.dot(weight, values, precision=highest) / weight_sum
            side = jnp.dot(kernel.T, weighted, precision=highest) - means[:, None] * totals[None, :]
            side_b = round_trip(side)
            raw = raw + jnp.dot(kernel, side_b, precision=highest)
            shift = shift + jnp.dot(means, side_b, precision=highest)
            return ((raw, shift), None)
        init = (jnp.zeros((total_rows, VECS), jnp.float32), jnp.zeros((VECS,), jnp.float32))
        (raw, shift), _ = lax.scan(visit, init, marks_blocks)
        image = weight[:, None] * (raw - shift[None, :])
        scale = jnp.sqrt(lax.optimization_barrier(jnp.mean(image * image, axis=0)) + 1e-06)
        vectors = image / scale[None, :]
    return vectors
```

```python
import jax
import jax.numpy as jnp
from jax import lax
from jax.sharding import Mesh
from jax.sharding import PartitionSpec as P

ITERS = 2
AXES = ("y", "zh", "x", "zl", "core")
ROW_AXES = ("x", "zl")
MARK_AXES = ("y", "zh")
F32, B16 = jnp.float32, jnp.bfloat16
DOWN = 2.0**-20
UP = 2.0**20


def unit_rows(values):
    values = values.astype(F32)
    scale = lax.rsqrt(jnp.sum(values * values, axis=1, keepdims=True) + 1e-06)
    return (values * scale).astype(B16)


def split3(values):
    high = lax.reduce_precision(values, 8, 7)
    rest = values - high
    mid = lax.reduce_precision(rest, 8, 7)
    low = rest - mid
    return [high.astype(B16), mid.astype(B16), low.astype(B16)]


def join3(parts):
    parts = parts.astype(F32)
    return (parts[..., 2, :] + parts[..., 1, :]) + parts[..., 0, :]


def spread_to(payload, axes):
    count = lax.axis_size(axes)
    return lax.all_to_all(jnp.broadcast_to(payload[None], (count,) + payload.shape), axes, 0, 0)


def swap_core(values):
    return lax.ppermute(values, "core", [(0, 1), (1, 0)])


def with_tail(body, stats):
    width = body.shape[1]
    parts = [jnp.pad(part, (0, width - part.shape[0])) for stat in stats for part in split3(stat)]
    tail = jnp.pad(jnp.stack(parts), ((0, 16 - len(parts)), (0, 0)))
    return jnp.concatenate([body, tail], axis=0)


def local(embeddings, landmarks, start_vectors, row_weight, spread):
    own = embeddings.shape[0]
    marks = landmarks.shape[0]
    width = start_vectors.shape[1]
    members = lax.axis_size(ROW_AXES)
    groups = lax.axis_size(MARK_AXES)
    piece = marks // groups
    total_rows = own * lax.axis_size(AXES)
    gamma = spread[0]

    rows_unit = unit_rows(embeddings)
    gathered = spread_to(with_tail(rows_unit, [row_weight]), ROW_AXES)
    part_rows = gathered[:, :own].reshape(members * own, -1)
    part_weight = join3(gathered[:, own : own + 3, :own]).reshape(-1)

    marks_unit = unit_rows(landmarks)
    marks_unit = jnp.concatenate([marks_unit, swap_core(marks_unit)], axis=0)

    product = row_weight[:, None] * start_vectors
    packed = spread_to(with_tail(product.astype(B16), [jnp.sum(product, axis=0)]), ROW_AXES)

    cosine = jnp.einsum("rd,ld->rl", part_rows, marks_unit, preferred_element_type=F32)
    values = jnp.exp(gamma * cosine)
    tile = values.astype(B16)
    sums = jnp.sum(part_weight[:, None] * values, axis=0)
    sums = sums.reshape(2, groups, piece // width, width)
    weight_sum = jnp.full((width,), jnp.sum(part_weight), F32)

    means = None
    scale = None
    for step in range(ITERS):
        weighted = packed[:, :own].reshape(members * own, width)
        totals = jnp.sum(join3(packed[:, own : own + 3]), axis=0)
        if step == 0:
            squares = jnp.zeros_like(totals)
        else:
            squares = jnp.sum(join3(packed[:, own + 3 : own + 6]), axis=0)
        raw = jnp.einsum("rl,rv->lv", tile, weighted, preferred_element_type=F32)
        raw = raw.reshape(2, groups, piece, width)
        stats = jnp.stack([totals, squares, weight_sum] + [jnp.zeros_like(totals)] * 3)
        stats = jnp.broadcast_to(stats, (2, groups) + stats.shape)
        payload = jnp.concatenate([raw, sums, stats], axis=2)
        both = payload[0] + swap_core(payload[1])
        summed = jnp.sum(lax.all_to_all(both, MARK_AXES, 0, 0), axis=0)
        side = summed[:piece]
        totals, squares, all_weight = summed[piece + 2], summed[piece + 3], summed[piece + 4]
        if step == 0:
            means = summed[piece : piece + 2].reshape(piece) / all_weight[0]
            side = side - means[:, None] * totals[None, :]
        else:
            scale = jnp.sqrt(squares / total_rows + 1e-06)
            side = (side * UP - means[:, None] * totals[None, :]) / scale[None, :]
        side_b = lax.reduce_precision(side, 8, 7)
        shift = jnp.sum(means[:, None] * side_b, axis=0)
        sides = spread_to(with_tail(side_b.astype(B16), [shift]), MARK_AXES)
        sides = jnp.stack([sides, swap_core(sides)])
        shift = jnp.sum(join3(sides[:, :, piece : piece + 3]), axis=(0, 1))
        side_all = sides[:, :, :piece].reshape(2 * marks, width)
        part = jnp.dot(tile, side_all, preferred_element_type=F32) - shift[None, :]
        part = part.astype(B16).reshape(members, own, width)
        image = jnp.sum(lax.all_to_all(part, ROW_AXES, 0, 0).astype(F32), axis=0)
        image = row_weight[:, None] * image
        squares = jnp.sum(image * image, axis=0)
        if step + 1 < ITERS:
            product = row_weight[:, None] * image
            packed = spread_to(
                with_tail((product * DOWN).astype(B16), [jnp.sum(product, axis=0), squares]),
                ROW_AXES,
            )
    every = spread_to(jnp.broadcast_to(squares[None], (8, width)), AXES)
    scale = jnp.sqrt(jnp.sum(every[:, 0], axis=0) / total_rows + 1e-06)
    return image / scale[None, :]


def solution(mesh):
    fine = Mesh(mesh.devices.reshape(4, 2, 4, 2, 2), AXES)
    rows = P(AXES, None)
    in_specs = (rows, P(("x", "zl", "core"), None), rows, P(AXES), P())
    return jax.shard_map(local, mesh=fine, in_specs=in_specs, out_specs=rows, check_vma=False)
```

```python
import jax
import jax.numpy as jnp
from jax import lax
from jax.experimental import pallas as pl
from jax.experimental.pallas import tpu as pltpu
from jax.sharding import Mesh
from jax.sharding import PartitionSpec as P

ITERS = 2
AXES = ("y", "zh", "x", "zl", "core")
ROW_AXES = ("x", "zl")
MARK_AXES = ("y", "zh")
F32, B16 = jnp.float32, jnp.bfloat16
DOWN = 2.0**-20
UP = 2.0**20
LOG2E = 1.4426950408889634
VMEM = pl.BlockSpec(memory_space=pltpu.VMEM)
SMEM = pl.BlockSpec(memory_space=pltpu.SMEM)
OWN = 256
PIECE = 256
WIDTH = 128
MARKS = 2048
EIGHT = 8
ROWS = EIGHT * OWN
PACK = OWN + WIDTH // 2 + 16


def params(mib):
    return pltpu.CompilerParams(vmem_limit_bytes=mib * 2**20)


def dot(left, right, left_dim, right_dim):
    dims = (((left_dim,), (right_dim,)), ((), ()))
    return lax.dot_general(left, right, dims, preferred_element_type=F32)


def unit_rows(values):
    values = values.astype(F32)
    scale = lax.rsqrt(jnp.sum(values * values, axis=1, keepdims=True) + 1e-06)
    return (values * scale).astype(B16)


def split3(values):
    high = lax.reduce_precision(values, 8, 7)
    rest = values - high
    mid = lax.reduce_precision(rest, 8, 7)
    low = rest - mid
    return [high.astype(B16), mid.astype(B16), low.astype(B16)]


def parts_in_kernel(values):
    high = values.astype(B16)
    rest = values - high.astype(F32)
    mid = rest.astype(B16)
    low = (rest - mid.astype(F32)).astype(B16)
    return high.astype(F32), mid.astype(F32), low.astype(F32)


def tail_in_kernel(row):
    at = lax.broadcasted_iota(jnp.int32, (16, row.shape[1]), 0)
    high, mid, low = parts_in_kernel(row)
    zero = jnp.zeros((16, row.shape[1]), F32)
    block = jnp.where(at == 0, high, jnp.where(at == 1, mid, jnp.where(at == 2, low, zero)))
    return block.astype(B16)


def join_tail(block):
    block = block.astype(F32)
    return (block[2:3] + block[1:2]) + block[0:1]


def stat_rows(first, second, third):
    at = lax.broadcasted_iota(jnp.int32, (8, PIECE), 0)
    zero = jnp.zeros((8, PIECE), F32)
    return jnp.where(at == 0, first, jnp.where(at == 1, second, jnp.where(at == 2, third, zero)))


def first_kernel(spread_ref, packed_ref, near_ref, far_ref, tile_ref, own_ref, other_ref, wt_ref, wide_ref):
    gamma = spread_ref[0] * LOG2E
    totals = jnp.zeros((1, WIDTH), F32)
    weight_sum = jnp.zeros((1, 1), F32)
    for source in range(EIGHT):
        half = WIDTH // 2
        wt_ref[source, :half] = packed_ref[source, OWN : OWN + half, :OWN]
        wt_ref[source, half:] = packed_ref[source, OWN : OWN + half, OWN:]
        tail = join_tail(packed_ref[source, OWN + half :, :])
        weight = tail[:, :OWN]
        totals = totals + tail[:, OWN : OWN + WIDTH]
        weight_sum = weight_sum + jnp.sum(weight, axis=1, keepdims=True)
        column = jnp.transpose(jnp.broadcast_to(weight, (WIDTH, OWN)))
        wide_ref[source * OWN : (source + 1) * OWN, :] = column
    second = jnp.concatenate([totals, jnp.zeros((1, PIECE - WIDTH), F32)], axis=1)
    third = jnp.broadcast_to(weight_sum, (1, PIECE))
    block = 2 * PIECE
    chunk = 2 * OWN

    def half_of(marks_ref, out_ref, base):
        def body(index, _):
            start = pl.multiple_of(index * block, block)
            marks = marks_ref[pl.ds(start, block), :]
            lanes = pl.ds(pl.multiple_of(base + start, block), block)
            sums = [jnp.zeros((8, WIDTH), F32) for _ in range(block // WIDTH)]
            product = None
            for part in range(ROWS // chunk):
                rows = packed_ref[2 * part : 2 * part + 2, :OWN, :].reshape(chunk, -1)
                values = jnp.exp2(dot(rows, marks, 1, 1) * gamma)
                kernel = values.astype(B16)
                tile_ref[part * chunk : (part + 1) * chunk, lanes] = kernel
                wide = wide_ref[part * chunk : (part + 1) * chunk, :]
                for at in range(block // WIDTH):
                    term = values[:, at * WIDTH : (at + 1) * WIDTH] * wide
                    sums[at] = sums[at] + jnp.sum(term.reshape(chunk // 8, 8, WIDTH), axis=0)
                for at in range(2):
                    term = dot(wt_ref[2 * part + at], kernel[at * OWN : (at + 1) * OWN], 1, 0)
                    product = term if product is None else product + term
            sums = jnp.sum(jnp.concatenate(sums, axis=1), axis=0, keepdims=True)
            for at in range(2):
                lane = slice(at * PIECE, (at + 1) * PIECE)
                out_ref[2 * index + at, :WIDTH, :] = product[:, lane]
                out_ref[2 * index + at, WIDTH:, :] = stat_rows(sums[:, lane], second, third)
            return 0

        lax.fori_loop(0, MARKS // block, body, 0)

    half_of(near_ref, own_ref, 0)
    half_of(far_ref, other_ref, MARKS)


def build(spread, packed, near, far):
    side = jax.ShapeDtypeStruct((EIGHT, WIDTH + 8, PIECE), F32)
    return pl.pallas_call(
        first_kernel,
        out_shape=[pltpu.VMEM((ROWS, 2 * MARKS), B16), side, side],
        in_specs=[SMEM, VMEM, VMEM, VMEM],
        out_specs=[VMEM, VMEM, VMEM],
        scratch_shapes=[pltpu.VMEM((EIGHT, WIDTH, OWN), B16), pltpu.VMEM((ROWS, WIDTH), F32)],
        compiler_params=params(24),
        name="build",
    )(spread, packed, near, far)


def side_kernel(tile_ref, packed_ref, own_ref, other_ref):
    totals = jnp.zeros((1, PIECE), F32)
    for source in range(EIGHT):
        totals = totals + join_tail(packed_ref[source, WIDTH:, :])
    stats = stat_rows(jnp.zeros((1, PIECE), F32), totals, jnp.zeros((1, PIECE), F32))
    block = 4 * PIECE

    def half_of(out_ref, base):
        def body(index, _):
            lanes = pl.ds(pl.multiple_of(base + index * block, block), block)
            product = None
            for source in range(EIGHT):
                kernel = tile_ref[source * OWN : (source + 1) * OWN, lanes]
                term = dot(packed_ref[source, :WIDTH, :], kernel, 1, 0)
                product = term if product is None else product + term
            for at in range(4):
                out_ref[4 * index + at, :WIDTH, :] = product[:, at * PIECE : (at + 1) * PIECE]
                out_ref[4 * index + at, WIDTH:, :] = stats
            return 0

        lax.fori_loop(0, MARKS // block, body, 0)

    half_of(own_ref, 0)
    half_of(other_ref, MARKS)


def side_terms(tile, packed):
    side = jax.ShapeDtypeStruct((EIGHT, WIDTH + 8, PIECE), F32)
    return pl.pallas_call(
        side_kernel,
        out_shape=[side, side],
        in_specs=[VMEM, VMEM],
        out_specs=[VMEM, VMEM],
        compiler_params=params(24),
        name="side_terms",
    )(tile, packed)


def centre_kernel(first, total_rows, *refs):
    if first:
        terms_ref, out_ref, means_ref = refs
    else:
        terms_ref, before_ref, out_ref = refs
    summed = terms_ref[0]
    for group in range(1, EIGHT):
        summed = summed + terms_ref[group]
    stats = summed[WIDTH:]
    if first:
        means = stats[0:1] / stats[2:3]
        means_ref[...] = jnp.broadcast_to(means, (8, PIECE))
    else:
        means = before_ref[0:1]
    columns = jnp.transpose(jnp.broadcast_to(stats[1:2], (WIDTH, PIECE)))
    totals = columns[:WIDTH, 0:1]
    side = summed[:WIDTH]
    if first:
        side = side - totals * means
    else:
        squares = columns[WIDTH:, 0:1]
        side = (side * UP - totals * means) / jnp.sqrt(squares / total_rows + 1e-06)
    side = side.astype(B16)
    tail = tail_in_kernel(means)
    for group in range(EIGHT):
        out_ref[group, :WIDTH, :] = side
        out_ref[group, WIDTH:, :] = tail


def centre(first, total_rows, *args):
    shapes = [jax.ShapeDtypeStruct((EIGHT, WIDTH + 16, PIECE), B16)]
    if first:
        shapes.append(jax.ShapeDtypeStruct((8, PIECE), F32))
    return pl.pallas_call(
        lambda *refs: centre_kernel(first, total_rows, *refs),
        out_shape=shapes,
        in_specs=[VMEM] * len(args),
        out_specs=[VMEM] * len(shapes),
        compiler_params=params(16),
        name="centre",
    )(*args)


def image_kernel(tile_ref, own_ref, other_ref, out_ref, side_ref, shift_ref):
    shift = jnp.zeros((16, WIDTH), F32)
    for half, ref in enumerate((own_ref, other_ref)):
        for piece in range(EIGHT):
            side = ref[piece, :WIDTH, :]
            lane = half * MARKS + piece * PIECE
            side_ref[:, lane : lane + PIECE] = side
            shift = shift + dot(ref[piece, WIDTH:, :], side, 1, 1)
    shift_ref[...] = (shift[2:3] + shift[1:2]) + shift[0:1]

    def body(index, _):
        rows = pl.ds(pl.multiple_of(index * 2 * OWN, 2 * OWN), 2 * OWN)
        term = dot(tile_ref[rows, :], side_ref[...], 1, 1) - shift_ref[...]
        out_ref[pl.ds(2 * index, 2)] = term.astype(B16).reshape(2, OWN, WIDTH)
        return 0

    lax.fori_loop(0, EIGHT // 2, body, 0)


def image_terms(tile, own, other):
    return pl.pallas_call(
        image_kernel,
        out_shape=jax.ShapeDtypeStruct((EIGHT, OWN, WIDTH), B16),
        in_specs=[VMEM] * 3,
        out_specs=VMEM,
        scratch_shapes=[pltpu.VMEM((WIDTH, 2 * MARKS), B16), pltpu.VMEM((1, WIDTH), F32)],
        compiler_params=params(24),
        name="image_terms",
    )(tile, own, other)


def owner_kernel(last, terms_ref, weight_ref, out_ref, *more):
    image = terms_ref[0].astype(F32)
    for member in range(1, EIGHT):
        image = image + terms_ref[member].astype(F32)
    weight = weight_ref[...]
    image = weight * image
    squares = jnp.sum(image * image, axis=0, keepdims=True)
    if last:
        out_ref[...] = image
        more[0][...] = jnp.broadcast_to(squares, (8, WIDTH))
    else:
        product = weight * image
        totals = jnp.sum(product, axis=0, keepdims=True)
        body = jnp.transpose(product * DOWN).astype(B16)
        tail = tail_in_kernel(jnp.concatenate([totals, squares], axis=1))
        for member in range(EIGHT):
            out_ref[member, :WIDTH, :] = body
            out_ref[member, WIDTH:, :] = tail


def owner(last, terms, weight):
    if last:
        shapes = [jax.ShapeDtypeStruct((OWN, WIDTH), F32), jax.ShapeDtypeStruct((8, WIDTH), F32)]
    else:
        shapes = [jax.ShapeDtypeStruct((EIGHT, WIDTH + 16, OWN), B16)]
    return pl.pallas_call(
        lambda *refs: owner_kernel(last, *refs),
        out_shape=shapes,
        in_specs=[VMEM, VMEM],
        out_specs=[VMEM] * len(shapes),
        compiler_params=params(16),
        name="owner",
    )(terms, weight)


def spread_to(payload, axes):
    count = lax.axis_size(axes)
    return lax.all_to_all(jnp.broadcast_to(payload[None], (count,) + payload.shape), axes, 0, 0)


def exchange(payload, axes):
    return lax.all_to_all(payload, axes, 0, 0)


def swap_core(values):
    return lax.ppermute(values, "core", [(0, 1), (1, 0)])


def pack(rows_unit, product, row_weight):
    transposed = product.T.astype(B16)
    half = WIDTH // 2
    vectors = jnp.concatenate([transposed[:half], transposed[half:]], axis=1)
    totals = jnp.pad(jnp.sum(product, axis=0), (0, OWN - WIDTH))
    tail = jnp.stack(split3(jnp.concatenate([row_weight, totals])))
    tail = jnp.pad(tail, ((0, 13), (0, 0)))
    return jnp.concatenate([rows_unit, vectors, tail], axis=0)


def local(embeddings, landmarks, start_vectors, row_weight, spread):
    total_rows = embeddings.shape[0] * lax.axis_size(AXES)
    weight = jnp.broadcast_to(row_weight[:, None], (OWN, WIDTH))
    product = row_weight[:, None] * start_vectors
    packed = spread_to(pack(unit_rows(embeddings), product, row_weight), ROW_AXES)
    near = unit_rows(landmarks)
    far = swap_core(near)
    tile, own, other = build(spread, packed, near, far)
    means = None
    for step in range(ITERS):
        if step > 0:
            own, other = side_terms(tile, packed)
        terms = exchange(own + swap_core(other), MARK_AXES)
        if step == 0:
            sides, means = centre(True, total_rows, terms)
        else:
            (sides,) = centre(False, total_rows, terms, means)
        sides = exchange(sides, MARK_AXES)
        parts = exchange(image_terms(tile, sides, swap_core(sides)), ROW_AXES)
        if step + 1 < ITERS:
            (packed,) = owner(False, parts, weight)
            packed = exchange(packed, ROW_AXES)
    image, squares = owner(True, parts, weight)
    every = spread_to(squares, AXES)
    scale = jnp.sqrt(jnp.sum(every[:, 0], axis=0) / total_rows + 1e-06)
    return image / scale[None, :]


def solution(mesh):
    fine = Mesh(mesh.devices.reshape(4, 2, 4, 2, 2), AXES)
    rows = P(AXES, None)
    in_specs = (rows, P(("x", "zl", "core"), None), rows, P(AXES), P())
    return jax.shard_map(local, mesh=fine, in_specs=in_specs, out_specs=rows, check_vma=False)
```

```python
import jax
import jax.numpy as jnp
from jax import lax
from jax.experimental import pallas as pl
from jax.experimental.pallas import tpu as pltpu
from jax.sharding import Mesh
from jax.sharding import PartitionSpec as P

ITERS = 2
AXES = ("y", "zh", "x", "zl", "core")
ROW_AXES = ("x", "zl")
MARK_AXES = ("y", "zh")
F32, B16 = jnp.float32, jnp.bfloat16
DOWN = 2.0**-20
UP = 2.0**20
LOG2E = 1.4426950408889634
VMEM = pl.BlockSpec(memory_space=pltpu.VMEM)
SMEM = pl.BlockSpec(memory_space=pltpu.SMEM)
OWN = 256
PIECE = 256
WIDTH = 128
MARKS = 2048
EIGHT = 8
ROWS = EIGHT * OWN
PACK = OWN + WIDTH // 2 + 16
BLOCK = 4 * PIECE


def params(mib):
    return pltpu.CompilerParams(vmem_limit_bytes=mib * 2**20)


def dot(left, right, left_dim, right_dim):
    dims = (((left_dim,), (right_dim,)), ((), ()))
    return lax.dot_general(left, right, dims, preferred_element_type=F32)


def unit_rows(values):
    values = values.astype(F32)
    scale = lax.rsqrt(jnp.sum(values * values, axis=1, keepdims=True) + 1e-06)
    return (values * scale).astype(B16)


def split3(values):
    high = lax.reduce_precision(values, 8, 7)
    rest = values - high
    mid = lax.reduce_precision(rest, 8, 7)
    low = rest - mid
    return [high.astype(B16), mid.astype(B16), low.astype(B16)]


def parts_in_kernel(values):
    high = values.astype(B16)
    rest = values - high.astype(F32)
    mid = rest.astype(B16)
    low = (rest - mid.astype(F32)).astype(B16)
    return high.astype(F32), mid.astype(F32), low.astype(F32)


def tail_in_kernel(row):
    at = lax.broadcasted_iota(jnp.int32, (16, row.shape[1]), 0)
    high, mid, low = parts_in_kernel(row)
    zero = jnp.zeros((16, row.shape[1]), F32)
    block = jnp.where(at == 0, high, jnp.where(at == 1, mid, jnp.where(at == 2, low, zero)))
    return block.astype(B16)


def join_tail(block):
    block = block.astype(F32)
    return (block[2:3] + block[1:2]) + block[0:1]


def stat_rows(first, second, third):
    at = lax.broadcasted_iota(jnp.int32, (8, PIECE), 0)
    zero = jnp.zeros((8, PIECE), F32)
    return jnp.where(at == 0, first, jnp.where(at == 1, second, jnp.where(at == 2, third, zero)))


def tails_in_kernel(rows):
    at = lax.broadcasted_iota(jnp.int32, (16, rows[0].shape[1]), 0)
    block = jnp.zeros(at.shape, F32)
    for index, row in enumerate(rows):
        for part, value in enumerate(parts_in_kernel(row)):
            block = jnp.where(at == 3 * index + part, value, block)
    return block.astype(B16)


def join_at(block, index):
    block = block[3 * index : 3 * index + 3].astype(F32)
    return (block[2:3] + block[1:2]) + block[0:1]


def columns_of(rows):
    at = lax.broadcasted_iota(jnp.int32, (WIDTH, WIDTH), 0)
    block = jnp.zeros((WIDTH, WIDTH), F32)
    for index, row in enumerate(rows):
        block = jnp.where(at == index, row, block)
    return jnp.transpose(block)


def call(kernel, shapes, specs, args, name, scratch=(), flops=0, mib=24):
    cost = pl.CostEstimate(flops=flops, bytes_accessed=0, transcendentals=0)
    return pl.pallas_call(
        kernel,
        out_shape=shapes,
        in_specs=specs,
        out_specs=[VMEM] * len(shapes),
        scratch_shapes=list(scratch),
        compiler_params=params(mib),
        cost_estimate=cost,
        name=name,
    )(*args)


def build_kernel(groups, block, *refs):
    count = sum(groups)
    spread_ref, packed, (near_ref, far_ref) = refs[0], refs[1 : 1 + count], refs[1 + count : 3 + count]
    tile_ref, sums_ref, wide_ref = refs[3 + count :]
    gamma = spread_ref[0] * LOG2E
    for source in range(count):
        weight = join_tail(packed[source][PACK - 16 :, :])[:, :OWN]
        column = jnp.transpose(jnp.broadcast_to(weight, (WIDTH, OWN)))
        wide_ref[source * OWN : (source + 1) * OWN, :] = column

    def half_of(marks_ref, base):
        def body(index, _):
            start = pl.multiple_of(index * block, block)
            marks = marks_ref[pl.ds(start, block), :]
            lanes = pl.ds(pl.multiple_of(base + start, block), block)
            sums = [jnp.zeros((8, WIDTH), F32) for _ in range(block // WIDTH)]
            first = 0
            for size in groups:
                rows = jnp.concatenate([ref[:OWN, :] for ref in packed[first : first + size]], axis=0)
                values = jnp.exp2(dot(rows, marks, 1, 1) * gamma)
                at = slice(first * OWN, (first + size) * OWN)
                tile_ref[at, lanes] = values.astype(B16)
                wide = wide_ref[at, :]
                for lane in range(block // WIDTH):
                    term = values[:, lane * WIDTH : (lane + 1) * WIDTH] * wide
                    sums[lane] = sums[lane] + jnp.sum(term.reshape(-1, 8, WIDTH), axis=0)
                first += size
            sums_ref[:, lanes] = jnp.concatenate(sums, axis=1)
            return 0

        lax.fori_loop(0, MARKS // block, body, 0)

    half_of(near_ref, 0)
    half_of(far_ref, MARKS)


def build(groups, block, spread, packed, near, far):
    rows = sum(groups) * OWN
    return call(
        lambda *refs: build_kernel(groups, block, *refs),
        [pltpu.VMEM((rows, 2 * MARKS), B16), jax.ShapeDtypeStruct((8, 2 * MARKS), F32)],
        [SMEM] + [VMEM] * (len(packed) + 2),
        [spread, *packed, near, far],
        "build",
        scratch=[pltpu.VMEM((rows, WIDTH), F32)],
        flops=4 * rows * 2 * MARKS * 512,
    )


def tile_rows(tiles, slot, lanes):
    for tile in tiles:
        if slot * OWN < tile.shape[0]:
            return tile[slot * OWN : (slot + 1) * OWN, lanes]
        slot -= tile.shape[0] // OWN


def side_kernel(first, *refs):
    slots_ref, tiles, refs = refs[0], refs[1:4], refs[4:]
    zero = jnp.zeros((1, PIECE - WIDTH), F32)
    ones = jnp.ones((16, OWN), B16)
    totals = jnp.zeros((1, WIDTH), F32)
    third = jnp.zeros((1, WIDTH), F32)
    rounded = jnp.zeros((16, WIDTH), F32)
    half = WIDTH // 2
    if first:
        packed, sums, (own_ref, other_ref, wt_ref) = refs[:8], refs[8:11], refs[11:]
    else:
        packed_ref, own_ref, other_ref, wt_ref = refs
    for slot in range(EIGHT):
        if first:
            wt_ref[slot, :half] = packed[slot][OWN : OWN + half, :OWN]
            wt_ref[slot, half:] = packed[slot][OWN : OWN + half, OWN:]
            tail = join_tail(packed[slot][OWN + half :, :])
            totals = totals + tail[:, OWN : OWN + WIDTH]
            third = third + jnp.sum(tail[:, :OWN], axis=1, keepdims=True)
        else:
            wt_ref[slot] = packed_ref[slots_ref[slot], :WIDTH, :]
            tail = join_tail(packed_ref[slot, WIDTH:, :])
            totals = totals + tail[:, :WIDTH]
            third = third + tail[:, WIDTH:]
        rounded = rounded + dot(ones, wt_ref[slot], 1, 1)
    second = jnp.concatenate([totals, rounded[:1]], axis=1)
    third = jnp.concatenate([third, zero], axis=1)

    def half_of(out_ref, base):
        def body(index, _):
            lanes = pl.ds(pl.multiple_of(base + index * BLOCK, BLOCK), BLOCK)
            product = None
            for slot in range(EIGHT):
                term = dot(wt_ref[slot], tile_rows(tiles, slot, lanes), 1, 0)
                product = term if product is None else product + term
            if first:
                column = (sums[0][:, lanes] + sums[1][:, lanes]) + sums[2][:, lanes]
                column = jnp.sum(column, axis=0, keepdims=True)
            else:
                column = jnp.zeros((1, BLOCK), F32)
            for at in range(BLOCK // PIECE):
                lane = slice(at * PIECE, (at + 1) * PIECE)
                out_ref[BLOCK // PIECE * index + at, :WIDTH, :] = product[:, lane]
                out_ref[BLOCK // PIECE * index + at, WIDTH:, :] = stat_rows(column[:, lane], second, third)
            return 0

        lax.fori_loop(0, MARKS // BLOCK, body, 0)

    half_of(own_ref, 0)
    half_of(other_ref, MARKS)


def side_terms(first, slots, tiles, more):
    side = jax.ShapeDtypeStruct((EIGHT, WIDTH + 8, PIECE), F32)
    return call(
        lambda *refs: side_kernel(first, *refs),
        [side, side],
        [SMEM] + [VMEM] * (3 + len(more)),
        [slots, *tiles, *more],
        "side_terms",
        scratch=[pltpu.VMEM((EIGHT, WIDTH, OWN), B16)],
        flops=2 * ROWS * 2 * MARKS * WIDTH,
    )


def pair_kernel(first, *refs):
    refs = refs[3:]
    if first:
        own_ref, other_ref, out_ref, pair_ref = refs
    else:
        own_ref, other_ref, before_ref, out_ref = refs
    stats = own_ref[0, WIDTH:, :] + other_ref[0, WIDTH:, :]
    second, third = stats[1:2], stats[2:3]
    rounded = columns_of([second[:, WIDTH:]])[:, 0:1]
    for piece in range(EIGHT):
        if first:
            column = own_ref[piece, WIDTH : WIDTH + 8, :] + other_ref[piece, WIDTH : WIDTH + 8, :]
            means = column[0:1] / third[:, 0:1]
            pair_ref[piece : piece + 1, :] = means
        else:
            means = before_ref[piece : piece + 1, :]
        side = own_ref[piece, :WIDTH, :] + other_ref[piece, :WIDTH, :]
        out_ref[piece, :WIDTH, :] = (side - rounded * means).astype(B16)
        out_ref[piece, WIDTH:, :] = tails_in_kernel([means, second, third])


def pair(first, tiles, *args):
    shapes = [jax.ShapeDtypeStruct((EIGHT, WIDTH + 16, PIECE), B16)]
    if first:
        shapes.append(jax.ShapeDtypeStruct((EIGHT, PIECE), F32))
    return call(
        lambda *refs: pair_kernel(first, *refs),
        shapes,
        [VMEM] * (3 + len(args)),
        [*tiles, *args],
        "pair",
        flops=10**9,
    )


def centre_kernel(first, total_rows, *refs):
    refs = refs[3:]
    if first:
        terms_ref, out_ref, means_ref = refs
    else:
        terms_ref, before_ref, out_ref = refs
    tails = [terms_ref[group, WIDTH:, :] for group in range(EIGHT)]
    pairs = [join_at(tail, 0) for tail in tails]
    second = [join_at(tail, 1) for tail in tails]
    third = [join_at(tail, 2) for tail in tails]
    total, every = second[0], third[0]
    for group in range(1, EIGHT):
        total, every = total + second[group], every + third[group]
    columns = columns_of([row[:, WIDTH:] for row in second] + [total[:, :WIDTH], every[:, :WIDTH]])
    if first:
        means = third[0][:, 0:1] * pairs[0]
        for group in range(1, EIGHT):
            means = means + third[group][:, 0:1] * pairs[group]
        means = means / every[:, 0:1]
        means_ref[...] = jnp.broadcast_to(means, (8, PIECE))
    else:
        means = before_ref[0:1]
    side = terms_ref[0, :WIDTH, :].astype(F32) + columns[:, 0:1] * pairs[0]
    for group in range(1, EIGHT):
        side = side + (terms_ref[group, :WIDTH, :].astype(F32) + columns[:, group : group + 1] * pairs[group])
    totals = columns[:, EIGHT : EIGHT + 1]
    if first:
        side = side - totals * means
    else:
        squares = columns[:, EIGHT + 1 : EIGHT + 2]
        side = (side * UP - totals * means) / jnp.sqrt(squares / total_rows + 1e-06)
    side = side.astype(B16)
    tail = tail_in_kernel(means)
    for group in range(EIGHT):
        out_ref[group, :WIDTH, :] = side
        out_ref[group, WIDTH:, :] = tail


def centre(first, total_rows, tiles, *args):
    shapes = [jax.ShapeDtypeStruct((EIGHT, WIDTH + 16, PIECE), B16)]
    if first:
        shapes.append(jax.ShapeDtypeStruct((8, PIECE), F32))
    return call(
        lambda *refs: centre_kernel(first, total_rows, *refs),
        shapes,
        [VMEM] * (3 + len(args)),
        [*tiles, *args],
        "centre",
        flops=10**9,
    )


def image_kernel(slots_ref, *refs):
    tiles, (own_ref, other_ref, out_ref, side_ref) = refs[:3], refs[3:]
    shift = jnp.zeros((16, WIDTH), F32)
    for half, ref in enumerate((own_ref, other_ref)):
        for piece in range(EIGHT):
            side = ref[piece, :WIDTH, :]
            lane = half * MARKS + piece * PIECE
            side_ref[:, lane : lane + PIECE] = side
            shift = shift + dot(ref[piece, WIDTH:, :], side, 1, 1)
    shift = (shift[2:3] + shift[1:2]) + shift[0:1]
    slot = 0
    for tile in tiles:
        term = dot(tile[...], side_ref[...], 1, 1) - shift
        for at in range(tile.shape[0] // OWN):
            out_ref[slots_ref[slot]] = term[at * OWN : (at + 1) * OWN].astype(B16)
            slot += 1


def image_terms(slots, tiles, own, other):
    return call(
        image_kernel,
        [jax.ShapeDtypeStruct((EIGHT, OWN, WIDTH), B16)],
        [SMEM] + [VMEM] * 5,
        [slots, *tiles, own, other],
        "image_terms",
        scratch=[pltpu.VMEM((WIDTH, 2 * MARKS), B16)],
        flops=2 * ROWS * 2 * MARKS * WIDTH,
    )[0]


def owner_kernel(last, *refs):
    if not last:
        refs = refs[3:]
    terms_ref, weight_ref, out_ref, *more = refs
    image = terms_ref[0].astype(F32)
    for member in range(1, EIGHT):
        image = image + terms_ref[member].astype(F32)
    weight = weight_ref[...]
    image = weight * image
    squares = jnp.sum(image * image, axis=0, keepdims=True)
    if last:
        out_ref[...] = image
        more[0][...] = jnp.broadcast_to(squares, (8, WIDTH))
    else:
        product = weight * image
        totals = jnp.sum(product, axis=0, keepdims=True)
        body = jnp.transpose(product * DOWN).astype(B16)
        tail = tail_in_kernel(jnp.concatenate([totals, squares], axis=1))
        for member in range(EIGHT):
            out_ref[member, :WIDTH, :] = body
            out_ref[member, WIDTH:, :] = tail


def owner(last, tiles, terms, weight):
    if last:
        shapes = [jax.ShapeDtypeStruct((OWN, WIDTH), F32), jax.ShapeDtypeStruct((8, WIDTH), F32)]
        tiles = []
    else:
        shapes = [jax.ShapeDtypeStruct((EIGHT, WIDTH + 16, OWN), B16)]
    return call(
        lambda *refs: owner_kernel(last, *refs),
        shapes,
        [VMEM] * (len(tiles) + 2),
        [*tiles, terms, weight],
        "owner",
        flops=10**9,
    )


def exchange(payload, axes):
    return lax.all_to_all(payload, axes, 0, 0)


def swap_core(values):
    return lax.ppermute(values, "core", [(0, 1), (1, 0)])


def swap_z(values):
    return lax.ppermute(values, "zl", [(0, 1), (1, 0)])


def from_below(values):
    return lax.ppermute(values, "x", [(at, (at + 1) % 4) for at in range(4)])


def from_above(values):
    return lax.ppermute(values, "x", [(at, (at + 3) % 4) for at in range(4)])


def pack(rows_unit, product, row_weight):
    transposed = product.T.astype(B16)
    half = WIDTH // 2
    vectors = jnp.concatenate([transposed[:half], transposed[half:]], axis=1)
    totals = jnp.pad(jnp.sum(product, axis=0), (0, OWN - WIDTH))
    tail = jnp.stack(split3(jnp.concatenate([row_weight, totals])))
    tail = jnp.pad(tail, ((0, 13), (0, 0)))
    return jnp.concatenate([rows_unit, vectors, tail], axis=0)


def slot_owners():
    x, z = lax.axis_index("x"), lax.axis_index("zl")
    moves = [(0, 0), (3, 0), (1, 0), (0, 1), (2, 0), (1, 1), (3, 1), (2, 1)]
    return jnp.stack([(x + dx) % 4 * 2 + (z + dz) % 2 for dx, dz in moves]).astype(jnp.int32)


def local(embeddings, landmarks, start_vectors, row_weight, spread):
    total_rows = embeddings.shape[0] * lax.axis_size(AXES)
    slots = slot_owners()
    weight = jnp.broadcast_to(row_weight[:, None], (OWN, WIDTH))
    packed = pack(unit_rows(embeddings), row_weight[:, None] * start_vectors, row_weight)
    near = unit_rows(landmarks)
    far = swap_core(near)
    below, above, across = from_below(packed), from_above(packed), swap_z(packed)
    opposite, across_above, across_below = from_below(below), from_above(across), swap_z(below)
    last = swap_z(opposite)
    packs = [packed, below, above, across, opposite, across_above, across_below, last]
    one, sums_one = build((2, 2), 1024, spread, packs[:4], near, far)
    two, sums_two = build((3,), 512, spread, packs[4:7], near, far)
    three, sums_three = build((1,), 1024, spread, packs[7:], near, far)
    tiles = (one, two, three)
    own, other = side_terms(True, slots, tiles, [*packs, sums_one, sums_two, sums_three])
    for step in range(ITERS):
        if step == 0:
            payload, pair_means = pair(True, tiles, own, swap_core(other))
            sides, means = centre(True, total_rows, tiles, exchange(payload, MARK_AXES))
        else:
            own, other = side_terms(False, slots, tiles, [vectors])
            (payload,) = pair(False, tiles, own, swap_core(other), pair_means)
            (sides,) = centre(False, total_rows, tiles, exchange(payload, MARK_AXES), means)
        sides = exchange(sides, MARK_AXES)
        parts = exchange(image_terms(slots, tiles, sides, swap_core(sides)), ROW_AXES)
        if step + 1 < ITERS:
            (vectors,) = owner(False, tiles, parts, weight)
            vectors = exchange(vectors, ROW_AXES)
    image, squares = owner(True, tiles, parts, weight)
    count = lax.axis_size(AXES)
    every = exchange(jnp.broadcast_to(squares[:1][None], (count, 1, WIDTH)), AXES)
    scale = jnp.sqrt(jnp.sum(every[:, 0], axis=0) / total_rows + 1e-06)
    return image / scale[None, :]


def solution(mesh):
    fine = Mesh(mesh.devices.reshape(4, 2, 4, 2, 2), AXES)
    rows = P(AXES, None)
    in_specs = (rows, P(("x", "zl", "core"), None), rows, P(AXES), P())
    return jax.shard_map(local, mesh=fine, in_specs=in_specs, out_specs=rows, check_vma=False)
```

```python
import jax
import jax.numpy as jnp
from jax import lax
from jax.experimental import pallas as pl
from jax.experimental.pallas import tpu as pltpu
from jax.sharding import Mesh
from jax.sharding import PartitionSpec as P

ITERS = 2
AXES = ("y", "zh", "x", "zl", "core")
ROW_AXES = ("x", "zl")
MARK_AXES = ("y", "zh")
F32, B16 = jnp.float32, jnp.bfloat16
DOWN = 2.0**-20
UP = 2.0**20
LOG2E = 1.4426950408889634
VMEM = pl.BlockSpec(memory_space=pltpu.VMEM)
SMEM = pl.BlockSpec(memory_space=pltpu.SMEM)
OWN = 256
PIECE = 256
WIDTH = 128
MARKS = 2048
EIGHT = 8
ROWS = EIGHT * OWN
PACK = OWN + WIDTH // 2 + 16
BLOCK = 4 * PIECE


def params(mib):
    return pltpu.CompilerParams(vmem_limit_bytes=mib * 2**20)


def dot(left, right, left_dim, right_dim):
    dims = (((left_dim,), (right_dim,)), ((), ()))
    return lax.dot_general(left, right, dims, preferred_element_type=F32)


def unit_rows(values):
    values = values.astype(F32)
    scale = lax.rsqrt(jnp.sum(values * values, axis=1, keepdims=True) + 1e-06)
    return (values * scale).astype(B16)


def parts_in_kernel(values):
    high = values.astype(B16)
    rest = values - high.astype(F32)
    mid = rest.astype(B16)
    low = (rest - mid.astype(F32)).astype(B16)
    return high.astype(F32), mid.astype(F32), low.astype(F32)


def tail_in_kernel(row):
    at = lax.broadcasted_iota(jnp.int32, (16, row.shape[1]), 0)
    high, mid, low = parts_in_kernel(row)
    zero = jnp.zeros((16, row.shape[1]), F32)
    block = jnp.where(at == 0, high, jnp.where(at == 1, mid, jnp.where(at == 2, low, zero)))
    return block.astype(B16)


def join_tail(block):
    block = block.astype(F32)
    return (block[2:3] + block[1:2]) + block[0:1]


def stat_rows(first, second, third):
    at = lax.broadcasted_iota(jnp.int32, (8, PIECE), 0)
    zero = jnp.zeros((8, PIECE), F32)
    return jnp.where(at == 0, first, jnp.where(at == 1, second, jnp.where(at == 2, third, zero)))


def tails_in_kernel(rows):
    at = lax.broadcasted_iota(jnp.int32, (16, rows[0].shape[1]), 0)
    block = jnp.zeros(at.shape, F32)
    for index, row in enumerate(rows):
        for part, value in enumerate(parts_in_kernel(row)):
            block = jnp.where(at == 3 * index + part, value, block)
    return block.astype(B16)


def join_at(block, index):
    block = block[3 * index : 3 * index + 3].astype(F32)
    return (block[2:3] + block[1:2]) + block[0:1]


def columns_of(rows):
    at = lax.broadcasted_iota(jnp.int32, (WIDTH, WIDTH), 0)
    block = jnp.zeros((WIDTH, WIDTH), F32)
    for index, row in enumerate(rows):
        block = jnp.where(at == index, row, block)
    return jnp.transpose(block)


def call(kernel, shapes, specs, args, name, scratch=(), flops=0, mib=24):
    cost = pl.CostEstimate(flops=flops, bytes_accessed=0, transcendentals=0)
    return pl.pallas_call(
        kernel,
        out_shape=shapes,
        in_specs=specs,
        out_specs=[VMEM] * len(shapes),
        scratch_shapes=list(scratch),
        compiler_params=params(mib),
        cost_estimate=cost,
        name=name,
    )(*args)


def build_kernel(groups, block, *refs):
    count = sum(groups)
    spread_ref, packed, (near_ref, far_ref) = refs[0], refs[1 : 1 + count], refs[1 + count : 3 + count]
    tile_ref, sums_ref, wide_ref = refs[3 + count :]
    gamma = spread_ref[0] * LOG2E
    for source in range(count):
        weight = join_tail(packed[source][PACK - 16 :, :])[:, :OWN]
        column = jnp.transpose(jnp.broadcast_to(weight, (WIDTH, OWN)))
        wide_ref[source * OWN : (source + 1) * OWN, :] = column

    def half_of(marks_ref, base):
        def body(index, _):
            start = pl.multiple_of(index * block, block)
            marks = marks_ref[pl.ds(start, block), :]
            lanes = pl.ds(pl.multiple_of(base + start, block), block)
            sums = [jnp.zeros((8, WIDTH), F32) for _ in range(block // WIDTH)]
            first = 0
            for size in groups:
                rows = jnp.concatenate([ref[:OWN, :] for ref in packed[first : first + size]], axis=0)
                values = jnp.exp2(dot(rows, marks, 1, 1) * gamma)
                at = slice(first * OWN, (first + size) * OWN)
                tile_ref[at, lanes] = values.astype(B16)
                wide = wide_ref[at, :]
                for lane in range(block // WIDTH):
                    term = values[:, lane * WIDTH : (lane + 1) * WIDTH] * wide
                    sums[lane] = sums[lane] + jnp.sum(term.reshape(-1, 8, WIDTH), axis=0)
                first += size
            sums_ref[:, lanes] = jnp.concatenate(sums, axis=1)
            return 0

        lax.fori_loop(0, MARKS // block, body, 0)

    half_of(near_ref, 0)
    half_of(far_ref, MARKS)


def build(groups, block, spread, packed, near, far):
    rows = sum(groups) * OWN
    return call(
        lambda *refs: build_kernel(groups, block, *refs),
        [pltpu.VMEM((rows, 2 * MARKS), B16), jax.ShapeDtypeStruct((8, 2 * MARKS), F32)],
        [SMEM] + [VMEM] * (len(packed) + 2),
        [spread, *packed, near, far],
        "build",
        scratch=[pltpu.VMEM((rows, WIDTH), F32)],
        flops=4 * rows * 2 * MARKS * 512,
    )


def tile_rows(tiles, slot, lanes):
    for tile in tiles:
        if slot * OWN < tile.shape[0]:
            return tile[slot * OWN : (slot + 1) * OWN, lanes]
        slot -= tile.shape[0] // OWN


def side_kernel(first, base, *refs):
    slots_ref, tiles, refs = refs[0], refs[1:4], refs[4:]
    zero = jnp.zeros((1, PIECE - WIDTH), F32)
    ones = jnp.ones((16, OWN), B16)
    totals = jnp.zeros((1, WIDTH), F32)
    third = jnp.zeros((1, WIDTH), F32)
    rounded = jnp.zeros((16, WIDTH), F32)
    half = WIDTH // 2
    if first:
        packed, sums, (out_ref, wt_ref) = refs[:8], refs[8:11], refs[11:]
    else:
        packed_ref, out_ref, wt_ref = refs
    for slot in range(EIGHT):
        if first:
            wt_ref[slot, :half] = packed[slot][OWN : OWN + half, :OWN]
            wt_ref[slot, half:] = packed[slot][OWN : OWN + half, OWN:]
            tail = join_tail(packed[slot][OWN + half :, :])
            totals = totals + tail[:, OWN : OWN + WIDTH]
            third = third + jnp.sum(tail[:, :OWN], axis=1, keepdims=True)
        else:
            wt_ref[slot] = packed_ref[slots_ref[slot], :WIDTH, :]
            tail = join_tail(packed_ref[slot, WIDTH:, :])
            totals = totals + tail[:, :WIDTH]
            third = third + tail[:, WIDTH:]
        rounded = rounded + dot(ones, wt_ref[slot], 1, 1)
    second = jnp.concatenate([totals, rounded[:1]], axis=1)
    third = jnp.concatenate([third, zero], axis=1)

    def body(index, _):
        lanes = pl.ds(pl.multiple_of(base + index * BLOCK, BLOCK), BLOCK)
        product = None
        for slot in range(EIGHT):
            term = dot(wt_ref[slot], tile_rows(tiles, slot, lanes), 1, 0)
            product = term if product is None else product + term
        if first:
            column = (sums[0][:, lanes] + sums[1][:, lanes]) + sums[2][:, lanes]
            column = jnp.sum(column, axis=0, keepdims=True)
        else:
            column = jnp.zeros((1, BLOCK), F32)
        for at in range(BLOCK // PIECE):
            lane = slice(at * PIECE, (at + 1) * PIECE)
            out_ref[BLOCK // PIECE * index + at, :WIDTH, :] = product[:, lane]
            out_ref[BLOCK // PIECE * index + at, WIDTH:, :] = stat_rows(column[:, lane], second, third)
        return 0

    lax.fori_loop(0, MARKS // BLOCK, body, 0)


def side_terms(first, base, slots, tiles, more):
    return call(
        lambda *refs: side_kernel(first, base, *refs),
        [jax.ShapeDtypeStruct((EIGHT, WIDTH + 8, PIECE), F32)],
        [SMEM] + [VMEM] * (3 + len(more)),
        [slots, *tiles, *more],
        "side_terms",
        scratch=[pltpu.VMEM((EIGHT, WIDTH, OWN), B16)],
        flops=2 * ROWS * MARKS * WIDTH,
    )[0]


def pair_kernel(first, *refs):
    refs = refs[3:]
    if first:
        own_ref, other_ref, out_ref, pair_ref = refs
    else:
        own_ref, other_ref, before_ref, out_ref = refs
    stats = own_ref[0, WIDTH:, :] + other_ref[0, WIDTH:, :]
    second, third = stats[1:2], stats[2:3]
    rounded = columns_of([second[:, WIDTH:]])[:, 0:1]
    for piece in range(EIGHT):
        if first:
            column = own_ref[piece, WIDTH : WIDTH + 8, :] + other_ref[piece, WIDTH : WIDTH + 8, :]
            means = column[0:1] / third[:, 0:1]
            pair_ref[piece : piece + 1, :] = means
        else:
            means = before_ref[piece : piece + 1, :]
        side = own_ref[piece, :WIDTH, :] + other_ref[piece, :WIDTH, :]
        out_ref[piece, :WIDTH, :] = (side - rounded * means).astype(B16)
        out_ref[piece, WIDTH:, :] = tails_in_kernel([means, second, third])


def pair(first, tiles, *args):
    shapes = [jax.ShapeDtypeStruct((EIGHT, WIDTH + 16, PIECE), B16)]
    if first:
        shapes.append(jax.ShapeDtypeStruct((EIGHT, PIECE), F32))
    return call(
        lambda *refs: pair_kernel(first, *refs),
        shapes,
        [VMEM] * (3 + len(args)),
        [*tiles, *args],
        "pair",
        flops=10**9,
    )


def centre_kernel(first, total_rows, *refs):
    refs = refs[3:]
    if first:
        terms_ref, out_ref, means_ref = refs
    else:
        terms_ref, before_ref, out_ref = refs
    tails = [terms_ref[group, WIDTH:, :] for group in range(EIGHT)]
    pairs = [join_at(tail, 0) for tail in tails]
    second = [join_at(tail, 1) for tail in tails]
    third = [join_at(tail, 2) for tail in tails]
    total, every = second[0], third[0]
    for group in range(1, EIGHT):
        total, every = total + second[group], every + third[group]
    columns = columns_of([row[:, WIDTH:] for row in second] + [total[:, :WIDTH], every[:, :WIDTH]])
    if first:
        means = third[0][:, 0:1] * pairs[0]
        for group in range(1, EIGHT):
            means = means + third[group][:, 0:1] * pairs[group]
        means = means / every[:, 0:1]
        means_ref[...] = jnp.broadcast_to(means, (8, PIECE))
    else:
        means = before_ref[0:1]
    side = terms_ref[0, :WIDTH, :].astype(F32) + columns[:, 0:1] * pairs[0]
    for group in range(1, EIGHT):
        side = side + (terms_ref[group, :WIDTH, :].astype(F32) + columns[:, group : group + 1] * pairs[group])
    totals = columns[:, EIGHT : EIGHT + 1]
    if first:
        side = side - totals * means
    else:
        squares = columns[:, EIGHT + 1 : EIGHT + 2]
        side = (side * UP - totals * means) / jnp.sqrt(squares / total_rows + 1e-06)
    side = side.astype(B16)
    tail = tail_in_kernel(means)
    for group in range(EIGHT):
        out_ref[group, :WIDTH, :] = side
        out_ref[group, WIDTH:, :] = tail


def centre(first, total_rows, tiles, *args):
    shapes = [jax.ShapeDtypeStruct((EIGHT, WIDTH + 16, PIECE), B16)]
    if first:
        shapes.append(jax.ShapeDtypeStruct((8, PIECE), F32))
    return call(
        lambda *refs: centre_kernel(first, total_rows, *refs),
        shapes,
        [VMEM] * (3 + len(args)),
        [*tiles, *args],
        "centre",
        flops=10**9,
    )


def image_kernel(base, slots_ref, *refs):
    tiles, half_ref, refs = refs[:3], refs[3], refs[4:]
    if base:
        before_ref, out_ref, side_ref = refs
    else:
        out_ref, side_ref = refs
    shift = jnp.zeros((16, WIDTH), F32)
    for piece in range(EIGHT):
        side = half_ref[piece, :WIDTH, :]
        side_ref[:, piece * PIECE : (piece + 1) * PIECE] = side
        shift = shift + dot(half_ref[piece, WIDTH:, :], side, 1, 1)
    shift = (shift[2:3] + shift[1:2]) + shift[0:1]
    slot = 0
    for tile in tiles:
        count = tile.shape[0] // OWN
        term = dot(tile[:, base : base + MARKS], side_ref[...], 1, 1) - shift
        if base:
            term = term + before_ref[slot * OWN : (slot + count) * OWN, :]
            for at in range(count):
                out_ref[slots_ref[slot + at]] = term[at * OWN : (at + 1) * OWN].astype(B16)
        else:
            out_ref[slot * OWN : (slot + count) * OWN, :] = term
        slot += count


def image_terms(slots, tiles, half, before=None):
    if before is None:
        base, more, shape = 0, [], jax.ShapeDtypeStruct((ROWS, WIDTH), F32)
    else:
        base, more, shape = MARKS, [before], jax.ShapeDtypeStruct((EIGHT, OWN, WIDTH), B16)
    return call(
        lambda *refs: image_kernel(base, *refs),
        [shape],
        [SMEM] + [VMEM] * (4 + len(more)),
        [slots, *tiles, half, *more],
        "image_terms",
        scratch=[pltpu.VMEM((WIDTH, MARKS), B16)],
        flops=2 * ROWS * MARKS * WIDTH,
    )[0]


def owner_kernel(last, *refs):
    if not last:
        refs = refs[3:]
    terms_ref, weight_ref, out_ref, *more = refs
    image = terms_ref[0].astype(F32)
    for member in range(1, EIGHT):
        image = image + terms_ref[member].astype(F32)
    weight = weight_ref[...]
    image = weight * image
    squares = jnp.sum(image * image, axis=0, keepdims=True)
    if last:
        out_ref[...] = image
        more[0][...] = jnp.broadcast_to(squares, (8, WIDTH))
    else:
        product = weight * image
        totals = jnp.sum(product, axis=0, keepdims=True)
        body = jnp.transpose(product * DOWN).astype(B16)
        tail = tail_in_kernel(jnp.concatenate([totals, squares], axis=1))
        for member in range(EIGHT):
            out_ref[member, :WIDTH, :] = body
            out_ref[member, WIDTH:, :] = tail


def owner(last, tiles, terms, weight):
    if last:
        shapes = [jax.ShapeDtypeStruct((OWN, WIDTH), F32), jax.ShapeDtypeStruct((8, WIDTH), F32)]
        tiles = []
    else:
        shapes = [jax.ShapeDtypeStruct((EIGHT, WIDTH + 16, OWN), B16)]
    return call(
        lambda *refs: owner_kernel(last, *refs),
        shapes,
        [VMEM] * (len(tiles) + 2),
        [*tiles, terms, weight],
        "owner",
        flops=10**9,
    )


def exchange(payload, axes):
    return lax.all_to_all(payload, axes, 0, 0)


def swap_core(values):
    return lax.ppermute(values, "core", [(0, 1), (1, 0)])


def swap_z(values):
    return lax.ppermute(values, "zl", [(0, 1), (1, 0)])


def from_below(values):
    return lax.ppermute(values, "x", [(at, (at + 1) % 4) for at in range(4)])


def from_above(values):
    return lax.ppermute(values, "x", [(at, (at + 3) % 4) for at in range(4)])


def pack_kernel(rows_ref, start_ref, weight_ref, out_ref, wide_ref):
    values = rows_ref[...].astype(F32)
    scale = lax.rsqrt(jnp.sum(values * values, axis=1, keepdims=True) + 1e-06)
    out_ref[:OWN, :] = (values * scale).astype(B16)
    weight = weight_ref[...]
    wide = jnp.transpose(jnp.broadcast_to(weight, (WIDTH, OWN)))
    wide_ref[...] = wide
    product = wide * start_ref[...]
    totals = jnp.sum(product, axis=0, keepdims=True)
    vectors = jnp.transpose(product).astype(B16)
    half = WIDTH // 2
    out_ref[OWN : OWN + half, :OWN] = vectors[:half]
    out_ref[OWN : OWN + half, OWN:] = vectors[half:]
    rest = jnp.zeros((1, OWN - WIDTH), F32)
    out_ref[OWN + half :, :] = tail_in_kernel(jnp.concatenate([weight, totals, rest], axis=1))


def pack(rows, start, weight):
    shapes = [jax.ShapeDtypeStruct((PACK, rows.shape[1]), B16), jax.ShapeDtypeStruct((OWN, WIDTH), F32)]
    return call(pack_kernel, shapes, [VMEM] * 3, [rows, start, weight], "pack")


def slot_owners():
    x, z = lax.axis_index("x"), lax.axis_index("zl")
    moves = [(0, 0), (3, 0), (1, 0), (0, 1), (2, 0), (1, 1), (3, 1), (2, 1)]
    return jnp.stack([(x + dx) % 4 * 2 + (z + dz) % 2 for dx, dz in moves]).astype(jnp.int32)


def local(embeddings, landmarks, start_vectors, row_weight, spread):
    total_rows = embeddings.shape[0] * lax.axis_size(AXES)
    slots = slot_owners()
    packed, weight = pack(embeddings, start_vectors, row_weight[None, :])
    below, above, across = from_below(packed), from_above(packed), swap_z(packed)
    far = unit_rows(swap_core(landmarks))
    near = unit_rows(landmarks)
    opposite, across_above, across_below = from_below(below), from_above(across), swap_z(below)
    packs = [packed, below, above, across, opposite, across_above, across_below]
    one, sums_one = build((2, 2), 1024, spread, packs[:4], near, far)
    opposite, sums_one = lax.optimization_barrier((opposite, sums_one))
    last = swap_z(opposite)
    packs[4] = opposite
    packs.append(last)
    two, sums_two = build((3,), 512, spread, packs[4:7], near, far)
    last, sums_two = lax.optimization_barrier((last, sums_two))
    packs[7] = last
    three, sums_three = build((1,), 1024, spread, packs[7:], near, far)
    tiles = (one, two, three)
    first = [*packs, sums_one, sums_two, sums_three]
    for step in range(ITERS):
        more = first if step == 0 else [vectors]
        other = swap_core(side_terms(step == 0, MARKS, slots, tiles, more))
        own = side_terms(step == 0, 0, slots, tiles, more)
        if step == 0:
            payload, pair_means = pair(True, tiles, own, other)
            sides, means = centre(True, total_rows, tiles, exchange(payload, MARK_AXES))
        else:
            (payload,) = pair(False, tiles, own, other, pair_means)
            (sides,) = centre(False, total_rows, tiles, exchange(payload, MARK_AXES), means)
        sides = exchange(sides, MARK_AXES)
        across_core = swap_core(sides)
        parts = image_terms(slots, tiles, across_core, image_terms(slots, tiles, sides))
        parts = exchange(parts, ROW_AXES)
        if step + 1 < ITERS:
            (vectors,) = owner(False, tiles, parts, weight)
            vectors = exchange(vectors, ROW_AXES)
    image, squares = owner(True, tiles, parts, weight)
    count = lax.axis_size(AXES)
    every = exchange(jnp.broadcast_to(squares[:1][None], (count, 1, WIDTH)), AXES)
    scale = jnp.sqrt(jnp.sum(every[:, 0], axis=0) / total_rows + 1e-06)
    return image / scale[None, :]


def solution(mesh):
    fine = Mesh(mesh.devices.reshape(4, 2, 4, 2, 2), AXES)
    rows = P(AXES, None)
    in_specs = (rows, P(("x", "zl", "core"), None), rows, P(AXES), P())
    return jax.shard_map(local, mesh=fine, in_specs=in_specs, out_specs=rows, check_vma=False)
```

```python
import jax
import jax.numpy as jnp
from jax import lax
from jax.experimental import pallas as pl
from jax.experimental.pallas import tpu as pltpu
from jax.sharding import Mesh
from jax.sharding import PartitionSpec as P

ITERS = 2
AXES = ("y", "zh", "x", "zl", "core")
ROW_AXES = ("x", "zl")
MARK_AXES = ("y", "zh")
F32, B16 = jnp.float32, jnp.bfloat16
DOWN = 2.0**-20
UP = 2.0**20
LOG2E = 1.4426950408889634
VMEM = pl.BlockSpec(memory_space=pltpu.VMEM)
SMEM = pl.BlockSpec(memory_space=pltpu.SMEM)
OWN = 256
PIECE = 256
WIDTH = 128
MARKS = 2048
EIGHT = 8
ROWS = EIGHT * OWN
PACK = OWN + WIDTH // 2 + 16
BLOCK = 4 * PIECE
THIRD = PACK // 3
TILES = 4


def params(mib):
    return pltpu.CompilerParams(vmem_limit_bytes=mib * 2**20)


def dot(left, right, left_dim, right_dim):
    dims = (((left_dim,), (right_dim,)), ((), ()))
    return lax.dot_general(left, right, dims, preferred_element_type=F32)


def parts_in_kernel(values):
    high = values.astype(B16)
    rest = values - high.astype(F32)
    mid = rest.astype(B16)
    low = (rest - mid.astype(F32)).astype(B16)
    return high.astype(F32), mid.astype(F32), low.astype(F32)


def tail_in_kernel(row):
    at = lax.broadcasted_iota(jnp.int32, (16, row.shape[1]), 0)
    high, mid, low = parts_in_kernel(row)
    zero = jnp.zeros((16, row.shape[1]), F32)
    block = jnp.where(at == 0, high, jnp.where(at == 1, mid, jnp.where(at == 2, low, zero)))
    return block.astype(B16)


def join_tail(block):
    block = block.astype(F32)
    return (block[2:3] + block[1:2]) + block[0:1]


def stat_rows(first, second, third):
    at = lax.broadcasted_iota(jnp.int32, (8, PIECE), 0)
    zero = jnp.zeros((8, PIECE), F32)
    return jnp.where(at == 0, first, jnp.where(at == 1, second, jnp.where(at == 2, third, zero)))


def tails_in_kernel(rows):
    at = lax.broadcasted_iota(jnp.int32, (16, rows[0].shape[1]), 0)
    block = jnp.zeros(at.shape, F32)
    for index, row in enumerate(rows):
        for part, value in enumerate(parts_in_kernel(row)):
            block = jnp.where(at == 3 * index + part, value, block)
    return block.astype(B16)


def join_at(block, index):
    block = block[3 * index : 3 * index + 3].astype(F32)
    return (block[2:3] + block[1:2]) + block[0:1]


def columns_of(rows):
    at = lax.broadcasted_iota(jnp.int32, (WIDTH, WIDTH), 0)
    block = jnp.zeros((WIDTH, WIDTH), F32)
    for index, row in enumerate(rows):
        block = jnp.where(at == index, row, block)
    return jnp.transpose(block)


def call(kernel, shapes, specs, args, name, scratch=(), flops=0, mib=24):
    cost = pl.CostEstimate(flops=flops, bytes_accessed=0, transcendentals=0)
    return pl.pallas_call(
        kernel,
        out_shape=shapes,
        in_specs=specs,
        out_specs=[VMEM] * len(shapes),
        scratch_shapes=list(scratch),
        compiler_params=params(mib),
        cost_estimate=cost,
        name=name,
    )(*args)


def rows_of(refs):
    if len(refs) == 1:
        return refs[0][:OWN, :]
    return jnp.concatenate([refs[0][...], refs[1][...], refs[2][: OWN - 2 * THIRD, :]], axis=0)


def rest_of(refs, start, stop, lanes=slice(None)):
    skip = 0 if len(refs) == 1 else 2 * THIRD
    return refs[-1][start - skip : stop - skip, lanes]


def take(refs, counts):
    taken = []
    for count in counts:
        taken.append(refs[:count])
        refs = refs[count:]
    return taken, refs


def unit_kernel(in_ref, out_ref):
    block = 2 * OWN

    def body(index, _):
        rows = pl.ds(pl.multiple_of(index * block, block), block)
        values = in_ref[rows, :].astype(F32)
        scale = lax.rsqrt(jnp.sum(values * values, axis=1, keepdims=True) + 1e-06)
        out_ref[rows, :] = (values * scale).astype(B16)
        return 0

    lax.fori_loop(0, MARKS // block, body, 0)


def unit(values):
    shape = jax.ShapeDtypeStruct(values.shape, B16)
    return call(unit_kernel, [shape], [VMEM], [values], "unit", flops=2 * 10**9)[0]


def build_kernel(counts, groups, block, *refs):
    spread_ref = refs[0]
    packed, refs = take(refs[1:], counts)
    near_ref, far_ref, tile_ref, sums_ref, wide_ref = refs
    gamma = spread_ref[0] * LOG2E
    for source, parts in enumerate(packed):
        weight = join_tail(rest_of(parts, PACK - 16, PACK))[:, :OWN]
        column = jnp.transpose(jnp.broadcast_to(weight, (WIDTH, OWN)))
        wide_ref[source * OWN : (source + 1) * OWN, :] = column

    def half_of(marks_ref, base):
        def body(index, _):
            start = pl.multiple_of(index * block, block)
            marks = marks_ref[pl.ds(start, block), :]
            lanes = pl.ds(pl.multiple_of(base + start, block), block)
            sums = [jnp.zeros((8, WIDTH), F32) for _ in range(block // WIDTH)]
            first = 0
            for size in groups:
                rows = jnp.concatenate([rows_of(parts) for parts in packed[first : first + size]], axis=0)
                values = jnp.exp2(dot(rows, marks, 1, 1) * gamma)
                at = slice(first * OWN, (first + size) * OWN)
                tile_ref[at, lanes] = values.astype(B16)
                wide = wide_ref[at, :]
                for lane in range(block // WIDTH):
                    term = values[:, lane * WIDTH : (lane + 1) * WIDTH] * wide
                    sums[lane] = sums[lane] + jnp.sum(term.reshape(-1, 8, WIDTH), axis=0)
                first += size
            sums_ref[:, lanes] = jnp.concatenate(sums, axis=1)
            return 0

        lax.fori_loop(0, MARKS // block, body, 0)

    half_of(near_ref, 0)
    half_of(far_ref, MARKS)


def build(groups, block, spread, packed, near, far):
    rows = sum(groups) * OWN
    counts = [len(parts) for parts in packed]
    flat = [part for parts in packed for part in parts]
    return call(
        lambda *refs: build_kernel(counts, groups, block, *refs),
        [pltpu.VMEM((rows, 2 * MARKS), B16), jax.ShapeDtypeStruct((8, 2 * MARKS), F32)],
        [SMEM] + [VMEM] * (len(flat) + 2),
        [spread, *flat, near, far],
        "build",
        scratch=[pltpu.VMEM((rows, WIDTH), F32)],
        flops=4 * rows * 2 * MARKS * 512,
    )


def tile_rows(tiles, slot, lanes):
    for tile in tiles:
        if slot * OWN < tile.shape[0]:
            return tile[slot * OWN : (slot + 1) * OWN, lanes]
        slot -= tile.shape[0] // OWN


def side_kernel(first, base, *refs):
    slots_ref, tiles, refs = refs[0], refs[1 : 1 + TILES], refs[1 + TILES :]
    zero = jnp.zeros((1, PIECE - WIDTH), F32)
    ones = jnp.ones((16, OWN), B16)
    totals = jnp.zeros((1, WIDTH), F32)
    third = jnp.zeros((1, WIDTH), F32)
    rounded = jnp.zeros((16, WIDTH), F32)
    half = WIDTH // 2
    if first:
        packed, refs = take(refs, [1] * 7 + [3])
        sums, (out_ref, wt_ref) = refs[:TILES], refs[TILES:]
    else:
        packed_ref, out_ref, wt_ref = refs
    for slot in range(EIGHT):
        if first:
            wt_ref[slot, :half] = rest_of(packed[slot], OWN, OWN + half, slice(0, OWN))
            wt_ref[slot, half:] = rest_of(packed[slot], OWN, OWN + half, slice(OWN, 2 * OWN))
            tail = join_tail(rest_of(packed[slot], OWN + half, PACK))
            totals = totals + tail[:, OWN : OWN + WIDTH]
            third = third + jnp.sum(tail[:, :OWN], axis=1, keepdims=True)
        else:
            wt_ref[slot] = packed_ref[slots_ref[slot], :WIDTH, :]
            tail = join_tail(packed_ref[slot, WIDTH:, :])
            totals = totals + tail[:, :WIDTH]
            third = third + tail[:, WIDTH:]
        rounded = rounded + dot(ones, wt_ref[slot], 1, 1)
    second = jnp.concatenate([totals, rounded[:1]], axis=1)
    third = jnp.concatenate([third, zero], axis=1)

    def body(index, _):
        lanes = pl.ds(pl.multiple_of(base + index * BLOCK, BLOCK), BLOCK)
        product = None
        for slot in range(EIGHT):
            term = dot(wt_ref[slot], tile_rows(tiles, slot, lanes), 1, 0)
            product = term if product is None else product + term
        if first:
            column = sums[0][:, lanes]
            for more in sums[1:]:
                column = column + more[:, lanes]
            column = jnp.sum(column, axis=0, keepdims=True)
        else:
            column = jnp.zeros((1, BLOCK), F32)
        for at in range(BLOCK // PIECE):
            lane = slice(at * PIECE, (at + 1) * PIECE)
            out_ref[BLOCK // PIECE * index + at, :WIDTH, :] = product[:, lane]
            out_ref[BLOCK // PIECE * index + at, WIDTH:, :] = stat_rows(column[:, lane], second, third)
        return 0

    lax.fori_loop(0, MARKS // BLOCK, body, 0)


def side_terms(first, base, slots, tiles, more):
    return call(
        lambda *refs: side_kernel(first, base, *refs),
        [jax.ShapeDtypeStruct((EIGHT, WIDTH + 8, PIECE), F32)],
        [SMEM] + [VMEM] * (TILES + len(more)),
        [slots, *tiles, *more],
        "side_terms",
        scratch=[pltpu.VMEM((EIGHT, WIDTH, OWN), B16)],
        flops=2 * ROWS * MARKS * WIDTH,
    )[0]


def pair_kernel(first, *refs):
    refs = refs[TILES:]
    if first:
        own_ref, other_ref, out_ref, pair_ref = refs
    else:
        own_ref, other_ref, before_ref, out_ref = refs
    stats = own_ref[0, WIDTH:, :] + other_ref[0, WIDTH:, :]
    second, third = stats[1:2], stats[2:3]
    rounded = columns_of([second[:, WIDTH:]])[:, 0:1]
    for piece in range(EIGHT):
        if first:
            column = own_ref[piece, WIDTH : WIDTH + 8, :] + other_ref[piece, WIDTH : WIDTH + 8, :]
            means = column[0:1] / third[:, 0:1]
            pair_ref[piece : piece + 1, :] = means
        else:
            means = before_ref[piece : piece + 1, :]
        side = own_ref[piece, :WIDTH, :] + other_ref[piece, :WIDTH, :]
        out_ref[piece, :WIDTH, :] = (side - rounded * means).astype(B16)
        out_ref[piece, WIDTH:, :] = tails_in_kernel([means, second, third])


def pair(first, tiles, *args):
    shapes = [jax.ShapeDtypeStruct((EIGHT, WIDTH + 16, PIECE), B16)]
    if first:
        shapes.append(jax.ShapeDtypeStruct((EIGHT, PIECE), F32))
    return call(
        lambda *refs: pair_kernel(first, *refs),
        shapes,
        [VMEM] * (TILES + len(args)),
        [*tiles, *args],
        "pair",
        flops=10**9,
    )


def centre_kernel(first, total_rows, *refs):
    refs = refs[TILES:]
    if first:
        terms_ref, out_ref, means_ref = refs
    else:
        terms_ref, before_ref, out_ref = refs
    tails = [terms_ref[group, WIDTH:, :] for group in range(EIGHT)]
    pairs = [join_at(tail, 0) for tail in tails]
    second = [join_at(tail, 1) for tail in tails]
    third = [join_at(tail, 2) for tail in tails]
    total, every = second[0], third[0]
    for group in range(1, EIGHT):
        total, every = total + second[group], every + third[group]
    columns = columns_of([row[:, WIDTH:] for row in second] + [total[:, :WIDTH], every[:, :WIDTH]])
    if first:
        means = third[0][:, 0:1] * pairs[0]
        for group in range(1, EIGHT):
            means = means + third[group][:, 0:1] * pairs[group]
        means = means / every[:, 0:1]
        means_ref[...] = jnp.broadcast_to(means, (8, PIECE))
    else:
        means = before_ref[0:1]
    side = terms_ref[0, :WIDTH, :].astype(F32) + columns[:, 0:1] * pairs[0]
    for group in range(1, EIGHT):
        side = side + (terms_ref[group, :WIDTH, :].astype(F32) + columns[:, group : group + 1] * pairs[group])
    totals = columns[:, EIGHT : EIGHT + 1]
    if first:
        side = side - totals * means
    else:
        squares = columns[:, EIGHT + 1 : EIGHT + 2]
        side = (side * UP - totals * means) / jnp.sqrt(squares / total_rows + 1e-06)
    side = side.astype(B16)
    for group in range(EIGHT):
        out_ref[group, :WIDTH, :] = side
        if first:
            out_ref[group, WIDTH:, :] = tail_in_kernel(means)


def centre(first, total_rows, tiles, *args):
    shapes = [jax.ShapeDtypeStruct((EIGHT, WIDTH + 16 * first, PIECE), B16)]
    if first:
        shapes.append(jax.ShapeDtypeStruct((8, PIECE), F32))
    return call(
        lambda *refs: centre_kernel(first, total_rows, *refs),
        shapes,
        [VMEM] * (TILES + len(args)),
        [*tiles, *args],
        "centre",
        flops=10**9,
    )


def image_kernel(base, slots_ref, *refs):
    tiles, (half_ref, means_ref), refs = refs[:TILES], refs[TILES : TILES + 2], refs[TILES + 2 :]
    if base:
        before_ref, out_ref, side_ref = refs
    else:
        out_ref, side_ref = refs
    shift = jnp.zeros((16, WIDTH), F32)
    for piece in range(EIGHT):
        side = half_ref[piece, :WIDTH, :]
        side_ref[:, piece * PIECE : (piece + 1) * PIECE] = side
        shift = shift + dot(means_ref[piece, WIDTH:, :], side, 1, 1)
    shift = (shift[2:3] + shift[1:2]) + shift[0:1]
    slot = 0
    for tile in tiles:
        count = tile.shape[0] // OWN
        term = dot(tile[:, base : base + MARKS], side_ref[...], 1, 1) - shift
        if base:
            term = term + before_ref[slot * OWN : (slot + count) * OWN, :]
            for at in range(count):
                out_ref[slots_ref[slot + at]] = term[at * OWN : (at + 1) * OWN].astype(B16)
        else:
            out_ref[slot * OWN : (slot + count) * OWN, :] = term
        slot += count


def image_terms(slots, tiles, half, means, before=None):
    if before is None:
        base, more, shape = 0, [], jax.ShapeDtypeStruct((ROWS, WIDTH), F32)
    else:
        base, more, shape = MARKS, [before], jax.ShapeDtypeStruct((EIGHT, OWN, WIDTH), B16)
    return call(
        lambda *refs: image_kernel(base, *refs),
        [shape],
        [SMEM] + [VMEM] * (TILES + 2 + len(more)),
        [slots, *tiles, half, means, *more],
        "image_terms",
        scratch=[pltpu.VMEM((WIDTH, MARKS), B16)],
        flops=2 * ROWS * MARKS * WIDTH,
    )[0]


def owner_kernel(last, *refs):
    if not last:
        refs = refs[TILES:]
    terms_ref, weight_ref, out_ref, *more = refs
    image = terms_ref[0].astype(F32)
    for member in range(1, EIGHT):
        image = image + terms_ref[member].astype(F32)
    weight = weight_ref[...]
    image = weight * image
    squares = jnp.sum(image * image, axis=0, keepdims=True)
    if last:
        out_ref[...] = image
        more[0][...] = jnp.broadcast_to(squares, (8, WIDTH))
    else:
        product = weight * image
        totals = jnp.sum(product, axis=0, keepdims=True)
        body = jnp.transpose(product * DOWN).astype(B16)
        tail = tail_in_kernel(jnp.concatenate([totals, squares], axis=1))
        for member in range(EIGHT):
            out_ref[member, :WIDTH, :] = body
            out_ref[member, WIDTH:, :] = tail


def owner(last, tiles, terms, weight):
    if last:
        shapes = [jax.ShapeDtypeStruct((OWN, WIDTH), F32), jax.ShapeDtypeStruct((8, WIDTH), F32)]
        tiles = []
    else:
        shapes = [jax.ShapeDtypeStruct((EIGHT, WIDTH + 16, OWN), B16)]
    return call(
        lambda *refs: owner_kernel(last, *refs),
        shapes,
        [VMEM] * (len(tiles) + 2),
        [*tiles, terms, weight],
        "owner",
        flops=10**9,
    )


def exchange(payload, axes):
    return lax.all_to_all(payload, axes, 0, 0)


def swap_core(values):
    return lax.ppermute(values, "core", [(0, 1), (1, 0)])


def swap_z(values):
    return lax.ppermute(values, "zl", [(0, 1), (1, 0)])


def from_below(values):
    return lax.ppermute(values, "x", [(at, (at + 1) % 4) for at in range(4)])


def from_above(values):
    return lax.ppermute(values, "x", [(at, (at + 3) % 4) for at in range(4)])


def pack_kernel(rows_ref, start_ref, weight_ref, out_ref, wide_ref):
    values = rows_ref[...].astype(F32)
    scale = lax.rsqrt(jnp.sum(values * values, axis=1, keepdims=True) + 1e-06)
    out_ref[:OWN, :] = (values * scale).astype(B16)
    weight = weight_ref[...]
    wide = jnp.transpose(jnp.broadcast_to(weight, (WIDTH, OWN)))
    wide_ref[...] = wide
    product = wide * start_ref[...]
    totals = jnp.sum(product, axis=0, keepdims=True)
    vectors = jnp.transpose(product).astype(B16)
    half = WIDTH // 2
    out_ref[OWN : OWN + half, :OWN] = vectors[:half]
    out_ref[OWN : OWN + half, OWN:] = vectors[half:]
    rest = jnp.zeros((1, OWN - WIDTH), F32)
    out_ref[OWN + half :, :] = tail_in_kernel(jnp.concatenate([weight, totals, rest], axis=1))


def pack(rows, start, weight):
    shapes = [jax.ShapeDtypeStruct((PACK, rows.shape[1]), B16), jax.ShapeDtypeStruct((OWN, WIDTH), F32)]
    return call(pack_kernel, shapes, [VMEM] * 3, [rows, start, weight], "pack")


def slot_owners():
    x, z = lax.axis_index("x"), lax.axis_index("zl")
    moves = [(0, 0), (3, 0), (1, 0), (0, 1), (2, 0), (1, 1), (3, 1), (2, 1)]
    return jnp.stack([(x + dx) % 4 * 2 + (z + dz) % 2 for dx, dz in moves]).astype(jnp.int32)


def local(embeddings, landmarks, start_vectors, row_weight, spread):
    total_rows = embeddings.shape[0] * lax.axis_size(AXES)
    slots = slot_owners()
    packed, weight = pack(embeddings, start_vectors, row_weight[None, :])
    below, above, across = from_below(packed), from_above(packed), swap_z(packed)
    near = unit(landmarks)
    far = unit(swap_core(landmarks))
    zero, sums_zero = build((1,), 1024, spread, [[packed]], near, far)
    below, above, across, sums_zero = lax.optimization_barrier((below, above, across, sums_zero))
    opposite, across_above, across_below = from_below(below), from_above(across), swap_z(below)
    one, sums_one = build((3,), 512, spread, [[below], [above], [across]], near, far)
    opposite, across_above, across_below, sums_one = lax.optimization_barrier(
        (opposite, across_above, across_below, sums_one)
    )
    last = [
        swap_z(opposite[:THIRD]),
        from_above(across_above[THIRD : 2 * THIRD]),
        from_below(across_below[2 * THIRD :]),
    ]
    two, sums_two = build((3,), 512, spread, [[opposite], [across_above], [across_below]], near, far)
    *last, sums_two = lax.optimization_barrier((*last, sums_two))
    three, sums_three = build((1,), 1024, spread, [last], near, far)
    packs = [packed, below, above, across, opposite, across_above, across_below, *last]
    tiles = (zero, one, two, three)
    first = [*packs, sums_zero, sums_one, sums_two, sums_three]
    for step in range(ITERS):
        more = first if step == 0 else [vectors]
        other = swap_core(side_terms(step == 0, MARKS, slots, tiles, more))
        own = side_terms(step == 0, 0, slots, tiles, more)
        if step == 0:
            payload, pair_means = pair(True, tiles, own, other)
            sides, means = centre(True, total_rows, tiles, exchange(payload, MARK_AXES))
        else:
            (payload,) = pair(False, tiles, own, other, pair_means)
            (sides,) = centre(False, total_rows, tiles, exchange(payload, MARK_AXES), means)
        sides = exchange(sides, MARK_AXES)
        across_core = swap_core(sides)
        if step == 0:
            tails = (sides, across_core)
        parts = image_terms(slots, tiles, sides, tails[0])
        parts = image_terms(slots, tiles, across_core, tails[1], parts)
        parts = exchange(parts, ROW_AXES)
        if step + 1 < ITERS:
            (vectors,) = owner(False, tiles, parts, weight)
            vectors = exchange(vectors, ROW_AXES)
    image, squares = owner(True, tiles, parts, weight)
    count = lax.axis_size(AXES)
    every = exchange(jnp.broadcast_to(squares[:1][None], (count, 1, WIDTH)), AXES)
    scale = jnp.sqrt(jnp.sum(every[:, 0], axis=0) / total_rows + 1e-06)
    return image / scale[None, :]


def solution(mesh):
    fine = Mesh(mesh.devices.reshape(4, 2, 4, 2, 2), AXES)
    rows = P(AXES, None)
    in_specs = (rows, P(("x", "zl", "core"), None), rows, P(AXES), P())
    return jax.shard_map(local, mesh=fine, in_specs=in_specs, out_specs=rows, check_vma=False)
```

```python
import jax
import jax.numpy as jnp
from jax import lax
from jax.experimental import pallas as pl
from jax.experimental.pallas import tpu as pltpu
from jax.sharding import Mesh
from jax.sharding import PartitionSpec as P

ITERS = 2
AXES = ("y", "zh", "x", "zl", "core")
ROW_AXES = ("x", "zl")
MARK_AXES = ("y", "zh")
F32, B16 = jnp.float32, jnp.bfloat16
DOWN = 2.0**-20
UP = 2.0**20
LOG2E = 1.4426950408889634
VMEM = pl.BlockSpec(memory_space=pltpu.VMEM)
SMEM = pl.BlockSpec(memory_space=pltpu.SMEM)
OWN = 256
PIECE = 256
WIDTH = 128
MARKS = 2048
EIGHT = 8
ROWS = EIGHT * OWN
PACK = OWN + WIDTH // 2 + 16
BLOCK = 8 * PIECE
THIRD = PACK // 3
TILES = 4


def params(mib):
    return pltpu.CompilerParams(vmem_limit_bytes=mib * 2**20)


def dot(left, right, left_dim, right_dim):
    dims = (((left_dim,), (right_dim,)), ((), ()))
    return lax.dot_general(left, right, dims, preferred_element_type=F32)


def parts_in_kernel(values):
    high = values.astype(B16)
    rest = values - high.astype(F32)
    mid = rest.astype(B16)
    low = (rest - mid.astype(F32)).astype(B16)
    return high.astype(F32), mid.astype(F32), low.astype(F32)


def tail_in_kernel(row):
    at = lax.broadcasted_iota(jnp.int32, (16, row.shape[1]), 0)
    high, mid, low = parts_in_kernel(row)
    zero = jnp.zeros((16, row.shape[1]), F32)
    block = jnp.where(at == 0, high, jnp.where(at == 1, mid, jnp.where(at == 2, low, zero)))
    return block.astype(B16)


def join_tail(block):
    block = block.astype(F32)
    return (block[2:3] + block[1:2]) + block[0:1]


def stat_rows(first, second, third):
    at = lax.broadcasted_iota(jnp.int32, (8, PIECE), 0)
    zero = jnp.zeros((8, PIECE), F32)
    return jnp.where(at == 0, first, jnp.where(at == 1, second, jnp.where(at == 2, third, zero)))


def tails_in_kernel(rows):
    at = lax.broadcasted_iota(jnp.int32, (16, rows[0].shape[1]), 0)
    block = jnp.zeros(at.shape, F32)
    for index, row in enumerate(rows):
        for part, value in enumerate(parts_in_kernel(row)):
            block = jnp.where(at == 3 * index + part, value, block)
    return block.astype(B16)


def join_at(block, index):
    block = block[3 * index : 3 * index + 3].astype(F32)
    return (block[2:3] + block[1:2]) + block[0:1]


def columns_of(rows):
    at = lax.broadcasted_iota(jnp.int32, (WIDTH, WIDTH), 0)
    block = jnp.zeros((WIDTH, WIDTH), F32)
    for index, row in enumerate(rows):
        block = jnp.where(at == index, row, block)
    return jnp.transpose(block)


def call(kernel, shapes, specs, args, name, scratch=(), flops=0, mib=24):
    cost = pl.CostEstimate(flops=flops, bytes_accessed=0, transcendentals=0)
    return pl.pallas_call(
        kernel,
        out_shape=shapes,
        in_specs=specs,
        out_specs=[VMEM] * len(shapes),
        scratch_shapes=list(scratch),
        compiler_params=params(mib),
        cost_estimate=cost,
        name=name,
    )(*args)


def rows_of(refs):
    if len(refs) == 1:
        return refs[0][:OWN, :]
    return jnp.concatenate([refs[0][...], refs[1][...], refs[2][: OWN - 2 * THIRD, :]], axis=0)


def rest_of(refs, start, stop, lanes=slice(None)):
    skip = 0 if len(refs) == 1 else 2 * THIRD
    return refs[-1][start - skip : stop - skip, lanes]


def take(refs, counts):
    taken = []
    for count in counts:
        taken.append(refs[:count])
        refs = refs[count:]
    return taken, refs


def unit_kernel(in_ref, out_ref):
    block = 2 * OWN

    def body(index, _):
        rows = pl.ds(pl.multiple_of(index * block, block), block)
        values = in_ref[rows, :].astype(F32)
        scale = lax.rsqrt(jnp.sum(values * values, axis=1, keepdims=True) + 1e-06)
        out_ref[rows, :] = (values * scale).astype(B16)
        return 0

    lax.fori_loop(0, MARKS // block, body, 0)


def unit(values):
    shape = jax.ShapeDtypeStruct(values.shape, B16)
    return call(unit_kernel, [shape], [VMEM], [values], "unit", flops=2 * 10**9)[0]


def build_kernel(counts, groups, block, *refs):
    spread_ref = refs[0]
    packed, refs = take(refs[1:], counts)
    near_ref, far_ref, tile_ref, sums_ref, wide_ref = refs
    gamma = spread_ref[0] * LOG2E
    for source, parts in enumerate(packed):
        weight = join_tail(rest_of(parts, PACK - 16, PACK))[:, :OWN]
        column = jnp.transpose(jnp.broadcast_to(weight, (WIDTH, OWN)))
        wide_ref[source * OWN : (source + 1) * OWN, :] = column

    def half_of(marks_ref, base):
        def body(index, _):
            start = pl.multiple_of(index * block, block)
            marks = marks_ref[pl.ds(start, block), :]
            lanes = pl.ds(pl.multiple_of(base + start, block), block)
            sums = [jnp.zeros((8, WIDTH), F32) for _ in range(block // WIDTH)]
            first = 0
            for size in groups:
                rows = jnp.concatenate([rows_of(parts) for parts in packed[first : first + size]], axis=0)
                values = jnp.exp2(dot(rows, marks, 1, 1) * gamma)
                at = slice(first * OWN, (first + size) * OWN)
                tile_ref[at, lanes] = values.astype(B16)
                wide = wide_ref[at, :]
                for lane in range(block // WIDTH):
                    term = values[:, lane * WIDTH : (lane + 1) * WIDTH] * wide
                    sums[lane] = sums[lane] + jnp.sum(term.reshape(-1, 8, WIDTH), axis=0)
                first += size
            sums_ref[:, lanes] = jnp.concatenate(sums, axis=1)
            return 0

        lax.fori_loop(0, MARKS // block, body, 0)

    half_of(near_ref, 0)
    half_of(far_ref, MARKS)


def build(groups, block, spread, packed, near, far):
    rows = sum(groups) * OWN
    counts = [len(parts) for parts in packed]
    flat = [part for parts in packed for part in parts]
    return call(
        lambda *refs: build_kernel(counts, groups, block, *refs),
        [pltpu.VMEM((rows, 2 * MARKS), B16), jax.ShapeDtypeStruct((8, 2 * MARKS), F32)],
        [SMEM] + [VMEM] * (len(flat) + 2),
        [spread, *flat, near, far],
        "build",
        scratch=[pltpu.VMEM((rows, WIDTH), F32)],
        flops=4 * rows * 2 * MARKS * 512,
    )


def side_kernel(first, base, *refs):
    slots_ref, tiles, refs = refs[0], refs[1 : 1 + TILES], refs[1 + TILES :]
    half = WIDTH // 2
    if first:
        packed, refs = take(refs, [1] * 7 + [3])
        sums, (out_ref, wt_ref) = refs[:TILES], refs[TILES:]
        tails = [rest_of(parts, OWN + half, PACK) for parts in packed]
        for slot, parts in enumerate(packed):
            lanes = slice(slot * OWN, (slot + 1) * OWN)
            wt_ref[:half, lanes] = rest_of(parts, OWN, OWN + half, slice(0, OWN))
            wt_ref[half:, lanes] = rest_of(parts, OWN, OWN + half, slice(OWN, 2 * OWN))
    else:
        packed_ref, out_ref, wt_ref = refs
        for slot in range(EIGHT):
            wt_ref[:, slot * OWN : (slot + 1) * OWN] = packed_ref[slots_ref[slot], :WIDTH, :]
        tails = [packed_ref[source, WIDTH:, :] for source in range(EIGHT)]
    tail = tails[0].astype(F32)
    for more in tails[1:]:
        tail = tail + more.astype(F32)
    if first:
        tail = join_at(tail, 0)
        second = tail[:, OWN:]
        third = jnp.broadcast_to(jnp.sum(tail[:, :OWN], axis=1, keepdims=True), (1, PIECE))
    else:
        one, two = join_at(tail, 0), join_at(tail, 1)
        second = jnp.concatenate([one[:, :WIDTH], two[:, :WIDTH]], axis=1)
        third = jnp.concatenate([one[:, WIDTH:], two[:, WIDTH:]], axis=1)

    def body(index, _):
        lanes = pl.ds(pl.multiple_of(base + index * BLOCK, BLOCK), BLOCK)
        product, start = None, 0
        for tile in tiles:
            stop = start + tile.shape[0]
            term = dot(wt_ref[:, start:stop], tile[:, lanes], 1, 0)
            product, start = (term if product is None else product + term), stop
        if first:
            column = sums[0][:, lanes]
            for more in sums[1:]:
                column = column + more[:, lanes]
            column = jnp.sum(column, axis=0, keepdims=True)
        else:
            column = jnp.zeros((1, BLOCK), F32)
        for at in range(BLOCK // PIECE):
            lane = slice(at * PIECE, (at + 1) * PIECE)
            out_ref[BLOCK // PIECE * index + at, :WIDTH, :] = product[:, lane]
            out_ref[BLOCK // PIECE * index + at, WIDTH:, :] = stat_rows(column[:, lane], second, third)
        return 0

    lax.fori_loop(0, MARKS // BLOCK, body, 0)


def side_terms(first, base, slots, tiles, more):
    return call(
        lambda *refs: side_kernel(first, base, *refs),
        [jax.ShapeDtypeStruct((EIGHT, WIDTH + 8, PIECE), F32)],
        [SMEM] + [VMEM] * (TILES + len(more)),
        [slots, *tiles, *more],
        "side_terms",
        scratch=[pltpu.VMEM((WIDTH, ROWS), B16)],
        flops=2 * ROWS * MARKS * WIDTH,
    )[0]


def pair_kernel(first, *refs):
    refs = refs[TILES:]
    if first:
        own_ref, other_ref, out_ref, pair_ref = refs
    else:
        own_ref, other_ref, before_ref, out_ref = refs
    stats = own_ref[0, WIDTH:, :] + other_ref[0, WIDTH:, :]
    second, third = stats[1:2], stats[2:3]
    rounded = columns_of([second[:, WIDTH:]])[:, 0:1]
    for piece in range(EIGHT):
        if first:
            column = own_ref[piece, WIDTH : WIDTH + 8, :] + other_ref[piece, WIDTH : WIDTH + 8, :]
            means = column[0:1] / third[:, 0:1]
            pair_ref[piece : piece + 1, :] = means
        else:
            means = before_ref[piece : piece + 1, :]
        side = own_ref[piece, :WIDTH, :] + other_ref[piece, :WIDTH, :]
        out_ref[piece, :WIDTH, :] = (side - rounded * means).astype(B16)
        out_ref[piece, WIDTH:, :] = tails_in_kernel([means, second, third])


def pair(first, tiles, *args):
    shapes = [jax.ShapeDtypeStruct((EIGHT, WIDTH + 16, PIECE), B16)]
    if first:
        shapes.append(jax.ShapeDtypeStruct((EIGHT, PIECE), F32))
    return call(
        lambda *refs: pair_kernel(first, *refs),
        shapes,
        [VMEM] * (TILES + len(args)),
        [*tiles, *args],
        "pair",
        flops=10**9,
    )


def centre_kernel(first, total_rows, *refs):
    refs = refs[TILES:]
    if first:
        terms_ref, out_ref, means_ref = refs
    else:
        terms_ref, before_ref, out_ref = refs
    tails = [terms_ref[group, WIDTH:, :] for group in range(EIGHT)]
    pairs = [join_at(tail, 0) for tail in tails]
    second = [join_at(tail, 1) for tail in tails]
    third = [join_at(tail, 2) for tail in tails]
    total, every = second[0], third[0]
    for group in range(1, EIGHT):
        total, every = total + second[group], every + third[group]
    columns = columns_of([row[:, WIDTH:] for row in second] + [total[:, :WIDTH], every[:, :WIDTH]])
    if first:
        means = third[0][:, 0:1] * pairs[0]
        for group in range(1, EIGHT):
            means = means + third[group][:, 0:1] * pairs[group]
        means = means / every[:, 0:1]
        means_ref[...] = jnp.broadcast_to(means, (8, PIECE))
    else:
        means = before_ref[0:1]
    side = terms_ref[0, :WIDTH, :].astype(F32) + columns[:, 0:1] * pairs[0]
    for group in range(1, EIGHT):
        side = side + (terms_ref[group, :WIDTH, :].astype(F32) + columns[:, group : group + 1] * pairs[group])
    totals = columns[:, EIGHT : EIGHT + 1]
    if first:
        side = side - totals * means
    else:
        squares = columns[:, EIGHT + 1 : EIGHT + 2]
        side = (side * UP - totals * means) / jnp.sqrt(squares / total_rows + 1e-06)
    side = side.astype(B16)
    for group in range(EIGHT):
        out_ref[group, :WIDTH, :] = side
        if first:
            out_ref[group, WIDTH:, :] = tail_in_kernel(means)


def centre(first, total_rows, tiles, *args):
    shapes = [jax.ShapeDtypeStruct((EIGHT, WIDTH + 16 * first, PIECE), B16)]
    if first:
        shapes.append(jax.ShapeDtypeStruct((8, PIECE), F32))
    return call(
        lambda *refs: centre_kernel(first, total_rows, *refs),
        shapes,
        [VMEM] * (TILES + len(args)),
        [*tiles, *args],
        "centre",
        flops=10**9,
    )


def image_kernel(base, slots_ref, *refs):
    tiles, (half_ref, means_ref), refs = refs[:TILES], refs[TILES : TILES + 2], refs[TILES + 2 :]
    if base:
        before_ref, out_ref, side_ref, tail_ref = refs
    else:
        out_ref, side_ref, tail_ref = refs
    for piece in range(EIGHT):
        lanes = slice(piece * PIECE, (piece + 1) * PIECE)
        side_ref[:, lanes] = half_ref[piece, :WIDTH, :]
        tail_ref[:, lanes] = means_ref[piece, WIDTH:, :]
    shift = dot(tail_ref[...], side_ref[...], 1, 1)
    shift = (shift[2:3] + shift[1:2]) + shift[0:1]
    slot = 0
    for tile in tiles:
        count = tile.shape[0] // OWN
        term = dot(tile[:, base : base + MARKS], side_ref[...], 1, 1) - shift
        if base:
            term = term + before_ref[slot * OWN : (slot + count) * OWN, :]
            for at in range(count):
                out_ref[slots_ref[slot + at]] = term[at * OWN : (at + 1) * OWN].astype(B16)
        else:
            out_ref[slot * OWN : (slot + count) * OWN, :] = term
        slot += count


def image_terms(slots, tiles, half, means, before=None):
    if before is None:
        base, more, shape = 0, [], jax.ShapeDtypeStruct((ROWS, WIDTH), F32)
    else:
        base, more, shape = MARKS, [before], jax.ShapeDtypeStruct((EIGHT, OWN, WIDTH), B16)
    return call(
        lambda *refs: image_kernel(base, *refs),
        [shape],
        [SMEM] + [VMEM] * (TILES + 2 + len(more)),
        [slots, *tiles, half, means, *more],
        "image_terms",
        scratch=[pltpu.VMEM((WIDTH, MARKS), B16), pltpu.VMEM((16, MARKS), B16)],
        flops=2 * ROWS * MARKS * WIDTH,
    )[0]


def owner_kernel(last, *refs):
    if not last:
        refs = refs[TILES:]
    terms_ref, weight_ref, out_ref, *more = refs
    image = terms_ref[0].astype(F32)
    for member in range(1, EIGHT):
        image = image + terms_ref[member].astype(F32)
    weight = weight_ref[...]
    image = weight * image
    squares = jnp.sum(image * image, axis=0, keepdims=True)
    if last:
        out_ref[...] = image
        more[0][...] = jnp.broadcast_to(squares, (8, WIDTH))
    else:
        product = weight * image
        totals = jnp.sum(product, axis=0, keepdims=True)
        body = (product * DOWN).astype(B16).astype(F32)
        rounded = jnp.sum(body, axis=0, keepdims=True)
        body = jnp.transpose(body).astype(B16)
        first = jnp.concatenate([totals, squares], axis=1)
        second = jnp.concatenate([rounded, jnp.zeros((1, OWN - WIDTH), F32)], axis=1)
        tail = tails_in_kernel([first, second])
        for member in range(EIGHT):
            out_ref[member, :WIDTH, :] = body
            out_ref[member, WIDTH:, :] = tail


def owner(last, tiles, terms, weight):
    if last:
        shapes = [jax.ShapeDtypeStruct((OWN, WIDTH), F32), jax.ShapeDtypeStruct((8, WIDTH), F32)]
        tiles = []
    else:
        shapes = [jax.ShapeDtypeStruct((EIGHT, WIDTH + 16, OWN), B16)]
    return call(
        lambda *refs: owner_kernel(last, *refs),
        shapes,
        [VMEM] * (len(tiles) + 2),
        [*tiles, terms, weight],
        "owner",
        flops=10**9,
    )


def exchange(payload, axes):
    return lax.all_to_all(payload, axes, 0, 0)


def swap_core(values):
    return lax.ppermute(values, "core", [(0, 1), (1, 0)])


def swap_z(values):
    return lax.ppermute(values, "zl", [(0, 1), (1, 0)])


def from_below(values):
    return lax.ppermute(values, "x", [(at, (at + 1) % 4) for at in range(4)])


def from_above(values):
    return lax.ppermute(values, "x", [(at, (at + 3) % 4) for at in range(4)])


def pack_kernel(rows_ref, start_ref, weight_ref, out_ref, wide_ref):
    values = rows_ref[...].astype(F32)
    scale = lax.rsqrt(jnp.sum(values * values, axis=1, keepdims=True) + 1e-06)
    out_ref[:OWN, :] = (values * scale).astype(B16)
    weight = weight_ref[...]
    wide = jnp.transpose(jnp.broadcast_to(weight, (WIDTH, OWN)))
    wide_ref[...] = wide
    product = wide * start_ref[...]
    totals = jnp.sum(product, axis=0, keepdims=True)
    vectors = jnp.transpose(product).astype(B16)
    half = WIDTH // 2
    out_ref[OWN : OWN + half, :OWN] = vectors[:half]
    out_ref[OWN : OWN + half, OWN:] = vectors[half:]
    rounded = jnp.sum(product.astype(B16).astype(F32), axis=0, keepdims=True)
    out_ref[OWN + half :, :] = tail_in_kernel(jnp.concatenate([weight, totals, rounded], axis=1))


def pack(rows, start, weight):
    shapes = [jax.ShapeDtypeStruct((PACK, rows.shape[1]), B16), jax.ShapeDtypeStruct((OWN, WIDTH), F32)]
    return call(pack_kernel, shapes, [VMEM] * 3, [rows, start, weight], "pack")


def slot_owners():
    x, z = lax.axis_index("x"), lax.axis_index("zl")
    moves = [(0, 0), (3, 0), (1, 0), (0, 1), (2, 0), (1, 1), (3, 1), (2, 1)]
    return jnp.stack([(x + dx) % 4 * 2 + (z + dz) % 2 for dx, dz in moves]).astype(jnp.int32)


def local(embeddings, landmarks, start_vectors, row_weight, spread):
    total_rows = embeddings.shape[0] * lax.axis_size(AXES)
    slots = slot_owners()
    packed, weight = pack(embeddings, start_vectors, row_weight[None, :])
    below, above, across = from_below(packed), from_above(packed), swap_z(packed)
    near = unit(landmarks)
    far = unit(swap_core(landmarks))
    zero, sums_zero = build((1,), 2048, spread, [[packed]], near, far)
    below, above, across, sums_zero = lax.optimization_barrier((below, above, across, sums_zero))
    opposite, across_above, across_below = from_below(below), from_above(across), swap_z(below)
    one, sums_one = build((3,), 2048, spread, [[below], [above], [across]], near, far)
    opposite, across_above, across_below, sums_one = lax.optimization_barrier(
        (opposite, across_above, across_below, sums_one)
    )
    last = [
        swap_z(opposite[:THIRD]),
        from_above(across_above[THIRD : 2 * THIRD]),
        from_below(across_below[2 * THIRD :]),
    ]
    two, sums_two = build((3,), 2048, spread, [[opposite], [across_above], [across_below]], near, far)
    *last, sums_two = lax.optimization_barrier((*last, sums_two))
    three, sums_three = build((1,), 2048, spread, [last], near, far)
    packs = [packed, below, above, across, opposite, across_above, across_below, *last]
    tiles = (zero, one, two, three)
    first = [*packs, sums_zero, sums_one, sums_two, sums_three]
    for step in range(ITERS):
        more = first if step == 0 else [vectors]
        other = swap_core(side_terms(step == 0, MARKS, slots, tiles, more))
        own = side_terms(step == 0, 0, slots, tiles, more)
        if step == 0:
            payload, pair_means = pair(True, tiles, own, other)
            sides, means = centre(True, total_rows, tiles, exchange(payload, MARK_AXES))
        else:
            (payload,) = pair(False, tiles, own, other, pair_means)
            (sides,) = centre(False, total_rows, tiles, exchange(payload, MARK_AXES), means)
        sides = exchange(sides, MARK_AXES)
        across_core = swap_core(sides)
        if step == 0:
            tails = (sides, across_core)
        parts = image_terms(slots, tiles, sides, tails[0])
        parts = image_terms(slots, tiles, across_core, tails[1], parts)
        parts = exchange(parts, ROW_AXES)
        if step + 1 < ITERS:
            (vectors,) = owner(False, tiles, parts, weight)
            vectors = exchange(vectors, ROW_AXES)
    image, squares = owner(True, tiles, parts, weight)
    count = lax.axis_size(AXES)
    every = exchange(jnp.broadcast_to(squares[:1][None], (count, 1, WIDTH)), AXES)
    scale = jnp.sqrt(jnp.sum(every[:, 0], axis=0) / total_rows + 1e-06)
    return image / scale[None, :]


def solution(mesh):
    fine = Mesh(mesh.devices.reshape(4, 2, 4, 2, 2), AXES)
    rows = P(AXES, None)
    in_specs = (rows, P(("x", "zl", "core"), None), rows, P(AXES), P())
    return jax.shard_map(local, mesh=fine, in_specs=in_specs, out_specs=rows, check_vma=False)
```

```python
import jax
import jax.numpy as jnp
from jax import lax
from jax.experimental import pallas as pl
from jax.experimental.pallas import tpu as pltpu
from jax.sharding import Mesh
from jax.sharding import PartitionSpec as P

ITERS = 2
AXES = ("y", "zh", "x", "zl", "core")
ROW_AXES = ("x", "zl")
MARK_AXES = ("y", "zh")
F32, B16 = jnp.float32, jnp.bfloat16
DOWN = 2.0**-20
UP = 2.0**20
LOG2E = 1.4426950408889634
VMEM = pl.BlockSpec(memory_space=pltpu.VMEM)
SMEM = pl.BlockSpec(memory_space=pltpu.SMEM)
OWN = 256
PIECE = 256
WIDTH = 128
MARKS = 2048
EIGHT = 8
ROWS = EIGHT * OWN
PACK = OWN + WIDTH // 2 + 16
BLOCK = 8 * PIECE
SPLIT = 160
TILES = 4


def params(mib):
    return pltpu.CompilerParams(vmem_limit_bytes=mib * 2**20)


def dot(left, right, left_dim, right_dim):
    dims = (((left_dim,), (right_dim,)), ((), ()))
    return lax.dot_general(left, right, dims, preferred_element_type=F32)


def parts_in_kernel(values):
    high = values.astype(B16)
    rest = values - high.astype(F32)
    mid = rest.astype(B16)
    low = (rest - mid.astype(F32)).astype(B16)
    return high.astype(F32), mid.astype(F32), low.astype(F32)


def tail_in_kernel(row):
    at = lax.broadcasted_iota(jnp.int32, (16, row.shape[1]), 0)
    high, mid, low = parts_in_kernel(row)
    zero = jnp.zeros((16, row.shape[1]), F32)
    block = jnp.where(at == 0, high, jnp.where(at == 1, mid, jnp.where(at == 2, low, zero)))
    return block.astype(B16)


def join_tail(block):
    block = block.astype(F32)
    return (block[2:3] + block[1:2]) + block[0:1]


def stat_rows(first, second, third):
    at = lax.broadcasted_iota(jnp.int32, (8, PIECE), 0)
    zero = jnp.zeros((8, PIECE), F32)
    return jnp.where(at == 0, first, jnp.where(at == 1, second, jnp.where(at == 2, third, zero)))


def tails_in_kernel(rows):
    at = lax.broadcasted_iota(jnp.int32, (16, rows[0].shape[1]), 0)
    block = jnp.zeros(at.shape, F32)
    for index, row in enumerate(rows):
        for part, value in enumerate(parts_in_kernel(row)):
            block = jnp.where(at == 3 * index + part, value, block)
    return block.astype(B16)


def join_at(block, index):
    block = block[3 * index : 3 * index + 3].astype(F32)
    return (block[2:3] + block[1:2]) + block[0:1]


def columns_of(rows):
    at = lax.broadcasted_iota(jnp.int32, (WIDTH, WIDTH), 0)
    block = jnp.zeros((WIDTH, WIDTH), F32)
    for index, row in enumerate(rows):
        block = jnp.where(at == index, row, block)
    return jnp.transpose(block)


def call(kernel, shapes, specs, args, name, scratch=(), flops=0, mib=24):
    cost = pl.CostEstimate(flops=flops, bytes_accessed=0, transcendentals=0)
    return pl.pallas_call(
        kernel,
        out_shape=shapes,
        in_specs=specs,
        out_specs=[VMEM] * len(shapes),
        scratch_shapes=list(scratch),
        compiler_params=params(mib),
        cost_estimate=cost,
        name=name,
    )(*args)


def rows_of(refs):
    if len(refs) == 1:
        return refs[0][:OWN, :]
    return jnp.concatenate([refs[0][...], refs[1][: OWN - SPLIT, :]], axis=0)


def rest_of(refs, start, stop, lanes=slice(None)):
    skip = 0 if len(refs) == 1 else SPLIT
    return refs[-1][start - skip : stop - skip, lanes]


def take(refs, counts):
    taken = []
    for count in counts:
        taken.append(refs[:count])
        refs = refs[count:]
    return taken, refs


def unit_kernel(in_ref, out_ref):
    block = 2 * OWN

    def body(index, _):
        rows = pl.ds(pl.multiple_of(index * block, block), block)
        values = in_ref[rows, :].astype(F32)
        scale = lax.rsqrt(jnp.sum(values * values, axis=1, keepdims=True) + 1e-06)
        out_ref[rows, :] = (values * scale).astype(B16)
        return 0

    lax.fori_loop(0, MARKS // block, body, 0)


def unit(values):
    shape = jax.ShapeDtypeStruct(values.shape, B16)
    return call(unit_kernel, [shape], [VMEM], [values], "unit", flops=2 * 10**9)[0]


def build_kernel(counts, groups, block, *refs):
    spread_ref = refs[0]
    packed, refs = take(refs[1:], counts)
    near_ref, far_ref, tile_ref, sums_ref, wide_ref = refs
    gamma = spread_ref[0] * LOG2E
    for source, parts in enumerate(packed):
        weight = join_tail(rest_of(parts, PACK - 16, PACK))[:, :OWN]
        column = jnp.transpose(jnp.broadcast_to(weight, (WIDTH, OWN)))
        wide_ref[source * OWN : (source + 1) * OWN, :] = column

    def half_of(marks_ref, base):
        def body(index, _):
            start = pl.multiple_of(index * block, block)
            marks = marks_ref[pl.ds(start, block), :]
            lanes = pl.ds(pl.multiple_of(base + start, block), block)
            sums = [jnp.zeros((8, WIDTH), F32) for _ in range(block // WIDTH)]
            first = 0
            for size in groups:
                rows = jnp.concatenate([rows_of(parts) for parts in packed[first : first + size]], axis=0)
                values = jnp.exp2(dot(rows, marks, 1, 1) * gamma)
                at = slice(first * OWN, (first + size) * OWN)
                tile_ref[at, lanes] = values.astype(B16)
                wide = wide_ref[at, :]
                for lane in range(block // WIDTH):
                    term = values[:, lane * WIDTH : (lane + 1) * WIDTH] * wide
                    sums[lane] = sums[lane] + jnp.sum(term.reshape(-1, 8, WIDTH), axis=0)
                first += size
            sums_ref[:, lanes] = jnp.concatenate(sums, axis=1)
            return 0

        lax.fori_loop(0, MARKS // block, body, 0)

    half_of(near_ref, 0)
    half_of(far_ref, MARKS)


def build(groups, block, spread, packed, near, far):
    rows = sum(groups) * OWN
    counts = [len(parts) for parts in packed]
    flat = [part for parts in packed for part in parts]
    return call(
        lambda *refs: build_kernel(counts, groups, block, *refs),
        [pltpu.VMEM((rows, 2 * MARKS), B16), jax.ShapeDtypeStruct((8, 2 * MARKS), F32)],
        [SMEM] + [VMEM] * (len(flat) + 2),
        [spread, *flat, near, far],
        "build",
        scratch=[pltpu.VMEM((rows, WIDTH), F32)],
        flops=4 * rows * 2 * MARKS * 512,
    )


def side_kernel(first, base, *refs):
    slots_ref, tiles, refs = refs[0], refs[1 : 1 + TILES], refs[1 + TILES :]
    half = WIDTH // 2
    if first:
        packed, refs = take(refs, [1] * 7 + [2])
        sums, (out_ref, wt_ref) = refs[:TILES], refs[TILES:]
        tails = [rest_of(parts, OWN + half, PACK) for parts in packed]
        for slot, parts in enumerate(packed):
            lanes = slice(slot * OWN, (slot + 1) * OWN)
            wt_ref[:half, lanes] = rest_of(parts, OWN, OWN + half, slice(0, OWN))
            wt_ref[half:, lanes] = rest_of(parts, OWN, OWN + half, slice(OWN, 2 * OWN))
    else:
        packed_ref, out_ref, wt_ref = refs
        for slot in range(EIGHT):
            wt_ref[:, slot * OWN : (slot + 1) * OWN] = packed_ref[slots_ref[slot], :WIDTH, :]
        tails = [packed_ref[source, WIDTH:, :] for source in range(EIGHT)]
    tail = tails[0].astype(F32)
    for more in tails[1:]:
        tail = tail + more.astype(F32)
    if first:
        tail = join_at(tail, 0)
        second = tail[:, OWN:]
        third = jnp.broadcast_to(jnp.sum(tail[:, :OWN], axis=1, keepdims=True), (1, PIECE))
    else:
        one, two = join_at(tail, 0), join_at(tail, 1)
        second = jnp.concatenate([one[:, :WIDTH], two[:, :WIDTH]], axis=1)
        third = jnp.concatenate([one[:, WIDTH:], two[:, WIDTH:]], axis=1)

    def body(index, _):
        lanes = pl.ds(pl.multiple_of(base + index * BLOCK, BLOCK), BLOCK)
        product, start = None, 0
        for tile in tiles:
            stop = start + tile.shape[0]
            term = dot(wt_ref[:, start:stop], tile[:, lanes], 1, 0)
            product, start = (term if product is None else product + term), stop
        if first:
            column = sums[0][:, lanes]
            for more in sums[1:]:
                column = column + more[:, lanes]
            column = jnp.sum(column, axis=0, keepdims=True)
        else:
            column = jnp.zeros((1, BLOCK), F32)
        for at in range(BLOCK // PIECE):
            lane = slice(at * PIECE, (at + 1) * PIECE)
            out_ref[BLOCK // PIECE * index + at, :WIDTH, :] = product[:, lane]
            out_ref[BLOCK // PIECE * index + at, WIDTH:, :] = stat_rows(column[:, lane], second, third)
        return 0

    lax.fori_loop(0, MARKS // BLOCK, body, 0)


def side_terms(first, base, slots, tiles, more):
    return call(
        lambda *refs: side_kernel(first, base, *refs),
        [jax.ShapeDtypeStruct((EIGHT, WIDTH + 8, PIECE), F32)],
        [SMEM] + [VMEM] * (TILES + len(more)),
        [slots, *tiles, *more],
        "side_terms",
        scratch=[pltpu.VMEM((WIDTH, ROWS), B16)],
        flops=2 * ROWS * MARKS * WIDTH,
    )[0]


def pair_kernel(first, *refs):
    refs = refs[TILES:]
    if first:
        own_ref, other_ref, out_ref, pair_ref = refs
    else:
        own_ref, other_ref, before_ref, out_ref = refs
    stats = own_ref[0, WIDTH:, :] + other_ref[0, WIDTH:, :]
    second, third = stats[1:2], stats[2:3]
    rounded = columns_of([second[:, WIDTH:]])[:, 0:1]
    for piece in range(EIGHT):
        if first:
            column = own_ref[piece, WIDTH : WIDTH + 8, :] + other_ref[piece, WIDTH : WIDTH + 8, :]
            means = column[0:1] / third[:, 0:1]
            pair_ref[piece : piece + 1, :] = means
        else:
            means = before_ref[piece : piece + 1, :]
        side = own_ref[piece, :WIDTH, :] + other_ref[piece, :WIDTH, :]
        out_ref[piece, :WIDTH, :] = (side - rounded * means).astype(B16)
        out_ref[piece, WIDTH:, :] = tails_in_kernel([means, second, third])


def pair(first, tiles, *args):
    shapes = [jax.ShapeDtypeStruct((EIGHT, WIDTH + 16, PIECE), B16)]
    if first:
        shapes.append(jax.ShapeDtypeStruct((EIGHT, PIECE), F32))
    return call(
        lambda *refs: pair_kernel(first, *refs),
        shapes,
        [VMEM] * (TILES + len(args)),
        [*tiles, *args],
        "pair",
        flops=10**9,
    )


def centre_kernel(first, total_rows, *refs):
    refs = refs[TILES:]
    if first:
        terms_ref, out_ref, means_ref = refs
    else:
        terms_ref, before_ref, out_ref = refs
    tails = [terms_ref[group, WIDTH:, :] for group in range(EIGHT)]
    pairs = [join_at(tail, 0) for tail in tails]
    second = [join_at(tail, 1) for tail in tails]
    third = [join_at(tail, 2) for tail in tails]
    total, every = second[0], third[0]
    for group in range(1, EIGHT):
        total, every = total + second[group], every + third[group]
    columns = columns_of([row[:, WIDTH:] for row in second] + [total[:, :WIDTH], every[:, :WIDTH]])
    if first:
        means = third[0][:, 0:1] * pairs[0]
        for group in range(1, EIGHT):
            means = means + third[group][:, 0:1] * pairs[group]
        means = means / every[:, 0:1]
        means_ref[...] = jnp.broadcast_to(means, (8, PIECE))
    else:
        means = before_ref[0:1]
    side = terms_ref[0, :WIDTH, :].astype(F32) + columns[:, 0:1] * pairs[0]
    for group in range(1, EIGHT):
        side = side + (terms_ref[group, :WIDTH, :].astype(F32) + columns[:, group : group + 1] * pairs[group])
    totals = columns[:, EIGHT : EIGHT + 1]
    if first:
        side = side - totals * means
    else:
        squares = columns[:, EIGHT + 1 : EIGHT + 2]
        side = (side * UP - totals * means) / jnp.sqrt(squares / total_rows + 1e-06)
    side = side.astype(B16)
    for group in range(EIGHT):
        out_ref[group, :WIDTH, :] = side
        if first:
            out_ref[group, WIDTH:, :] = tail_in_kernel(means)


def centre(first, total_rows, tiles, *args):
    shapes = [jax.ShapeDtypeStruct((EIGHT, WIDTH + 16 * first, PIECE), B16)]
    if first:
        shapes.append(jax.ShapeDtypeStruct((8, PIECE), F32))
    return call(
        lambda *refs: centre_kernel(first, total_rows, *refs),
        shapes,
        [VMEM] * (TILES + len(args)),
        [*tiles, *args],
        "centre",
        flops=10**9,
    )


def image_kernel(base, slots_ref, *refs):
    tiles, (half_ref, means_ref), refs = refs[:TILES], refs[TILES : TILES + 2], refs[TILES + 2 :]
    if base:
        before_ref, out_ref, side_ref, tail_ref = refs
    else:
        out_ref, side_ref, tail_ref = refs
    for piece in range(EIGHT):
        lanes = slice(piece * PIECE, (piece + 1) * PIECE)
        side_ref[:, lanes] = half_ref[piece, :WIDTH, :]
        tail_ref[:, lanes] = means_ref[piece, WIDTH:, :]
    shift = dot(tail_ref[...], side_ref[...], 1, 1)
    shift = (shift[2:3] + shift[1:2]) + shift[0:1]
    slot = 0
    for tile in tiles:
        count = tile.shape[0] // OWN
        term = dot(tile[:, base : base + MARKS], side_ref[...], 1, 1) - shift
        if base:
            term = term + before_ref[slot * OWN : (slot + count) * OWN, :]
            for at in range(count):
                out_ref[slots_ref[slot + at]] = term[at * OWN : (at + 1) * OWN].astype(B16)
        else:
            out_ref[slot * OWN : (slot + count) * OWN, :] = term
        slot += count


def image_terms(slots, tiles, half, means, before=None):
    if before is None:
        base, more, shape = 0, [], jax.ShapeDtypeStruct((ROWS, WIDTH), F32)
    else:
        base, more, shape = MARKS, [before], jax.ShapeDtypeStruct((EIGHT, OWN, WIDTH), B16)
    return call(
        lambda *refs: image_kernel(base, *refs),
        [shape],
        [SMEM] + [VMEM] * (TILES + 2 + len(more)),
        [slots, *tiles, half, means, *more],
        "image_terms",
        scratch=[pltpu.VMEM((WIDTH, MARKS), B16), pltpu.VMEM((16, MARKS), B16)],
        flops=2 * ROWS * MARKS * WIDTH,
    )[0]


def owner_kernel(last, *refs):
    if not last:
        refs = refs[TILES:]
    terms_ref, weight_ref, out_ref, *more = refs
    image = terms_ref[0].astype(F32)
    for member in range(1, EIGHT):
        image = image + terms_ref[member].astype(F32)
    weight = weight_ref[...]
    image = weight * image
    squares = jnp.sum(image * image, axis=0, keepdims=True)
    if last:
        out_ref[...] = image
        more[0][...] = jnp.broadcast_to(squares, (8, WIDTH))
    else:
        product = weight * image
        totals = jnp.sum(product, axis=0, keepdims=True)
        body = (product * DOWN).astype(B16).astype(F32)
        rounded = jnp.sum(body, axis=0, keepdims=True)
        body = jnp.transpose(body).astype(B16)
        first = jnp.concatenate([totals, squares], axis=1)
        second = jnp.concatenate([rounded, jnp.zeros((1, OWN - WIDTH), F32)], axis=1)
        tail = tails_in_kernel([first, second])
        for member in range(EIGHT):
            out_ref[member, :WIDTH, :] = body
            out_ref[member, WIDTH:, :] = tail


def owner(last, tiles, terms, weight):
    if last:
        shapes = [jax.ShapeDtypeStruct((OWN, WIDTH), F32), jax.ShapeDtypeStruct((8, WIDTH), F32)]
        tiles = []
    else:
        shapes = [jax.ShapeDtypeStruct((EIGHT, WIDTH + 16, OWN), B16)]
    return call(
        lambda *refs: owner_kernel(last, *refs),
        shapes,
        [VMEM] * (len(tiles) + 2),
        [*tiles, terms, weight],
        "owner",
        flops=10**9,
    )


def exchange(payload, axes):
    return lax.all_to_all(payload, axes, 0, 0)


def swap_core(values):
    return lax.ppermute(values, "core", [(0, 1), (1, 0)])


def swap_z(values):
    return lax.ppermute(values, "zl", [(0, 1), (1, 0)])


def from_below(values):
    return lax.ppermute(values, "x", [(at, (at + 1) % 4) for at in range(4)])


def from_above(values):
    return lax.ppermute(values, "x", [(at, (at + 3) % 4) for at in range(4)])


def pack_kernel(rows_hbm, start_hbm, weight_hbm, out_ref, wide_ref, rows_ref, start_ref, weight_ref, sems):
    copies = [
        pltpu.make_async_copy(rows_hbm, rows_ref, sems.at[0]),
        pltpu.make_async_copy(start_hbm, start_ref, sems.at[1]),
        pltpu.make_async_copy(weight_hbm, weight_ref, sems.at[2]),
    ]
    for copy in copies:
        copy.start()
    for copy in copies:
        copy.wait()
    values = rows_ref[...].astype(F32)
    scale = lax.rsqrt(jnp.sum(values * values, axis=1, keepdims=True) + 1e-06)
    out_ref[:OWN, :] = (values * scale).astype(B16)
    weight = weight_ref[...]
    wide = jnp.transpose(jnp.broadcast_to(weight, (WIDTH, OWN)))
    wide_ref[...] = wide
    product = wide * start_ref[...]
    totals = jnp.sum(product, axis=0, keepdims=True)
    vectors = jnp.transpose(product).astype(B16)
    half = WIDTH // 2
    out_ref[OWN : OWN + half, :OWN] = vectors[:half]
    out_ref[OWN : OWN + half, OWN:] = vectors[half:]
    rounded = jnp.sum(product.astype(B16).astype(F32), axis=0, keepdims=True)
    out_ref[OWN + half :, :] = tail_in_kernel(jnp.concatenate([weight, totals, rounded], axis=1))


def pack(rows, start, weight):
    shapes = [jax.ShapeDtypeStruct((PACK, rows.shape[1]), B16), jax.ShapeDtypeStruct((OWN, WIDTH), F32)]
    scratch = [
        pltpu.VMEM(rows.shape, B16),
        pltpu.VMEM(start.shape, F32),
        pltpu.VMEM(weight.shape, F32),
        pltpu.SemaphoreType.DMA((3,)),
    ]
    specs = [pl.BlockSpec(memory_space=pl.ANY)] * 3
    return call(pack_kernel, shapes, specs, [rows, start, weight], "pack", scratch=scratch, mib=56)


def slot_owners():
    x, z = lax.axis_index("x"), lax.axis_index("zl")
    moves = [(0, 0), (3, 0), (1, 0), (0, 1), (2, 0), (1, 1), (3, 1), (2, 1)]
    return jnp.stack([(x + dx) % 4 * 2 + (z + dz) % 2 for dx, dz in moves]).astype(jnp.int32)


def local(embeddings, landmarks, start_vectors, row_weight, spread):
    total_rows = embeddings.shape[0] * lax.axis_size(AXES)
    slots = slot_owners()
    packed, weight = pack(embeddings, start_vectors, row_weight[None, :])
    below, above, across = from_below(packed), from_above(packed), swap_z(packed)
    near = unit(landmarks)
    far = unit(swap_core(landmarks))
    zero, sums_zero = build((1,), 2048, spread, [[packed]], near, far)
    below, above, across, sums_zero = lax.optimization_barrier((below, above, across, sums_zero))
    opposite, across_above, across_below = from_below(below), from_above(across), swap_z(below)
    one, sums_one = build((3,), 2048, spread, [[below], [above], [across]], near, far)
    opposite, across_above, across_below, sums_one = lax.optimization_barrier(
        (opposite, across_above, across_below, sums_one)
    )
    last = [swap_z(opposite[:SPLIT]), from_above(across_above[SPLIT:])]
    two, sums_two = build((3,), 2048, spread, [[opposite], [across_above], [across_below]], near, far)
    *last, sums_two = lax.optimization_barrier((*last, sums_two))
    three, sums_three = build((1,), 2048, spread, [last], near, far)
    packs = [packed, below, above, across, opposite, across_above, across_below, *last]
    tiles = (zero, one, two, three)
    first = [*packs, sums_zero, sums_one, sums_two, sums_three]
    for step in range(ITERS):
        more = first if step == 0 else [vectors]
        other = swap_core(side_terms(step == 0, MARKS, slots, tiles, more))
        own = side_terms(step == 0, 0, slots, tiles, more)
        if step == 0:
            payload, pair_means = pair(True, tiles, own, other)
            sides, means = centre(True, total_rows, tiles, exchange(payload, MARK_AXES))
        else:
            (payload,) = pair(False, tiles, own, other, pair_means)
            (sides,) = centre(False, total_rows, tiles, exchange(payload, MARK_AXES), means)
        sides = exchange(sides, MARK_AXES)
        across_core = swap_core(sides)
        if step == 0:
            tails = (sides, across_core)
        parts = image_terms(slots, tiles, sides, tails[0])
        parts = image_terms(slots, tiles, across_core, tails[1], parts)
        parts = exchange(parts, ROW_AXES)
        if step + 1 < ITERS:
            (vectors,) = owner(False, tiles, parts, weight)
            vectors = exchange(vectors, ROW_AXES)
    image, squares = owner(True, tiles, parts, weight)
    count = lax.axis_size(AXES)
    every = exchange(jnp.broadcast_to(squares[:1][None], (count, 1, WIDTH)), AXES)
    scale = jnp.sqrt(jnp.sum(every[:, 0], axis=0) / total_rows + 1e-06)
    return image / scale[None, :]


def solution(mesh):
    fine = Mesh(mesh.devices.reshape(4, 2, 4, 2, 2), AXES)
    rows = P(AXES, None)
    in_specs = (rows, P(("x", "zl", "core"), None), rows, P(AXES), P())
    return jax.shard_map(local, mesh=fine, in_specs=in_specs, out_specs=rows, check_vma=False)
```

```python
import jax
import jax.numpy as jnp
from jax import lax
from jax.experimental import pallas as pl
from jax.experimental.pallas import tpu as pltpu
from jax.sharding import Mesh
from jax.sharding import PartitionSpec as P

ITERS = 2
AXES = ("y", "zh", "x", "zl", "core")
ROW_AXES = ("x", "zl")
MARK_AXES = ("y", "zh")
F32, B16 = jnp.float32, jnp.bfloat16
DOWN = 2.0**-20
UP = 2.0**20
LOG2E = 1.4426950408889634
VMEM = pl.BlockSpec(memory_space=pltpu.VMEM)
SMEM = pl.BlockSpec(memory_space=pltpu.SMEM)
OWN = 256
PIECE = 256
WIDTH = 128
MARKS = 2048
EIGHT = 8
ROWS = EIGHT * OWN
PACK = OWN + WIDTH // 2 + 16
BLOCK = 8 * PIECE
SPLIT = 160
TILES = 4


def params(mib):
    return pltpu.CompilerParams(vmem_limit_bytes=mib * 2**20)


def dot(left, right, left_dim, right_dim):
    dims = (((left_dim,), (right_dim,)), ((), ()))
    return lax.dot_general(left, right, dims, preferred_element_type=F32)


def parts_in_kernel(values):
    high = values.astype(B16)
    rest = values - high.astype(F32)
    mid = rest.astype(B16)
    low = (rest - mid.astype(F32)).astype(B16)
    return high.astype(F32), mid.astype(F32), low.astype(F32)


def tail_in_kernel(row):
    at = lax.broadcasted_iota(jnp.int32, (16, row.shape[1]), 0)
    high, mid, low = parts_in_kernel(row)
    zero = jnp.zeros((16, row.shape[1]), F32)
    block = jnp.where(at == 0, high, jnp.where(at == 1, mid, jnp.where(at == 2, low, zero)))
    return block.astype(B16)


def join_tail(block):
    block = block.astype(F32)
    return (block[2:3] + block[1:2]) + block[0:1]


def stat_rows(first, second, third):
    at = lax.broadcasted_iota(jnp.int32, (8, PIECE), 0)
    zero = jnp.zeros((8, PIECE), F32)
    return jnp.where(at == 0, first, jnp.where(at == 1, second, jnp.where(at == 2, third, zero)))


def tails_in_kernel(rows):
    at = lax.broadcasted_iota(jnp.int32, (16, rows[0].shape[1]), 0)
    block = jnp.zeros(at.shape, F32)
    for index, row in enumerate(rows):
        for part, value in enumerate(parts_in_kernel(row)):
            block = jnp.where(at == 3 * index + part, value, block)
    return block.astype(B16)


def join_at(block, index):
    block = block[3 * index : 3 * index + 3].astype(F32)
    return (block[2:3] + block[1:2]) + block[0:1]


def columns_of(rows):
    at = lax.broadcasted_iota(jnp.int32, (WIDTH, WIDTH), 0)
    block = jnp.zeros((WIDTH, WIDTH), F32)
    for index, row in enumerate(rows):
        block = jnp.where(at == index, row, block)
    return jnp.transpose(block)


def call(kernel, shapes, specs, args, name, scratch=(), flops=0, mib=24):
    cost = pl.CostEstimate(flops=flops, bytes_accessed=0, transcendentals=0)
    return pl.pallas_call(
        kernel,
        out_shape=shapes,
        in_specs=specs,
        out_specs=[VMEM] * len(shapes),
        scratch_shapes=list(scratch),
        compiler_params=params(mib),
        cost_estimate=cost,
        name=name,
    )(*args)


def rows_of(refs):
    if len(refs) == 1:
        return refs[0][:OWN, :]
    return jnp.concatenate([refs[0][...], refs[1][: OWN - SPLIT, :]], axis=0)


def rest_of(refs, start, stop, lanes=slice(None)):
    skip = 0 if len(refs) == 1 else SPLIT
    return refs[-1][start - skip : stop - skip, lanes]


def take(refs, counts):
    taken = []
    for count in counts:
        taken.append(refs[:count])
        refs = refs[count:]
    return taken, refs


def unit_kernel(in_ref, out_ref):
    block = 2 * OWN

    def body(index, _):
        rows = pl.ds(pl.multiple_of(index * block, block), block)
        values = in_ref[rows, :].astype(F32)
        scale = lax.rsqrt(jnp.sum(values * values, axis=1, keepdims=True) + 1e-06)
        out_ref[rows, :] = (values * scale).astype(B16)
        return 0

    lax.fori_loop(0, MARKS // block, body, 0)


def unit(values):
    shape = jax.ShapeDtypeStruct(values.shape, B16)
    return call(unit_kernel, [shape], [VMEM], [values], "unit", flops=2 * 10**9, mib=12)[0]


def build_kernel(counts, groups, block, *refs):
    spread_ref = refs[0]
    packed, refs = take(refs[1:], counts)
    near_ref, far_ref, tile_ref, sums_ref, wide_ref = refs
    gamma = spread_ref[0] * LOG2E
    for source, parts in enumerate(packed):
        weight = join_tail(rest_of(parts, PACK - 16, PACK))[:, :OWN]
        column = jnp.transpose(jnp.broadcast_to(weight, (WIDTH, OWN)))
        wide_ref[source * OWN : (source + 1) * OWN, :] = column

    def half_of(marks_ref, base):
        def body(index, _):
            start = pl.multiple_of(index * block, block)
            marks = marks_ref[pl.ds(start, block), :]
            lanes = pl.ds(pl.multiple_of(base + start, block), block)
            sums = [jnp.zeros((8, WIDTH), F32) for _ in range(block // WIDTH)]
            first = 0
            for size in groups:
                rows = jnp.concatenate([rows_of(parts) for parts in packed[first : first + size]], axis=0)
                values = jnp.exp2(dot(rows, marks, 1, 1) * gamma)
                at = slice(first * OWN, (first + size) * OWN)
                tile_ref[at, lanes] = values.astype(B16)
                wide = wide_ref[at, :]
                for lane in range(block // WIDTH):
                    term = values[:, lane * WIDTH : (lane + 1) * WIDTH] * wide
                    sums[lane] = sums[lane] + jnp.sum(term.reshape(-1, 8, WIDTH), axis=0)
                first += size
            sums_ref[:, lanes] = jnp.concatenate(sums, axis=1)
            return 0

        lax.fori_loop(0, MARKS // block, body, 0)

    half_of(near_ref, 0)
    half_of(far_ref, MARKS)


def build(groups, block, spread, packed, near, far, after=()):
    rows = sum(groups) * OWN
    counts = [len(parts) for parts in packed]
    flat = [part for parts in packed for part in parts]
    return call(
        lambda *refs: build_kernel(counts, groups, block, *refs[len(after) :]),
        [pltpu.VMEM((rows, 2 * MARKS), B16), jax.ShapeDtypeStruct((8, 2 * MARKS), F32)],
        [VMEM] * len(after) + [SMEM] + [VMEM] * (len(flat) + 2),
        [*after, spread, *flat, near, far],
        "build",
        mib=18,
        scratch=[pltpu.VMEM((rows, WIDTH), F32)],
        flops=4 * rows * 2 * MARKS * 512,
    )


def side_kernel(first, base, *refs):
    slots_ref, tiles, refs = refs[0], refs[1 : 1 + TILES], refs[1 + TILES :]
    half = WIDTH // 2
    if first:
        packed, refs = take(refs, [1] * 7 + [2])
        sums, (out_ref, wt_ref) = refs[:TILES], refs[TILES:]
        tails = [rest_of(parts, OWN + half, PACK) for parts in packed]
        for slot, parts in enumerate(packed):
            lanes = slice(slot * OWN, (slot + 1) * OWN)
            wt_ref[:half, lanes] = rest_of(parts, OWN, OWN + half, slice(0, OWN))
            wt_ref[half:, lanes] = rest_of(parts, OWN, OWN + half, slice(OWN, 2 * OWN))
    else:
        packed_ref, out_ref, wt_ref = refs
        for slot in range(EIGHT):
            wt_ref[:, slot * OWN : (slot + 1) * OWN] = packed_ref[slots_ref[slot], :WIDTH, :]
        tails = [packed_ref[source, WIDTH:, :] for source in range(EIGHT)]
    tail = tails[0].astype(F32)
    for more in tails[1:]:
        tail = tail + more.astype(F32)
    if first:
        tail = join_at(tail, 0)
        second = tail[:, OWN:]
        third = jnp.broadcast_to(jnp.sum(tail[:, :OWN], axis=1, keepdims=True), (1, PIECE))
    else:
        one, two = join_at(tail, 0), join_at(tail, 1)
        second = jnp.concatenate([one[:, :WIDTH], two[:, :WIDTH]], axis=1)
        third = jnp.concatenate([one[:, WIDTH:], two[:, WIDTH:]], axis=1)

    def body(index, _):
        lanes = pl.ds(pl.multiple_of(base + index * BLOCK, BLOCK), BLOCK)
        product, start = None, 0
        for tile in tiles:
            stop = start + tile.shape[0]
            term = dot(wt_ref[:, start:stop], tile[:, lanes], 1, 0)
            product, start = (term if product is None else product + term), stop
        if first:
            column = sums[0][:, lanes]
            for more in sums[1:]:
                column = column + more[:, lanes]
            column = jnp.sum(column, axis=0, keepdims=True)
        else:
            column = jnp.zeros((1, BLOCK), F32)
        for at in range(BLOCK // PIECE):
            lane = slice(at * PIECE, (at + 1) * PIECE)
            out_ref[BLOCK // PIECE * index + at, :WIDTH, :] = product[:, lane]
            out_ref[BLOCK // PIECE * index + at, WIDTH:, :] = stat_rows(column[:, lane], second, third)
        return 0

    lax.fori_loop(0, MARKS // BLOCK, body, 0)


def side_terms(first, base, slots, tiles, more):
    return call(
        lambda *refs: side_kernel(first, base, *refs),
        [jax.ShapeDtypeStruct((EIGHT, WIDTH + 8, PIECE), F32)],
        [SMEM] + [VMEM] * (TILES + len(more)),
        [slots, *tiles, *more],
        "side_terms",
        scratch=[pltpu.VMEM((WIDTH, ROWS), B16)],
        flops=2 * ROWS * MARKS * WIDTH,
        mib=12,
    )[0]


def pair_kernel(first, *refs):
    if first:
        own_ref, other_ref, out_ref, pair_ref = refs
    else:
        own_ref, other_ref, before_ref, out_ref = refs
    stats = own_ref[0, WIDTH:, :] + other_ref[0, WIDTH:, :]
    second, third = stats[1:2], stats[2:3]
    rounded = columns_of([second[:, WIDTH:]])[:, 0:1]
    for piece in range(EIGHT):
        if first:
            column = own_ref[piece, WIDTH : WIDTH + 8, :] + other_ref[piece, WIDTH : WIDTH + 8, :]
            means = column[0:1] / third[:, 0:1]
            pair_ref[piece : piece + 1, :] = means
        else:
            means = before_ref[piece : piece + 1, :]
        side = own_ref[piece, :WIDTH, :] + other_ref[piece, :WIDTH, :]
        out_ref[piece, :WIDTH, :] = (side - rounded * means).astype(B16)
        out_ref[piece, WIDTH:, :] = tails_in_kernel([means, second, third])


def pair(first, keep, *args):
    shapes = [jax.ShapeDtypeStruct((EIGHT, WIDTH + 16, PIECE), B16)]
    if first:
        shapes.append(jax.ShapeDtypeStruct((EIGHT, PIECE), F32))
    return call(
        lambda *refs: pair_kernel(first, *refs[len(keep) :]),
        shapes,
        [VMEM] * (len(keep) + len(args)),
        [*keep, *args],
        "pair",
        flops=10**9,
        mib=12,
    )


def centre_kernel(first, total_rows, *refs):
    if first:
        terms_ref, out_ref, means_ref = refs
    else:
        terms_ref, before_ref, out_ref = refs
    tails = [terms_ref[group, WIDTH:, :] for group in range(EIGHT)]
    pairs = [join_at(tail, 0) for tail in tails]
    second = [join_at(tail, 1) for tail in tails]
    third = [join_at(tail, 2) for tail in tails]
    total, every = second[0], third[0]
    for group in range(1, EIGHT):
        total, every = total + second[group], every + third[group]
    columns = columns_of([row[:, WIDTH:] for row in second] + [total[:, :WIDTH], every[:, :WIDTH]])
    if first:
        means = third[0][:, 0:1] * pairs[0]
        for group in range(1, EIGHT):
            means = means + third[group][:, 0:1] * pairs[group]
        means = means / every[:, 0:1]
        means_ref[...] = jnp.broadcast_to(means, (8, PIECE))
    else:
        means = before_ref[0:1]
    side = terms_ref[0, :WIDTH, :].astype(F32) + columns[:, 0:1] * pairs[0]
    for group in range(1, EIGHT):
        side = side + (terms_ref[group, :WIDTH, :].astype(F32) + columns[:, group : group + 1] * pairs[group])
    totals = columns[:, EIGHT : EIGHT + 1]
    if first:
        side = side - totals * means
    else:
        squares = columns[:, EIGHT + 1 : EIGHT + 2]
        side = (side * UP - totals * means) / jnp.sqrt(squares / total_rows + 1e-06)
    side = side.astype(B16)
    for group in range(EIGHT):
        out_ref[group, :WIDTH, :] = side
        if first:
            out_ref[group, WIDTH:, :] = tail_in_kernel(means)


def centre(first, total_rows, keep, *args):
    shapes = [jax.ShapeDtypeStruct((EIGHT, WIDTH + 16 * first, PIECE), B16)]
    if first:
        shapes.append(jax.ShapeDtypeStruct((8, PIECE), F32))
    return call(
        lambda *refs: centre_kernel(first, total_rows, *refs[len(keep) :]),
        shapes,
        [VMEM] * (len(keep) + len(args)),
        [*keep, *args],
        "centre",
        flops=10**9,
        mib=12,
    )


def turn_kernel(base, _, *refs):
    *tiles, out_ref, done_ref = refs
    start = 0
    for tile in tiles:
        for row in range(0, tile.shape[0], OWN):
            out_ref[:, start : start + OWN] = jnp.transpose(tile[row : row + OWN, base : base + MARKS])
            start += OWN
    done_ref[...] = jnp.zeros(done_ref.shape, F32)


def turn(base, slots, tiles):
    rows = sum(tile.shape[0] for tile in tiles)
    return call(
        lambda *refs: turn_kernel(base, *refs),
        [pltpu.VMEM((MARKS, rows), B16), jax.ShapeDtypeStruct((8, WIDTH), F32)],
        [SMEM] + [VMEM] * len(tiles),
        [slots, *tiles],
        "turn",
        flops=10**9,
        mib=12,
    )


def image_kernel(last, slots_ref, early_ref, late_ref, half_ref, means_ref, *refs):
    if last:
        before_ref, out_ref, side_ref, tail_ref = refs
    else:
        out_ref, side_ref, tail_ref = refs
    for piece in range(EIGHT):
        lanes = slice(piece * PIECE, (piece + 1) * PIECE)
        side_ref[:, lanes] = half_ref[piece, :WIDTH, :]
        tail_ref[:, lanes] = means_ref[piece, WIDTH:, :]
    shift = dot(side_ref[...], tail_ref[...], 1, 1)
    shift = (shift[:, 2:3] + shift[:, 1:2]) + shift[:, 0:1]
    for part, ref in enumerate((early_ref, late_ref)):
        lanes = slice(part * ROWS // 2, (part + 1) * ROWS // 2)
        term = dot(side_ref[...], ref[...], 1, 0) - shift
        if last:
            term = term + before_ref[:, lanes]
            for at in range(EIGHT // 2):
                slot = part * EIGHT // 2 + at
                out_ref[slots_ref[slot]] = term[:, at * OWN : (at + 1) * OWN].astype(B16)
        else:
            out_ref[:, lanes] = term


def image_terms(slots, early, late, half, means, before=None):
    if before is None:
        more, shape = [], jax.ShapeDtypeStruct((WIDTH, ROWS), F32)
    else:
        more, shape = [before], jax.ShapeDtypeStruct((EIGHT, WIDTH, OWN), B16)
    return call(
        lambda *refs: image_kernel(before is not None, *refs),
        [shape],
        [SMEM] + [VMEM] * (4 + len(more)),
        [slots, early, late, half, means, *more],
        "image_terms",
        scratch=[pltpu.VMEM((WIDTH, MARKS), B16), pltpu.VMEM((16, MARKS), B16)],
        flops=2 * ROWS * MARKS * WIDTH,
        mib=12,
    )[0]


def rows_from(columns):
    at = lax.broadcasted_iota(jnp.int32, (WIDTH, WIDTH), 1)
    block = jnp.zeros((WIDTH, WIDTH), F32)
    for index, column in enumerate(columns):
        block = jnp.where(at == index, column, block)
    block = jnp.transpose(block)
    return [block[index : index + 1] for index in range(len(columns))]


def owner_kernel(last, terms_ref, weight_ref, out_ref, *more):
    image = terms_ref[0].astype(F32)
    for member in range(1, EIGHT):
        image = image + terms_ref[member].astype(F32)
    weight = weight_ref[0:1, :]
    image = weight * image
    squares = jnp.sum(image * image, axis=1, keepdims=True)
    if last:
        out_ref[...] = jnp.transpose(image)
        more[0][...] = jnp.broadcast_to(rows_from([squares])[0], (8, WIDTH))
    else:
        product = weight * image
        totals = jnp.sum(product, axis=1, keepdims=True)
        body = (product * DOWN).astype(B16)
        rounded = jnp.sum(body.astype(F32), axis=1, keepdims=True)
        totals, squares, rounded = rows_from([totals, squares, rounded])
        first = jnp.concatenate([totals, squares], axis=1)
        second = jnp.concatenate([rounded, jnp.zeros((1, OWN - WIDTH), F32)], axis=1)
        tail = tails_in_kernel([first, second])
        for member in range(EIGHT):
            out_ref[member, :WIDTH, :] = body
            out_ref[member, WIDTH:, :] = tail


def owner(last, keep, terms, weight):
    if last:
        shapes = [jax.ShapeDtypeStruct((OWN, WIDTH), F32), jax.ShapeDtypeStruct((8, WIDTH), F32)]
    else:
        shapes = [jax.ShapeDtypeStruct((EIGHT, WIDTH + 16, OWN), B16)]
    return call(
        lambda *refs: owner_kernel(last, *refs[len(keep) :]),
        shapes,
        [VMEM] * (len(keep) + 2),
        [*keep, terms, weight],
        "owner",
        flops=10**9,
        mib=12,
    )


def exchange(payload, axes):
    return lax.all_to_all(payload, axes, 0, 0)


def swap_core(values):
    return lax.ppermute(values, "core", [(0, 1), (1, 0)])


def swap_z(values):
    return lax.ppermute(values, "zl", [(0, 1), (1, 0)])


def from_below(values):
    return lax.ppermute(values, "x", [(at, (at + 1) % 4) for at in range(4)])


def from_above(values):
    return lax.ppermute(values, "x", [(at, (at + 3) % 4) for at in range(4)])


def pack_kernel(rows_hbm, start_hbm, weight_hbm, out_ref, line_ref, rows_ref, start_ref, weight_ref, sems):
    copies = [
        pltpu.make_async_copy(rows_hbm, rows_ref, sems.at[0]),
        pltpu.make_async_copy(start_hbm, start_ref, sems.at[1]),
        pltpu.make_async_copy(weight_hbm, weight_ref, sems.at[2]),
    ]
    for copy in copies:
        copy.start()
    for copy in copies:
        copy.wait()
    values = rows_ref[...].astype(F32)
    scale = lax.rsqrt(jnp.sum(values * values, axis=1, keepdims=True) + 1e-06)
    out_ref[:OWN, :] = (values * scale).astype(B16)
    weight = weight_ref[...]
    wide = jnp.transpose(jnp.broadcast_to(weight, (WIDTH, OWN)))
    line_ref[...] = jnp.broadcast_to(weight, (8, OWN))
    product = wide * start_ref[...]
    totals = jnp.sum(product, axis=0, keepdims=True)
    vectors = jnp.transpose(product).astype(B16)
    half = WIDTH // 2
    out_ref[OWN : OWN + half, :OWN] = vectors[:half]
    out_ref[OWN : OWN + half, OWN:] = vectors[half:]
    rounded = jnp.sum(product.astype(B16).astype(F32), axis=0, keepdims=True)
    out_ref[OWN + half :, :] = tail_in_kernel(jnp.concatenate([weight, totals, rounded], axis=1))


def pack(rows, start, weight):
    shapes = [jax.ShapeDtypeStruct((PACK, rows.shape[1]), B16), jax.ShapeDtypeStruct((8, OWN), F32)]
    scratch = [
        pltpu.VMEM(rows.shape, B16),
        pltpu.VMEM(start.shape, F32),
        pltpu.VMEM(weight.shape, F32),
        pltpu.SemaphoreType.DMA((3,)),
    ]
    specs = [pl.BlockSpec(memory_space=pl.ANY)] * 3
    return call(pack_kernel, shapes, specs, [rows, start, weight], "pack", scratch=scratch, mib=56)


def slot_owners():
    x, z = lax.axis_index("x"), lax.axis_index("zl")
    moves = [(0, 0), (3, 0), (1, 0), (0, 1), (2, 0), (1, 1), (3, 1), (2, 1)]
    return jnp.stack([(x + dx) % 4 * 2 + (z + dz) % 2 for dx, dz in moves]).astype(jnp.int32)


def local(embeddings, landmarks, start_vectors, row_weight, spread):
    total_rows = embeddings.shape[0] * lax.axis_size(AXES)
    slots = slot_owners()
    packed, weight = pack(embeddings, start_vectors, row_weight[None, :])
    below, above, across = from_below(packed), from_above(packed), swap_z(packed)
    near = unit(landmarks)
    far = unit(swap_core(landmarks))
    zero, sums_zero = build((1,), 2048, spread, [[packed]], near, far)
    below, above, across, sums_zero = lax.optimization_barrier((below, above, across, sums_zero))
    opposite, across_above, across_below = from_below(below), from_above(across), swap_z(below)
    one, sums_one = build((3,), 2048, spread, [[below], [above], [across]], near, far)
    early_own, done_own = turn(0, slots, [zero, one])
    early_other, done_other = turn(MARKS, slots, [zero, one])
    opposite, across_above, across_below, sums_one, done_own, done_other = lax.optimization_barrier(
        (opposite, across_above, across_below, sums_one, done_own, done_other)
    )
    last = [swap_z(opposite[:SPLIT]), from_above(across_above[SPLIT:])]
    two, sums_two = build(
        (3,), 2048, spread, [[opposite], [across_above], [across_below]], near, far, [done_own, done_other]
    )
    *last, sums_two = lax.optimization_barrier((*last, sums_two))
    three, sums_three = build((1,), 2048, spread, [last], near, far)
    packs = [packed, below, above, across, opposite, across_above, across_below, *last]
    tiles = (zero, one, two, three)
    first = [*packs, sums_zero, sums_one, sums_two, sums_three]
    for step in range(ITERS):
        more = first if step == 0 else [vectors]
        other = swap_core(side_terms(step == 0, MARKS, slots, tiles, more))
        own = side_terms(step == 0, 0, slots, tiles, more)
        if step == 0:
            late_own, done = turn(0, slots, [two, three])
            own, done = lax.optimization_barrier((own, done))
            keep = [*tiles, early_own, late_own, early_other]
            payload, pair_means = pair(True, keep, own, other)
            sides, means = centre(True, total_rows, keep, exchange(payload, MARK_AXES))
        else:
            keep = []
            (payload,) = pair(False, keep, own, other, pair_means)
            (sides,) = centre(False, total_rows, keep, exchange(payload, MARK_AXES), means)
        sides = exchange(sides, MARK_AXES)
        across_core = swap_core(sides)
        if step == 0:
            tails = (sides, across_core)
        parts = image_terms(slots, early_own, late_own, sides, tails[0])
        if step == 0:
            parts, after = lax.optimization_barrier((parts, slots))
            late_other, _ = turn(MARKS, after, [two, three])
            keep = [*keep, late_other]
        parts = image_terms(slots, early_other, late_other, across_core, tails[1], parts)
        parts = exchange(parts, ROW_AXES)
        if step + 1 < ITERS:
            (vectors,) = owner(False, keep, parts, weight)
            vectors = exchange(vectors, ROW_AXES)
    image, squares = owner(True, [], parts, weight)
    count = lax.axis_size(AXES)
    every = exchange(jnp.broadcast_to(squares[:1][None], (count, 1, WIDTH)), AXES)
    scale = jnp.sqrt(jnp.sum(every[:, 0], axis=0) / total_rows + 1e-06)
    return image / scale[None, :]


def solution(mesh):
    fine = Mesh(mesh.devices.reshape(4, 2, 4, 2, 2), AXES)
    rows = P(AXES, None)
    in_specs = (rows, P(("x", "zl", "core"), None), rows, P(AXES), P())
    return jax.shard_map(local, mesh=fine, in_specs=in_specs, out_specs=rows, check_vma=False)
```

```python
import jax
import jax.numpy as jnp
from jax import lax
from jax.experimental import pallas as pl
from jax.experimental.pallas import tpu as pltpu
from jax.sharding import Mesh
from jax.sharding import PartitionSpec as P

ITERS = 2
AXES = ("y", "zh", "x", "zl", "core")
ROW_AXES = ("x", "zl")
MARK_AXES = ("y", "zh")
F32, B16 = jnp.float32, jnp.bfloat16
DOWN = 2.0**-20
UP = 2.0**20
LOG2E = 1.4426950408889634
VMEM = pl.BlockSpec(memory_space=pltpu.VMEM)
SMEM = pl.BlockSpec(memory_space=pltpu.SMEM)
OWN = 256
PIECE = 256
WIDTH = 128
MARKS = 2048
EIGHT = 8
ROWS = EIGHT * OWN
PACK = OWN + WIDTH // 2 + 16
BLOCK = 8 * PIECE
SPLIT = 160
TILES = 4


def params(mib):
    return pltpu.CompilerParams(vmem_limit_bytes=mib * 2**20)


def dot(left, right, left_dim, right_dim):
    dims = (((left_dim,), (right_dim,)), ((), ()))
    return lax.dot_general(left, right, dims, preferred_element_type=F32)


def parts_in_kernel(values):
    high = values.astype(B16)
    rest = values - high.astype(F32)
    mid = rest.astype(B16)
    low = (rest - mid.astype(F32)).astype(B16)
    return high.astype(F32), mid.astype(F32), low.astype(F32)


def tail_in_kernel(row):
    at = lax.broadcasted_iota(jnp.int32, (16, row.shape[1]), 0)
    high, mid, low = parts_in_kernel(row)
    zero = jnp.zeros((16, row.shape[1]), F32)
    block = jnp.where(at == 0, high, jnp.where(at == 1, mid, jnp.where(at == 2, low, zero)))
    return block.astype(B16)


def join_tail(block):
    block = block.astype(F32)
    return (block[2:3] + block[1:2]) + block[0:1]


def stat_rows(first, second, third):
    at = lax.broadcasted_iota(jnp.int32, (8, PIECE), 0)
    zero = jnp.zeros((8, PIECE), F32)
    return jnp.where(at == 0, first, jnp.where(at == 1, second, jnp.where(at == 2, third, zero)))


def tails_in_kernel(rows):
    at = lax.broadcasted_iota(jnp.int32, (16, rows[0].shape[1]), 0)
    block = jnp.zeros(at.shape, F32)
    for index, row in enumerate(rows):
        for part, value in enumerate(parts_in_kernel(row)):
            block = jnp.where(at == 3 * index + part, value, block)
    return block.astype(B16)


def join_at(block, index):
    block = block[3 * index : 3 * index + 3].astype(F32)
    return (block[2:3] + block[1:2]) + block[0:1]


def columns_of(rows):
    at = lax.broadcasted_iota(jnp.int32, (WIDTH, WIDTH), 0)
    block = jnp.zeros((WIDTH, WIDTH), F32)
    for index, row in enumerate(rows):
        block = jnp.where(at == index, row, block)
    return jnp.transpose(block)


def call(kernel, shapes, specs, args, name, scratch=(), flops=0, mib=24):
    cost = pl.CostEstimate(flops=flops, bytes_accessed=0, transcendentals=0)
    return pl.pallas_call(
        kernel,
        out_shape=shapes,
        in_specs=specs,
        out_specs=[VMEM] * len(shapes),
        scratch_shapes=list(scratch),
        compiler_params=params(mib),
        cost_estimate=cost,
        name=name,
    )(*args)


def rows_of(refs):
    if len(refs) == 1:
        return refs[0][:OWN, :]
    return jnp.concatenate([refs[0][...], refs[1][: OWN - SPLIT, :]], axis=0)


def rest_of(refs, start, stop, lanes=slice(None)):
    skip = 0 if len(refs) == 1 else SPLIT
    return refs[-1][start - skip : stop - skip, lanes]


def take(refs, counts):
    taken = []
    for count in counts:
        taken.append(refs[:count])
        refs = refs[count:]
    return taken, refs


def unit_kernel(in_ref, out_ref):
    block = 2 * OWN

    def body(index, _):
        rows = pl.ds(pl.multiple_of(index * block, block), block)
        values = in_ref[rows, :].astype(F32)
        scale = lax.rsqrt(jnp.sum(values * values, axis=1, keepdims=True) + 1e-06)
        out_ref[rows, :] = (values * scale).astype(B16)
        return 0

    lax.fori_loop(0, MARKS // block, body, 0)


def unit(values):
    shape = jax.ShapeDtypeStruct(values.shape, B16)
    return call(unit_kernel, [shape], [VMEM], [values], "unit", flops=2 * 10**9, mib=12)[0]


def build_kernel(counts, groups, block, *refs):
    spread_ref = refs[0]
    packed, refs = take(refs[1:], counts)
    near_ref, far_ref, tile_ref, sums_ref, wide_ref = refs
    gamma = spread_ref[0] * LOG2E
    for source, parts in enumerate(packed):
        weight = join_tail(rest_of(parts, PACK - 16, PACK))[:, :OWN]
        column = jnp.transpose(jnp.broadcast_to(weight, (WIDTH, OWN)))
        wide_ref[source * OWN : (source + 1) * OWN, :] = column

    def half_of(marks_ref, base):
        def body(index, _):
            start = pl.multiple_of(index * block, block)
            marks = marks_ref[pl.ds(start, block), :]
            lanes = pl.ds(pl.multiple_of(base + start, block), block)
            sums = [jnp.zeros((8, WIDTH), F32) for _ in range(block // WIDTH)]
            first = 0
            for size in groups:
                rows = jnp.concatenate([rows_of(parts) for parts in packed[first : first + size]], axis=0)
                values = jnp.exp2(dot(rows, marks, 1, 1) * gamma)
                at = slice(first * OWN, (first + size) * OWN)
                tile_ref[at, lanes] = values.astype(B16)
                wide = wide_ref[at, :]
                for lane in range(block // WIDTH):
                    term = values[:, lane * WIDTH : (lane + 1) * WIDTH] * wide
                    sums[lane] = sums[lane] + jnp.sum(term.reshape(-1, 8, WIDTH), axis=0)
                first += size
            sums_ref[:, lanes] = jnp.concatenate(sums, axis=1)
            return 0

        lax.fori_loop(0, MARKS // block, body, 0)

    half_of(near_ref, 0)
    half_of(far_ref, MARKS)


def build(groups, block, spread, packed, near, far, after=()):
    rows = sum(groups) * OWN
    counts = [len(parts) for parts in packed]
    flat = [part for parts in packed for part in parts]
    return call(
        lambda *refs: build_kernel(counts, groups, block, *refs[len(after) :]),
        [pltpu.VMEM((rows, 2 * MARKS), B16), jax.ShapeDtypeStruct((8, 2 * MARKS), F32)],
        [VMEM] * len(after) + [SMEM] + [VMEM] * (len(flat) + 2),
        [*after, spread, *flat, near, far],
        "build",
        mib=18,
        scratch=[pltpu.VMEM((rows, WIDTH), F32)],
        flops=4 * rows * 2 * MARKS * 512,
    )


def side_kernel(first, base, *refs):
    slots_ref, tiles, refs = refs[0], refs[1 : 1 + TILES], refs[1 + TILES :]
    half = WIDTH // 2
    if first:
        packed, refs = take(refs, [1] * 7 + [2])
        sums, (out_ref, wt_ref) = refs[:TILES], refs[TILES:]
        tails = [rest_of(parts, OWN + half, PACK) for parts in packed]
        for slot, parts in enumerate(packed):
            lanes = slice(slot * OWN, (slot + 1) * OWN)
            wt_ref[:half, lanes] = rest_of(parts, OWN, OWN + half, slice(0, OWN))
            wt_ref[half:, lanes] = rest_of(parts, OWN, OWN + half, slice(OWN, 2 * OWN))
    else:
        packed_ref, out_ref, wt_ref = refs
        for slot in range(EIGHT):
            wt_ref[:, slot * OWN : (slot + 1) * OWN] = packed_ref[slots_ref[slot], :WIDTH, :]
        tails = [packed_ref[source, WIDTH:, :] for source in range(EIGHT)]
    tail = tails[0].astype(F32)
    for more in tails[1:]:
        tail = tail + more.astype(F32)
    if first:
        tail = join_at(tail, 0)
        second = tail[:, OWN:]
        third = jnp.broadcast_to(jnp.sum(tail[:, :OWN], axis=1, keepdims=True), (1, PIECE))
    else:
        one, two = join_at(tail, 0), join_at(tail, 1)
        second = jnp.concatenate([one[:, :WIDTH], two[:, :WIDTH]], axis=1)
        third = jnp.concatenate([one[:, WIDTH:], two[:, WIDTH:]], axis=1)

    def body(index, _):
        lanes = pl.ds(pl.multiple_of(base + index * BLOCK, BLOCK), BLOCK)
        product, start = None, 0
        for tile in tiles:
            stop = start + tile.shape[0]
            term = dot(wt_ref[:, start:stop], tile[:, lanes], 1, 0)
            product, start = (term if product is None else product + term), stop
        if first:
            column = sums[0][:, lanes]
            for more in sums[1:]:
                column = column + more[:, lanes]
            column = jnp.sum(column, axis=0, keepdims=True)
        else:
            column = jnp.zeros((1, BLOCK), F32)
        for at in range(BLOCK // PIECE):
            lane = slice(at * PIECE, (at + 1) * PIECE)
            out_ref[BLOCK // PIECE * index + at, :WIDTH, :] = product[:, lane]
            out_ref[BLOCK // PIECE * index + at, WIDTH:, :] = stat_rows(column[:, lane], second, third)
        return 0

    lax.fori_loop(0, MARKS // BLOCK, body, 0)


def side_terms(first, base, slots, tiles, more):
    return call(
        lambda *refs: side_kernel(first, base, *refs),
        [jax.ShapeDtypeStruct((EIGHT, WIDTH + 8, PIECE), F32)],
        [SMEM] + [VMEM] * (TILES + len(more)),
        [slots, *tiles, *more],
        "side_terms",
        scratch=[pltpu.VMEM((WIDTH, ROWS), B16)],
        flops=2 * ROWS * MARKS * WIDTH,
        mib=12,
    )[0]


def pair_kernel(first, *refs):
    if first:
        own_ref, other_ref, out_ref, pair_ref = refs
    else:
        own_ref, other_ref, before_ref, out_ref = refs
    stats = own_ref[0, WIDTH:, :] + other_ref[0, WIDTH:, :]
    second, third = stats[1:2], stats[2:3]
    rounded = columns_of([second[:, WIDTH:]])[:, 0:1]
    for piece in range(EIGHT):
        if first:
            column = own_ref[piece, WIDTH : WIDTH + 8, :] + other_ref[piece, WIDTH : WIDTH + 8, :]
            means = column[0:1] / third[:, 0:1]
            pair_ref[piece : piece + 1, :] = means
        else:
            means = before_ref[piece : piece + 1, :]
        side = own_ref[piece, :WIDTH, :] + other_ref[piece, :WIDTH, :]
        out_ref[piece, :WIDTH, :] = (side - rounded * means).astype(B16)
        out_ref[piece, WIDTH:, :] = tails_in_kernel([means, second, third])


def pair(first, keep, *args):
    shapes = [jax.ShapeDtypeStruct((EIGHT, WIDTH + 16, PIECE), B16)]
    if first:
        shapes.append(jax.ShapeDtypeStruct((EIGHT, PIECE), F32))
    return call(
        lambda *refs: pair_kernel(first, *refs[len(keep) :]),
        shapes,
        [VMEM] * (len(keep) + len(args)),
        [*keep, *args],
        "pair",
        flops=10**9,
        mib=12,
    )


def centre_kernel(first, total_rows, *refs):
    if first:
        terms_ref, out_ref, means_ref = refs
    else:
        terms_ref, before_ref, out_ref = refs
    tails = [terms_ref[group, WIDTH:, :] for group in range(EIGHT)]
    pairs = [join_at(tail, 0) for tail in tails]
    second = [join_at(tail, 1) for tail in tails]
    third = [join_at(tail, 2) for tail in tails]
    total, every = second[0], third[0]
    for group in range(1, EIGHT):
        total, every = total + second[group], every + third[group]
    columns = columns_of([row[:, WIDTH:] for row in second] + [total[:, :WIDTH], every[:, :WIDTH]])
    if first:
        means = third[0][:, 0:1] * pairs[0]
        for group in range(1, EIGHT):
            means = means + third[group][:, 0:1] * pairs[group]
        means = means / every[:, 0:1]
        means_ref[...] = jnp.broadcast_to(means, (8, PIECE))
    else:
        means = before_ref[0:1]
    side = terms_ref[0, :WIDTH, :].astype(F32) + columns[:, 0:1] * pairs[0]
    for group in range(1, EIGHT):
        side = side + (terms_ref[group, :WIDTH, :].astype(F32) + columns[:, group : group + 1] * pairs[group])
    totals = columns[:, EIGHT : EIGHT + 1]
    if first:
        side = side - totals * means
    else:
        squares = columns[:, EIGHT + 1 : EIGHT + 2]
        side = (side * UP - totals * means) / jnp.sqrt(squares / total_rows + 1e-06)
    side = side.astype(B16)
    for group in range(EIGHT):
        out_ref[group, :WIDTH, :] = side
        if first:
            out_ref[group, WIDTH:, :] = tail_in_kernel(means)


def centre(first, total_rows, keep, *args):
    shapes = [jax.ShapeDtypeStruct((EIGHT, WIDTH + 16 * first, PIECE), B16)]
    if first:
        shapes.append(jax.ShapeDtypeStruct((8, PIECE), F32))
    return call(
        lambda *refs: centre_kernel(first, total_rows, *refs[len(keep) :]),
        shapes,
        [VMEM] * (len(keep) + len(args)),
        [*keep, *args],
        "centre",
        flops=10**9,
        mib=12,
    )


def turn_kernel(base, _, *refs):
    *tiles, out_ref, done_ref = refs
    start = 0
    for tile in tiles:
        for row in range(0, tile.shape[0], OWN):
            out_ref[:, start : start + OWN] = jnp.transpose(tile[row : row + OWN, base : base + MARKS])
            start += OWN
    done_ref[...] = jnp.zeros(done_ref.shape, F32)


def turn(base, slots, tiles):
    rows = sum(tile.shape[0] for tile in tiles)
    return call(
        lambda *refs: turn_kernel(base, *refs),
        [pltpu.VMEM((MARKS, rows), B16), jax.ShapeDtypeStruct((8, WIDTH), F32)],
        [SMEM] + [VMEM] * len(tiles),
        [slots, *tiles],
        "turn",
        flops=10**9,
        mib=12,
    )


def image_kernel(base, last, slots_ref, early_ref, two_ref, three_ref, half_ref, means_ref, *refs):
    if last:
        before_ref, out_ref, side_ref, tail_ref = refs
    else:
        out_ref, side_ref, tail_ref = refs
    for piece in range(EIGHT):
        lanes = slice(piece * PIECE, (piece + 1) * PIECE)
        side_ref[:, lanes] = half_ref[piece, :WIDTH, :]
        tail_ref[:, lanes] = means_ref[piece, WIDTH:, :]
    shift = dot(side_ref[...], tail_ref[...], 1, 1)
    shift = (shift[:, 2:3] + shift[:, 1:2]) + shift[:, 0:1]
    start = 0
    for ref in (early_ref, two_ref, three_ref):
        if start == 0:
            term = dot(side_ref[...], ref[...], 1, 0)
        else:
            term = jnp.transpose(dot(ref[:, base : base + MARKS], side_ref[...], 1, 1))
        term = term - shift
        stop = start + term.shape[1]
        if last:
            term = term + before_ref[:, start:stop]
            for at in range(0, stop - start, OWN):
                out_ref[slots_ref[(start + at) // OWN]] = term[:, at : at + OWN].astype(B16)
        else:
            out_ref[:, start:stop] = term
        start = stop


def image_terms(slots, base, early, late, half, means, before=None):
    if before is None:
        more, shape = [], jax.ShapeDtypeStruct((WIDTH, ROWS), F32)
    else:
        more, shape = [before], jax.ShapeDtypeStruct((EIGHT, WIDTH, OWN), B16)
    return call(
        lambda *refs: image_kernel(base, before is not None, *refs),
        [shape],
        [SMEM] + [VMEM] * (5 + len(more)),
        [slots, early, *late, half, means, *more],
        "image_terms",
        scratch=[pltpu.VMEM((WIDTH, MARKS), B16), pltpu.VMEM((16, MARKS), B16)],
        flops=2 * ROWS * MARKS * WIDTH,
        mib=12,
    )[0]


def rows_from(columns):
    at = lax.broadcasted_iota(jnp.int32, (WIDTH, WIDTH), 1)
    block = jnp.zeros((WIDTH, WIDTH), F32)
    for index, column in enumerate(columns):
        block = jnp.where(at == index, column, block)
    block = jnp.transpose(block)
    return [block[index : index + 1] for index in range(len(columns))]


def owner_kernel(last, terms_ref, weight_ref, out_ref, *more):
    image = terms_ref[0].astype(F32)
    for member in range(1, EIGHT):
        image = image + terms_ref[member].astype(F32)
    weight = weight_ref[0:1, :]
    image = weight * image
    squares = jnp.sum(image * image, axis=1, keepdims=True)
    if last:
        out_ref[...] = jnp.transpose(image)
        more[0][...] = jnp.broadcast_to(rows_from([squares])[0], (8, WIDTH))
    else:
        product = weight * image
        totals = jnp.sum(product, axis=1, keepdims=True)
        body = (product * DOWN).astype(B16)
        rounded = jnp.sum(body.astype(F32), axis=1, keepdims=True)
        totals, squares, rounded = rows_from([totals, squares, rounded])
        first = jnp.concatenate([totals, squares], axis=1)
        second = jnp.concatenate([rounded, jnp.zeros((1, OWN - WIDTH), F32)], axis=1)
        tail = tails_in_kernel([first, second])
        for member in range(EIGHT):
            out_ref[member, :WIDTH, :] = body
            out_ref[member, WIDTH:, :] = tail


def owner(last, keep, terms, weight):
    if last:
        shapes = [jax.ShapeDtypeStruct((OWN, WIDTH), F32), jax.ShapeDtypeStruct((8, WIDTH), F32)]
    else:
        shapes = [jax.ShapeDtypeStruct((EIGHT, WIDTH + 16, OWN), B16)]
    return call(
        lambda *refs: owner_kernel(last, *refs[len(keep) :]),
        shapes,
        [VMEM] * (len(keep) + 2),
        [*keep, terms, weight],
        "owner",
        flops=10**9,
        mib=12,
    )


def exchange(payload, axes):
    return lax.all_to_all(payload, axes, 0, 0)


def swap_core(values):
    return lax.ppermute(values, "core", [(0, 1), (1, 0)])


def swap_z(values):
    return lax.ppermute(values, "zl", [(0, 1), (1, 0)])


def from_below(values):
    return lax.ppermute(values, "x", [(at, (at + 1) % 4) for at in range(4)])


def from_above(values):
    return lax.ppermute(values, "x", [(at, (at + 3) % 4) for at in range(4)])


def pack_kernel(rows_hbm, start_hbm, weight_hbm, out_ref, line_ref, rows_ref, start_ref, weight_ref, sems):
    copies = [
        pltpu.make_async_copy(rows_hbm, rows_ref, sems.at[0]),
        pltpu.make_async_copy(start_hbm, start_ref, sems.at[1]),
        pltpu.make_async_copy(weight_hbm, weight_ref, sems.at[2]),
    ]
    for copy in copies:
        copy.start()
    for copy in copies:
        copy.wait()
    values = rows_ref[...].astype(F32)
    scale = lax.rsqrt(jnp.sum(values * values, axis=1, keepdims=True) + 1e-06)
    out_ref[:OWN, :] = (values * scale).astype(B16)
    weight = weight_ref[...]
    wide = jnp.transpose(jnp.broadcast_to(weight, (WIDTH, OWN)))
    line_ref[...] = jnp.broadcast_to(weight, (8, OWN))
    product = wide * start_ref[...]
    totals = jnp.sum(product, axis=0, keepdims=True)
    vectors = jnp.transpose(product).astype(B16)
    half = WIDTH // 2
    out_ref[OWN : OWN + half, :OWN] = vectors[:half]
    out_ref[OWN : OWN + half, OWN:] = vectors[half:]
    rounded = jnp.sum(product.astype(B16).astype(F32), axis=0, keepdims=True)
    out_ref[OWN + half :, :] = tail_in_kernel(jnp.concatenate([weight, totals, rounded], axis=1))


def pack(rows, start, weight):
    shapes = [jax.ShapeDtypeStruct((PACK, rows.shape[1]), B16), jax.ShapeDtypeStruct((8, OWN), F32)]
    scratch = [
        pltpu.VMEM(rows.shape, B16),
        pltpu.VMEM(start.shape, F32),
        pltpu.VMEM(weight.shape, F32),
        pltpu.SemaphoreType.DMA((3,)),
    ]
    specs = [pl.BlockSpec(memory_space=pl.ANY)] * 3
    return call(pack_kernel, shapes, specs, [rows, start, weight], "pack", scratch=scratch, mib=56)


def slot_owners():
    x, z = lax.axis_index("x"), lax.axis_index("zl")
    moves = [(0, 0), (3, 0), (1, 0), (0, 1), (2, 0), (1, 1), (3, 1), (2, 1)]
    return jnp.stack([(x + dx) % 4 * 2 + (z + dz) % 2 for dx, dz in moves]).astype(jnp.int32)


def local(embeddings, landmarks, start_vectors, row_weight, spread):
    total_rows = embeddings.shape[0] * lax.axis_size(AXES)
    slots = slot_owners()
    packed, weight = pack(embeddings, start_vectors, row_weight[None, :])
    below, above, across = from_below(packed), from_above(packed), swap_z(packed)
    near = unit(landmarks)
    far = unit(swap_core(landmarks))
    zero, sums_zero = build((1,), 2048, spread, [[packed]], near, far)
    below, above, across, sums_zero = lax.optimization_barrier((below, above, across, sums_zero))
    opposite, across_above, across_below = from_below(below), from_above(across), swap_z(below)
    one, sums_one = build((3,), 2048, spread, [[below], [above], [across]], near, far)
    early_own, done_own = turn(0, slots, [zero, one])
    early_other, done_other = turn(MARKS, slots, [zero, one])
    opposite, across_above, across_below, sums_one, done_own, done_other = lax.optimization_barrier(
        (opposite, across_above, across_below, sums_one, done_own, done_other)
    )
    last = [swap_z(opposite[:SPLIT]), from_above(across_above[SPLIT:])]
    two, sums_two = build(
        (3,), 2048, spread, [[opposite], [across_above], [across_below]], near, far, [done_own, done_other]
    )
    *last, sums_two = lax.optimization_barrier((*last, sums_two))
    three, sums_three = build((1,), 2048, spread, [last], near, far)
    packs = [packed, below, above, across, opposite, across_above, across_below, *last]
    tiles = (zero, one, two, three)
    first = [*packs, sums_zero, sums_one, sums_two, sums_three]
    for step in range(ITERS):
        more = first if step == 0 else [vectors]
        other = swap_core(side_terms(step == 0, MARKS, slots, tiles, more))
        own = side_terms(step == 0, 0, slots, tiles, more)
        if step == 0:
            keep = [*tiles, early_own, early_other]
            payload, pair_means = pair(True, keep, own, other)
            sides, means = centre(True, total_rows, keep, exchange(payload, MARK_AXES))
        else:
            (payload,) = pair(False, keep, own, other, pair_means)
            (sides,) = centre(False, total_rows, keep, exchange(payload, MARK_AXES), means)
        sides = exchange(sides, MARK_AXES)
        across_core = swap_core(sides)
        if step == 0:
            tails = (sides, across_core)
        parts = image_terms(slots, 0, early_own, (two, three), sides, tails[0])
        parts = image_terms(slots, MARKS, early_other, (two, three), across_core, tails[1], parts)
        parts = exchange(parts, ROW_AXES)
        if step + 1 < ITERS:
            (vectors,) = owner(False, keep, parts, weight)
            vectors = exchange(vectors, ROW_AXES)
    image, squares = owner(True, [], parts, weight)
    count = lax.axis_size(AXES)
    every = exchange(jnp.broadcast_to(squares[:1][None], (count, 1, WIDTH)), AXES)
    scale = jnp.sqrt(jnp.sum(every[:, 0], axis=0) / total_rows + 1e-06)
    return image / scale[None, :]


def solution(mesh):
    fine = Mesh(mesh.devices.reshape(4, 2, 4, 2, 2), AXES)
    rows = P(AXES, None)
    in_specs = (rows, P(("x", "zl", "core"), None), rows, P(AXES), P())
    return jax.shard_map(local, mesh=fine, in_specs=in_specs, out_specs=rows, check_vma=False)
```

```python
import jax
import jax.numpy as jnp
from jax import lax
from jax.experimental import pallas as pl
from jax.experimental.pallas import tpu as pltpu
from jax.sharding import Mesh
from jax.sharding import PartitionSpec as P

ITERS = 2
AXES = ("y", "zh", "x", "zl", "core")
ROW_AXES = ("x", "zl")
MARK_AXES = ("y", "zh")
F32, B16 = jnp.float32, jnp.bfloat16
DOWN = 2.0**-20
UP = 2.0**20
LOG2E = 1.4426950408889634
VMEM = pl.BlockSpec(memory_space=pltpu.VMEM)
SMEM = pl.BlockSpec(memory_space=pltpu.SMEM)
OWN = 256
PIECE = 256
WIDTH = 128
MARKS = 2048
EIGHT = 8
ROWS = EIGHT * OWN
PACK = OWN + WIDTH // 2 + 16
BLOCK = 8 * PIECE
SPLIT = 160
TILES = 4


def params(mib):
    return pltpu.CompilerParams(vmem_limit_bytes=int(mib * 2**20))


def dot(left, right, left_dim, right_dim):
    dims = (((left_dim,), (right_dim,)), ((), ()))
    return lax.dot_general(left, right, dims, preferred_element_type=F32)


def parts_in_kernel(values):
    high = values.astype(B16)
    rest = values - high.astype(F32)
    mid = rest.astype(B16)
    low = (rest - mid.astype(F32)).astype(B16)
    return high.astype(F32), mid.astype(F32), low.astype(F32)


def tail_in_kernel(row):
    at = lax.broadcasted_iota(jnp.int32, (16, row.shape[1]), 0)
    high, mid, low = parts_in_kernel(row)
    zero = jnp.zeros((16, row.shape[1]), F32)
    block = jnp.where(at == 0, high, jnp.where(at == 1, mid, jnp.where(at == 2, low, zero)))
    return block.astype(B16)


def join_tail(block):
    block = block.astype(F32)
    return (block[2:3] + block[1:2]) + block[0:1]


def stat_rows(first, second, third):
    at = lax.broadcasted_iota(jnp.int32, (8, PIECE), 0)
    zero = jnp.zeros((8, PIECE), F32)
    return jnp.where(at == 0, first, jnp.where(at == 1, second, jnp.where(at == 2, third, zero)))


def tails_in_kernel(rows):
    at = lax.broadcasted_iota(jnp.int32, (16, rows[0].shape[1]), 0)
    block = jnp.zeros(at.shape, F32)
    for index, row in enumerate(rows):
        for part, value in enumerate(parts_in_kernel(row)):
            block = jnp.where(at == 3 * index + part, value, block)
    return block.astype(B16)


def join_at(block, index):
    block = block[3 * index : 3 * index + 3].astype(F32)
    return (block[2:3] + block[1:2]) + block[0:1]


def columns_of(rows):
    at = lax.broadcasted_iota(jnp.int32, (WIDTH, WIDTH), 0)
    block = jnp.zeros((WIDTH, WIDTH), F32)
    for index, row in enumerate(rows):
        block = jnp.where(at == index, row, block)
    return jnp.transpose(block)


def call(kernel, shapes, specs, args, name, scratch=(), flops=0, mib=24):
    cost = pl.CostEstimate(flops=flops, bytes_accessed=0, transcendentals=0)
    return pl.pallas_call(
        kernel,
        out_shape=shapes,
        in_specs=specs,
        out_specs=[VMEM] * len(shapes),
        scratch_shapes=list(scratch),
        compiler_params=params(mib),
        cost_estimate=cost,
        name=name,
    )(*args)


def rows_of(refs):
    if len(refs) == 1:
        return refs[0][:OWN, :]
    return jnp.concatenate([refs[0][...], refs[1][: OWN - SPLIT, :]], axis=0)


def rest_of(refs, start, stop, lanes=slice(None)):
    skip = 0 if len(refs) == 1 else SPLIT
    return refs[-1][start - skip : stop - skip, lanes]


def take(refs, counts):
    taken = []
    for count in counts:
        taken.append(refs[:count])
        refs = refs[count:]
    return taken, refs


def unit_kernel(in_ref, out_ref):
    block = 2 * OWN

    def body(index, _):
        rows = pl.ds(pl.multiple_of(index * block, block), block)
        values = in_ref[rows, :].astype(F32)
        scale = lax.rsqrt(jnp.sum(values * values, axis=1, keepdims=True) + 1e-06)
        out_ref[rows, :] = (values * scale).astype(B16)
        return 0

    lax.fori_loop(0, MARKS // block, body, 0)


def unit(values):
    shape = jax.ShapeDtypeStruct(values.shape, B16)
    return call(unit_kernel, [shape], [VMEM], [values], "unit", flops=2 * 10**9)[0]


def build_kernel(counts, groups, block, *refs):
    spread_ref = refs[0]
    packed, refs = take(refs[1:], counts)
    near_ref, far_ref, tile_ref, sums_ref, wide_ref = refs
    gamma = spread_ref[0] * LOG2E
    for source, parts in enumerate(packed):
        weight = join_tail(rest_of(parts, PACK - 16, PACK))[:, :OWN]
        column = jnp.transpose(jnp.broadcast_to(weight, (WIDTH, OWN)))
        wide_ref[source * OWN : (source + 1) * OWN, :] = column

    def half_of(marks_ref, base):
        def body(index, _):
            start = pl.multiple_of(index * block, block)
            marks = marks_ref[pl.ds(start, block), :]
            lanes = pl.ds(pl.multiple_of(base + start, block), block)
            sums = [jnp.zeros((8, WIDTH), F32) for _ in range(block // WIDTH)]
            first = 0
            for size in groups:
                rows = jnp.concatenate([rows_of(parts) for parts in packed[first : first + size]], axis=0)
                values = jnp.exp2(dot(rows, marks, 1, 1) * gamma)
                at = slice(first * OWN, (first + size) * OWN)
                tile_ref[at, lanes] = values.astype(B16)
                wide = wide_ref[at, :]
                for lane in range(block // WIDTH):
                    term = values[:, lane * WIDTH : (lane + 1) * WIDTH] * wide
                    sums[lane] = sums[lane] + jnp.sum(term.reshape(-1, 8, WIDTH), axis=0)
                first += size
            sums_ref[:, lanes] = jnp.concatenate(sums, axis=1)
            return 0

        lax.fori_loop(0, MARKS // block, body, 0)

    half_of(near_ref, 0)
    half_of(far_ref, MARKS)


def build(groups, block, spread, packed, near, far):
    rows = sum(groups) * OWN
    counts = [len(parts) for parts in packed]
    flat = [part for parts in packed for part in parts]
    return call(
        lambda *refs: build_kernel(counts, groups, block, *refs),
        [pltpu.VMEM((rows, 2 * MARKS), B16), jax.ShapeDtypeStruct((8, 2 * MARKS), F32)],
        [SMEM] + [VMEM] * (len(flat) + 2),
        [spread, *flat, near, far],
        "build",
        scratch=[pltpu.VMEM((rows, WIDTH), F32)],
        flops=4 * rows * 2 * MARKS * 512,
    )


def side_kernel(first, base, *refs):
    slots_ref, tiles, refs = refs[0], refs[1 : 1 + TILES], refs[1 + TILES :]
    half = WIDTH // 2
    if first:
        packed, refs = take(refs, [1] * 7 + [2])
        sums, (out_ref, wt_ref) = refs[:TILES], refs[TILES:]
        tails = [rest_of(parts, OWN + half, PACK) for parts in packed]
        for slot, parts in enumerate(packed):
            lanes = slice(slot * OWN, (slot + 1) * OWN)
            wt_ref[:half, lanes] = rest_of(parts, OWN, OWN + half, slice(0, OWN))
            wt_ref[half:, lanes] = rest_of(parts, OWN, OWN + half, slice(OWN, 2 * OWN))
    else:
        packed_ref, out_ref, wt_ref = refs
        for slot in range(EIGHT):
            wt_ref[:, slot * OWN : (slot + 1) * OWN] = packed_ref[slots_ref[slot], :WIDTH, :]
        tails = [packed_ref[source, WIDTH:, :] for source in range(EIGHT)]
    tail = tails[0].astype(F32)
    for more in tails[1:]:
        tail = tail + more.astype(F32)
    if first:
        tail = join_at(tail, 0)
        second = tail[:, OWN:]
        third = jnp.broadcast_to(jnp.sum(tail[:, :OWN], axis=1, keepdims=True), (1, PIECE))
    else:
        one, two = join_at(tail, 0), join_at(tail, 1)
        second = jnp.concatenate([one[:, :WIDTH], two[:, :WIDTH]], axis=1)
        third = jnp.concatenate([one[:, WIDTH:], two[:, WIDTH:]], axis=1)

    def body(index, _):
        lanes = pl.ds(pl.multiple_of(base + index * BLOCK, BLOCK), BLOCK)
        product, start = None, 0
        for tile in tiles:
            stop = start + tile.shape[0]
            term = dot(wt_ref[:, start:stop], tile[:, lanes], 1, 0)
            product, start = (term if product is None else product + term), stop
        if first:
            column = sums[0][:, lanes]
            for more in sums[1:]:
                column = column + more[:, lanes]
            column = jnp.sum(column, axis=0, keepdims=True)
        else:
            column = jnp.zeros((1, BLOCK), F32)
        for at in range(BLOCK // PIECE):
            lane = slice(at * PIECE, (at + 1) * PIECE)
            out_ref[BLOCK // PIECE * index + at, :WIDTH, :] = product[:, lane]
            out_ref[BLOCK // PIECE * index + at, WIDTH:, :] = stat_rows(column[:, lane], second, third)
        return 0

    lax.fori_loop(0, MARKS // BLOCK, body, 0)


def side_terms(first, base, slots, tiles, more):
    return call(
        lambda *refs: side_kernel(first, base, *refs),
        [jax.ShapeDtypeStruct((EIGHT, WIDTH + 8, PIECE), F32)],
        [SMEM] + [VMEM] * (TILES + len(more)),
        [slots, *tiles, *more],
        "side_terms",
        scratch=[pltpu.VMEM((WIDTH, ROWS), B16)],
        flops=2 * ROWS * MARKS * WIDTH,
    )[0]


def pair_kernel(first, *refs):
    refs = refs[TILES:]
    if first:
        own_ref, other_ref, out_ref, pair_ref = refs
    else:
        own_ref, other_ref, before_ref, out_ref = refs
    stats = own_ref[0, WIDTH:, :] + other_ref[0, WIDTH:, :]
    second, third = stats[1:2], stats[2:3]
    rounded = columns_of([second[:, WIDTH:]])[:, 0:1]
    for piece in range(EIGHT):
        if first:
            column = own_ref[piece, WIDTH : WIDTH + 8, :] + other_ref[piece, WIDTH : WIDTH + 8, :]
            means = column[0:1] / third[:, 0:1]
            pair_ref[piece : piece + 1, :] = means
        else:
            means = before_ref[piece : piece + 1, :]
        side = own_ref[piece, :WIDTH, :] + other_ref[piece, :WIDTH, :]
        out_ref[piece, :WIDTH, :] = (side - rounded * means).astype(B16)
        out_ref[piece, WIDTH:, :] = tails_in_kernel([means, second, third])


def pair(first, tiles, *args):
    shapes = [jax.ShapeDtypeStruct((EIGHT, WIDTH + 16, PIECE), B16)]
    if first:
        shapes.append(jax.ShapeDtypeStruct((EIGHT, PIECE), F32))
    return call(
        lambda *refs: pair_kernel(first, *refs),
        shapes,
        [VMEM] * (TILES + len(args)),
        [*tiles, *args],
        "pair",
        flops=10**9,
    )


def centre_kernel(first, total_rows, *refs):
    refs = refs[TILES:]
    if first:
        terms_ref, out_ref, means_ref = refs
    else:
        terms_ref, before_ref, out_ref = refs
    tails = [terms_ref[group, WIDTH:, :] for group in range(EIGHT)]
    pairs = [join_at(tail, 0) for tail in tails]
    second = [join_at(tail, 1) for tail in tails]
    third = [join_at(tail, 2) for tail in tails]
    total, every = second[0], third[0]
    for group in range(1, EIGHT):
        total, every = total + second[group], every + third[group]
    columns = columns_of([row[:, WIDTH:] for row in second] + [total[:, :WIDTH], every[:, :WIDTH]])
    if first:
        means = third[0][:, 0:1] * pairs[0]
        for group in range(1, EIGHT):
            means = means + third[group][:, 0:1] * pairs[group]
        means = means / every[:, 0:1]
        means_ref[...] = jnp.broadcast_to(means, (8, PIECE))
    else:
        means = before_ref[0:1]
    side = terms_ref[0, :WIDTH, :].astype(F32) + columns[:, 0:1] * pairs[0]
    for group in range(1, EIGHT):
        side = side + (terms_ref[group, :WIDTH, :].astype(F32) + columns[:, group : group + 1] * pairs[group])
    totals = columns[:, EIGHT : EIGHT + 1]
    if first:
        side = side - totals * means
    else:
        squares = columns[:, EIGHT + 1 : EIGHT + 2]
        side = (side * UP - totals * means) / jnp.sqrt(squares / total_rows + 1e-06)
    side = side.astype(B16)
    for group in range(EIGHT):
        out_ref[group, :WIDTH, :] = side
        if first:
            out_ref[group, WIDTH:, :] = tail_in_kernel(means)


def centre(first, total_rows, tiles, *args):
    shapes = [jax.ShapeDtypeStruct((EIGHT, WIDTH + 16 * first, PIECE), B16)]
    if first:
        shapes.append(jax.ShapeDtypeStruct((8, PIECE), F32))
    return call(
        lambda *refs: centre_kernel(first, total_rows, *refs),
        shapes,
        [VMEM] * (TILES + len(args)),
        [*tiles, *args],
        "centre",
        flops=10**9,
    )


def image_kernel(base, slots_ref, *refs):
    tiles, (half_ref, means_ref), refs = refs[:TILES], refs[TILES : TILES + 2], refs[TILES + 2 :]
    if base:
        before_ref, out_ref, side_ref, tail_ref = refs
    else:
        out_ref, side_ref, tail_ref = refs
    for piece in range(EIGHT):
        lanes = slice(piece * PIECE, (piece + 1) * PIECE)
        side_ref[:, lanes] = half_ref[piece, :WIDTH, :]
        tail_ref[:, lanes] = means_ref[piece, WIDTH:, :]
    shift = dot(tail_ref[...], side_ref[...], 1, 1)
    shift = (shift[2:3] + shift[1:2]) + shift[0:1]
    slot = 0
    for tile in tiles:
        count = tile.shape[0] // OWN
        term = dot(tile[:, base : base + MARKS], side_ref[...], 1, 1) - shift
        if base:
            term = term + before_ref[slot * OWN : (slot + count) * OWN, :]
            for at in range(count):
                out_ref[slots_ref[slot + at]] = term[at * OWN : (at + 1) * OWN].astype(B16)
        else:
            out_ref[slot * OWN : (slot + count) * OWN, :] = term
        slot += count


def image_terms(slots, tiles, half, means, before=None):
    if before is None:
        base, more, shape = 0, [], jax.ShapeDtypeStruct((ROWS, WIDTH), F32)
    else:
        base, more, shape = MARKS, [before], jax.ShapeDtypeStruct((EIGHT, OWN, WIDTH), B16)
    return call(
        lambda *refs: image_kernel(base, *refs),
        [shape],
        [SMEM] + [VMEM] * (TILES + 2 + len(more)),
        [slots, *tiles, half, means, *more],
        "image_terms",
        scratch=[pltpu.VMEM((WIDTH, MARKS), B16), pltpu.VMEM((16, MARKS), B16)],
        flops=2 * ROWS * MARKS * WIDTH,
    )[0]


def owner_kernel(last, *refs):
    if not last:
        refs = refs[TILES:]
    terms_ref, weight_ref, out_ref, *more = refs
    image = terms_ref[0].astype(F32)
    for member in range(1, EIGHT):
        image = image + terms_ref[member].astype(F32)
    weight = jnp.transpose(jnp.broadcast_to(weight_ref[0:1, :], (WIDTH, OWN)))
    image = weight * image
    squares = jnp.sum(image * image, axis=0, keepdims=True)
    if last:
        out_ref[...] = image
        more[0][...] = jnp.broadcast_to(squares, (8, WIDTH))
    else:
        product = weight * image
        totals = jnp.sum(product, axis=0, keepdims=True)
        body = (product * DOWN).astype(B16).astype(F32)
        rounded = jnp.sum(body, axis=0, keepdims=True)
        body = jnp.transpose(body).astype(B16)
        first = jnp.concatenate([totals, squares], axis=1)
        second = jnp.concatenate([rounded, jnp.zeros((1, OWN - WIDTH), F32)], axis=1)
        tail = tails_in_kernel([first, second])
        for member in range(EIGHT):
            out_ref[member, :WIDTH, :] = body
            out_ref[member, WIDTH:, :] = tail


def owner(last, tiles, terms, weight):
    if last:
        shapes = [jax.ShapeDtypeStruct((OWN, WIDTH), F32), jax.ShapeDtypeStruct((8, WIDTH), F32)]
        tiles = []
    else:
        shapes = [jax.ShapeDtypeStruct((EIGHT, WIDTH + 16, OWN), B16)]
    return call(
        lambda *refs: owner_kernel(last, *refs),
        shapes,
        [VMEM] * (len(tiles) + 2),
        [*tiles, terms, weight],
        "owner",
        flops=10**9,
    )


def exchange(payload, axes):
    return lax.all_to_all(payload, axes, 0, 0)


def swap_core(values):
    return lax.ppermute(values, "core", [(0, 1), (1, 0)])


def swap_z(values):
    return lax.ppermute(values, "zl", [(0, 1), (1, 0)])


def from_below(values):
    return lax.ppermute(values, "x", [(at, (at + 1) % 4) for at in range(4)])


def from_above(values):
    return lax.ppermute(values, "x", [(at, (at + 3) % 4) for at in range(4)])


def pack_kernel(rows_hbm, start_hbm, weight_hbm, out_ref, line_ref, rows_ref, start_ref, weight_ref, sems):
    copies = [
        pltpu.make_async_copy(rows_hbm, rows_ref, sems.at[0]),
        pltpu.make_async_copy(start_hbm, start_ref, sems.at[1]),
        pltpu.make_async_copy(weight_hbm, weight_ref, sems.at[2]),
    ]
    for copy in copies:
        copy.start()
    copies[0].wait()
    values = rows_ref[...].astype(F32)
    scale = lax.rsqrt(jnp.sum(values * values, axis=1, keepdims=True) + 1e-06)
    out_ref[:OWN, :] = (values * scale).astype(B16)
    copies[1].wait()
    copies[2].wait()
    weight = weight_ref[...]
    wide = jnp.transpose(jnp.broadcast_to(weight, (WIDTH, OWN)))
    line_ref[...] = jnp.broadcast_to(weight, (8, OWN))
    product = wide * start_ref[...]
    totals = jnp.sum(product, axis=0, keepdims=True)
    vectors = jnp.transpose(product).astype(B16)
    half = WIDTH // 2
    out_ref[OWN : OWN + half, :OWN] = vectors[:half]
    out_ref[OWN : OWN + half, OWN:] = vectors[half:]
    rounded = jnp.sum(product.astype(B16).astype(F32), axis=0, keepdims=True)
    out_ref[OWN + half :, :] = tail_in_kernel(jnp.concatenate([weight, totals, rounded], axis=1))


def pack(rows, start, weight):
    shapes = [pltpu.VMEM((PACK, rows.shape[1]), B16), jax.ShapeDtypeStruct((8, OWN), F32)]
    scratch = [
        pltpu.VMEM(rows.shape, B16),
        pltpu.VMEM(start.shape, F32),
        pltpu.VMEM(weight.shape, F32),
        pltpu.SemaphoreType.DMA((3,)),
    ]
    specs = [pl.BlockSpec(memory_space=pl.ANY)] * 3
    return call(pack_kernel, shapes, specs, [rows, start, weight], "pack", scratch=scratch, mib=54)


def slot_owners():
    x, z = lax.axis_index("x"), lax.axis_index("zl")
    moves = [(0, 0), (3, 0), (1, 0), (0, 1), (2, 0), (1, 1), (3, 1), (2, 1)]
    return jnp.stack([(x + dx) % 4 * 2 + (z + dz) % 2 for dx, dz in moves]).astype(jnp.int32)


def local(embeddings, landmarks, start_vectors, row_weight, spread):
    total_rows = embeddings.shape[0] * lax.axis_size(AXES)
    slots = slot_owners()
    packed, weight = pack(embeddings, start_vectors, row_weight[None, :])
    below, above, across = from_below(packed), from_above(packed), swap_z(packed)
    near = unit(landmarks)
    far = unit(swap_core(landmarks))
    zero, sums_zero = build((1,), 2048, spread, [[packed]], near, far)
    below, above, across, sums_zero = lax.optimization_barrier((below, above, across, sums_zero))
    opposite, across_above, across_below = from_below(below), from_above(across), swap_z(below)
    one, sums_one = build((3,), 2048, spread, [[below], [above], [across]], near, far)
    opposite, across_above, across_below, sums_one = lax.optimization_barrier(
        (opposite, across_above, across_below, sums_one)
    )
    last = [swap_z(opposite[:SPLIT]), from_above(across_above[SPLIT:])]
    two, sums_two = build((3,), 2048, spread, [[opposite], [across_above], [across_below]], near, far)
    *last, sums_two = lax.optimization_barrier((*last, sums_two))
    three, sums_three = build((1,), 2048, spread, [last], near, far)
    packs = [packed, below, above, across, opposite, across_above, across_below, *last]
    tiles = (zero, one, two, three)
    first = [*packs, sums_zero, sums_one, sums_two, sums_three]
    for step in range(ITERS):
        more = first if step == 0 else [vectors]
        other = swap_core(side_terms(step == 0, MARKS, slots, tiles, more))
        own = side_terms(step == 0, 0, slots, tiles, more)
        if step == 0:
            payload, pair_means = pair(True, tiles, own, other)
            sides, means = centre(True, total_rows, tiles, exchange(payload, MARK_AXES))
        else:
            (payload,) = pair(False, tiles, own, other, pair_means)
            (sides,) = centre(False, total_rows, tiles, exchange(payload, MARK_AXES), means)
        sides = exchange(sides, MARK_AXES)
        across_core = swap_core(sides)
        if step == 0:
            tails = (sides, across_core)
        parts = image_terms(slots, tiles, sides, tails[0])
        parts = image_terms(slots, tiles, across_core, tails[1], parts)
        parts = exchange(parts, ROW_AXES)
        if step + 1 < ITERS:
            (vectors,) = owner(False, tiles, parts, weight)
            vectors = exchange(vectors, ROW_AXES)
    image, squares = owner(True, tiles, parts, weight)
    count = lax.axis_size(AXES)
    every = exchange(jnp.broadcast_to(squares[:1][None], (count, 1, WIDTH)), AXES)
    scale = jnp.sqrt(jnp.sum(every[:, 0], axis=0) / total_rows + 1e-06)
    return image / scale[None, :]


def solution(mesh):
    fine = Mesh(mesh.devices.reshape(4, 2, 4, 2, 2), AXES)
    rows = P(AXES, None)
    in_specs = (rows, P(("x", "zl", "core"), None), rows, P(AXES), P())
    return jax.shard_map(local, mesh=fine, in_specs=in_specs, out_specs=rows, check_vma=False)
```

```python
import jax
import jax.numpy as jnp
from jax import lax
from jax.experimental import pallas as pl
from jax.experimental.pallas import tpu as pltpu
from jax.sharding import Mesh
from jax.sharding import PartitionSpec as P

ITERS = 2
AXES = ("y", "zh", "x", "zl", "core")
ROW_AXES = ("x", "zl")
MARK_AXES = ("y", "zh")
F32, B16 = jnp.float32, jnp.bfloat16
DOWN = 2.0**-20
UP = 2.0**20
LOG2E = 1.4426950408889634
VMEM = pl.BlockSpec(memory_space=pltpu.VMEM)
SMEM = pl.BlockSpec(memory_space=pltpu.SMEM)
OWN = 256
PIECE = 256
WIDTH = 128
MARKS = 2048
EIGHT = 8
ROWS = EIGHT * OWN
PACK = OWN + WIDTH // 2 + 16
BLOCK = 8 * PIECE
SPLIT = 160
TILES = 4
MOVES = [(0, 0), (3, 0), (1, 0), (0, 1), (2, 0), (1, 1), (3, 1), (2, 1)]


def params(mib):
    return pltpu.CompilerParams(vmem_limit_bytes=int(mib * 2**20))


def dot(left, right, left_dim, right_dim):
    dims = (((left_dim,), (right_dim,)), ((), ()))
    return lax.dot_general(left, right, dims, preferred_element_type=F32)


def parts_in_kernel(values):
    high = values.astype(B16)
    rest = values - high.astype(F32)
    mid = rest.astype(B16)
    low = (rest - mid.astype(F32)).astype(B16)
    return high.astype(F32), mid.astype(F32), low.astype(F32)


def tail_in_kernel(row):
    at = lax.broadcasted_iota(jnp.int32, (16, row.shape[1]), 0)
    high, mid, low = parts_in_kernel(row)
    zero = jnp.zeros((16, row.shape[1]), F32)
    block = jnp.where(at == 0, high, jnp.where(at == 1, mid, jnp.where(at == 2, low, zero)))
    return block.astype(B16)


def join_tail(block):
    block = block.astype(F32)
    return (block[2:3] + block[1:2]) + block[0:1]


def stat_rows(first, second, third):
    at = lax.broadcasted_iota(jnp.int32, (8, PIECE), 0)
    zero = jnp.zeros((8, PIECE), F32)
    return jnp.where(at == 0, first, jnp.where(at == 1, second, jnp.where(at == 2, third, zero)))


def tails_in_kernel(rows):
    at = lax.broadcasted_iota(jnp.int32, (16, rows[0].shape[1]), 0)
    block = jnp.zeros(at.shape, F32)
    for index, row in enumerate(rows):
        for part, value in enumerate(parts_in_kernel(row)):
            block = jnp.where(at == 3 * index + part, value, block)
    return block.astype(B16)


def join_at(block, index):
    block = block[3 * index : 3 * index + 3].astype(F32)
    return (block[2:3] + block[1:2]) + block[0:1]


def columns_of(rows):
    at = lax.broadcasted_iota(jnp.int32, (WIDTH, WIDTH), 0)
    block = jnp.zeros((WIDTH, WIDTH), F32)
    for index, row in enumerate(rows):
        block = jnp.where(at == index, row, block)
    return jnp.transpose(block)


def call(kernel, shapes, specs, args, name, scratch=(), flops=0, mib=24):
    cost = pl.CostEstimate(flops=flops, bytes_accessed=0, transcendentals=0)
    return pl.pallas_call(
        kernel,
        out_shape=shapes,
        in_specs=specs,
        out_specs=[VMEM] * len(shapes),
        scratch_shapes=list(scratch),
        compiler_params=params(mib),
        cost_estimate=cost,
        name=name,
    )(*args)


def rows_of(refs):
    if len(refs) == 1:
        return refs[0][:OWN, :]
    return jnp.concatenate([refs[0][...], refs[1][: OWN - SPLIT, :]], axis=0)


def rest_of(refs, start, stop, lanes=slice(None)):
    skip = 0 if len(refs) == 1 else SPLIT
    return refs[-1][start - skip : stop - skip, lanes]


def take(refs, counts):
    taken = []
    for count in counts:
        taken.append(refs[:count])
        refs = refs[count:]
    return taken, refs


def unit_kernel(in_ref, out_ref):
    block = 2 * OWN

    def body(index, _):
        rows = pl.ds(pl.multiple_of(index * block, block), block)
        values = in_ref[rows, :].astype(F32)
        scale = lax.rsqrt(jnp.sum(values * values, axis=1, keepdims=True) + 1e-06)
        out_ref[rows, :] = (values * scale).astype(B16)
        return 0

    lax.fori_loop(0, MARKS // block, body, 0)


def unit(values):
    shape = jax.ShapeDtypeStruct(values.shape, B16)
    return call(unit_kernel, [shape], [VMEM], [values], "unit", flops=2 * 10**9)[0]


def build_kernel(counts, groups, block, *refs):
    spread_ref = refs[0]
    packed, refs = take(refs[1:], counts)
    near_ref, far_ref, tile_ref, sums_ref, wide_ref = refs
    gamma = spread_ref[0] * LOG2E
    for source, parts in enumerate(packed):
        weight = join_tail(rest_of(parts, PACK - 16, PACK))[:, :OWN]
        column = jnp.transpose(jnp.broadcast_to(weight, (WIDTH, OWN)))
        wide_ref[source * OWN : (source + 1) * OWN, :] = column

    def half_of(marks_ref, base):
        def body(index, _):
            start = pl.multiple_of(index * block, block)
            marks = marks_ref[pl.ds(start, block), :]
            lanes = pl.ds(pl.multiple_of(base + start, block), block)
            sums = [jnp.zeros((8, WIDTH), F32) for _ in range(block // WIDTH)]
            first = 0
            for size in groups:
                rows = jnp.concatenate([rows_of(parts) for parts in packed[first : first + size]], axis=0)
                values = jnp.exp2(dot(rows, marks, 1, 1) * gamma)
                at = slice(first * OWN, (first + size) * OWN)
                tile_ref[at, lanes] = values.astype(B16)
                wide = wide_ref[at, :]
                for lane in range(block // WIDTH):
                    term = values[:, lane * WIDTH : (lane + 1) * WIDTH] * wide
                    sums[lane] = sums[lane] + jnp.sum(term.reshape(-1, 8, WIDTH), axis=0)
                first += size
            sums_ref[:, lanes] = jnp.concatenate(sums, axis=1)
            return 0

        lax.fori_loop(0, MARKS // block, body, 0)

    half_of(near_ref, 0)
    half_of(far_ref, MARKS)


def build(groups, block, spread, packed, near, far):
    rows = sum(groups) * OWN
    counts = [len(parts) for parts in packed]
    flat = [part for parts in packed for part in parts]
    return call(
        lambda *refs: build_kernel(counts, groups, block, *refs),
        [pltpu.VMEM((rows, 2 * MARKS), B16), jax.ShapeDtypeStruct((8, 2 * MARKS), F32)],
        [SMEM] + [VMEM] * (len(flat) + 2),
        [spread, *flat, near, far],
        "build",
        scratch=[pltpu.VMEM((rows, WIDTH), F32)],
        flops=4 * rows * 2 * MARKS * 512,
    )


def side_kernel(first, base, *refs):
    tiles, refs = refs[:TILES], refs[TILES:]
    half = WIDTH // 2
    if first:
        packed, refs = take(refs, [1] * 7 + [2])
        sums, (out_ref, wt_ref) = refs[:TILES], refs[TILES:]
        tails = [rest_of(parts, OWN + half, PACK) for parts in packed]
        for slot, parts in enumerate(packed):
            lanes = slice(slot * OWN, (slot + 1) * OWN)
            wt_ref[:half, lanes] = rest_of(parts, OWN, OWN + half, slice(0, OWN))
            wt_ref[half:, lanes] = rest_of(parts, OWN, OWN + half, slice(OWN, 2 * OWN))
    else:
        packed_ref, out_ref, wt_ref = refs
        for slot in range(EIGHT):
            wt_ref[:, slot * OWN : (slot + 1) * OWN] = packed_ref[slot_owner(slot), :WIDTH, :]
        tails = [packed_ref[source, WIDTH:, :] for source in range(EIGHT)]
    tail = tails[0].astype(F32)
    for more in tails[1:]:
        tail = tail + more.astype(F32)
    if first:
        tail = join_at(tail, 0)
        second = tail[:, OWN:]
        third = jnp.broadcast_to(jnp.sum(tail[:, :OWN], axis=1, keepdims=True), (1, PIECE))
    else:
        one, two = join_at(tail, 0), join_at(tail, 1)
        second = jnp.concatenate([one[:, :WIDTH], two[:, :WIDTH]], axis=1)
        third = jnp.concatenate([one[:, WIDTH:], two[:, WIDTH:]], axis=1)

    def body(index, _):
        lanes = pl.ds(pl.multiple_of(base + index * BLOCK, BLOCK), BLOCK)
        product, start = None, 0
        for tile in tiles:
            stop = start + tile.shape[0]
            term = dot(wt_ref[:, start:stop], tile[:, lanes], 1, 0)
            product, start = (term if product is None else product + term), stop
        if first:
            column = sums[0][:, lanes]
            for more in sums[1:]:
                column = column + more[:, lanes]
            column = jnp.sum(column, axis=0, keepdims=True)
        else:
            column = jnp.zeros((1, BLOCK), F32)
        for at in range(BLOCK // PIECE):
            lane = slice(at * PIECE, (at + 1) * PIECE)
            out_ref[BLOCK // PIECE * index + at, :WIDTH, :] = product[:, lane]
            out_ref[BLOCK // PIECE * index + at, WIDTH:, :] = stat_rows(column[:, lane], second, third)
        return 0

    lax.fori_loop(0, MARKS // BLOCK, body, 0)


def side_terms(first, base, tiles, more):
    return call(
        lambda *refs: side_kernel(first, base, *refs),
        [jax.ShapeDtypeStruct((EIGHT, WIDTH + 8, PIECE), F32)],
        [VMEM] * (TILES + len(more)),
        [*tiles, *more],
        "side_terms",
        scratch=[pltpu.VMEM((WIDTH, ROWS), B16)],
        flops=2 * ROWS * MARKS * WIDTH,
    )[0]


def pair_kernel(first, *refs):
    refs = refs[TILES:]
    if first:
        own_ref, other_ref, out_ref, pair_ref = refs
    else:
        own_ref, other_ref, before_ref, out_ref = refs
    stats = own_ref[0, WIDTH:, :] + other_ref[0, WIDTH:, :]
    second, third = stats[1:2], stats[2:3]
    rounded = columns_of([second[:, WIDTH:]])[:, 0:1]
    for piece in range(EIGHT):
        if first:
            column = own_ref[piece, WIDTH : WIDTH + 8, :] + other_ref[piece, WIDTH : WIDTH + 8, :]
            means = column[0:1] / third[:, 0:1]
            pair_ref[piece : piece + 1, :] = means
        else:
            means = before_ref[piece : piece + 1, :]
        side = own_ref[piece, :WIDTH, :] + other_ref[piece, :WIDTH, :]
        out_ref[piece, :WIDTH, :] = (side - rounded * means).astype(B16)
        out_ref[piece, WIDTH:, :] = tails_in_kernel([means, second, third])


def pair(first, tiles, *args):
    shapes = [jax.ShapeDtypeStruct((EIGHT, WIDTH + 16, PIECE), B16)]
    if first:
        shapes.append(jax.ShapeDtypeStruct((EIGHT, PIECE), F32))
    return call(
        lambda *refs: pair_kernel(first, *refs),
        shapes,
        [VMEM] * (TILES + len(args)),
        [*tiles, *args],
        "pair",
        flops=10**9,
    )


def centre_kernel(first, total_rows, *refs):
    refs = refs[TILES:]
    if first:
        terms_ref, out_ref, means_ref = refs
    else:
        terms_ref, before_ref, out_ref = refs
    tails = [terms_ref[group, WIDTH:, :] for group in range(EIGHT)]
    pairs = [join_at(tail, 0) for tail in tails]
    second = [join_at(tail, 1) for tail in tails]
    third = [join_at(tail, 2) for tail in tails]
    total, every = second[0], third[0]
    for group in range(1, EIGHT):
        total, every = total + second[group], every + third[group]
    columns = columns_of([row[:, WIDTH:] for row in second] + [total[:, :WIDTH], every[:, :WIDTH]])
    if first:
        means = third[0][:, 0:1] * pairs[0]
        for group in range(1, EIGHT):
            means = means + third[group][:, 0:1] * pairs[group]
        means = means / every[:, 0:1]
        means_ref[...] = jnp.broadcast_to(means, (8, PIECE))
    else:
        means = before_ref[0:1]
    side = terms_ref[0, :WIDTH, :].astype(F32) + columns[:, 0:1] * pairs[0]
    for group in range(1, EIGHT):
        side = side + (terms_ref[group, :WIDTH, :].astype(F32) + columns[:, group : group + 1] * pairs[group])
    totals = columns[:, EIGHT : EIGHT + 1]
    if first:
        side = side - totals * means
    else:
        squares = columns[:, EIGHT + 1 : EIGHT + 2]
        side = (side * UP - totals * means) / jnp.sqrt(squares / total_rows + 1e-06)
    side = side.astype(B16)
    for group in range(EIGHT):
        out_ref[group, :WIDTH, :] = side
        if first:
            out_ref[group, WIDTH:, :] = tail_in_kernel(means)


def centre(first, total_rows, tiles, *args):
    shapes = [jax.ShapeDtypeStruct((EIGHT, WIDTH + 16 * first, PIECE), B16)]
    if first:
        shapes.append(jax.ShapeDtypeStruct((8, PIECE), F32))
    return call(
        lambda *refs: centre_kernel(first, total_rows, *refs),
        shapes,
        [VMEM] * (TILES + len(args)),
        [*tiles, *args],
        "centre",
        flops=10**9,
    )


def image_kernel(base, *refs):
    tiles, (half_ref, means_ref), refs = refs[:TILES], refs[TILES : TILES + 2], refs[TILES + 2 :]
    if base:
        before_ref, out_ref, side_ref, tail_ref = refs
    else:
        out_ref, side_ref, tail_ref = refs
    for piece in range(EIGHT):
        lanes = slice(piece * PIECE, (piece + 1) * PIECE)
        side_ref[:, lanes] = half_ref[piece, :WIDTH, :]
        tail_ref[:, lanes] = means_ref[piece, WIDTH:, :]
    shift = dot(tail_ref[...], side_ref[...], 1, 1)
    shift = (shift[2:3] + shift[1:2]) + shift[0:1]
    slot = 0
    for tile in tiles:
        count = tile.shape[0] // OWN
        term = dot(tile[:, base : base + MARKS], side_ref[...], 1, 1) - shift
        if base:
            term = term + before_ref[slot * OWN : (slot + count) * OWN, :]
            for at in range(count):
                out_ref[slot_owner(slot + at)] = term[at * OWN : (at + 1) * OWN].astype(B16)
        else:
            out_ref[slot * OWN : (slot + count) * OWN, :] = term
        slot += count


def image_terms(tiles, half, means, before=None):
    if before is None:
        base, more, shape = 0, [], jax.ShapeDtypeStruct((ROWS, WIDTH), F32)
    else:
        base, more, shape = MARKS, [before], jax.ShapeDtypeStruct((EIGHT, OWN, WIDTH), B16)
    return call(
        lambda *refs: image_kernel(base, *refs),
        [shape],
        [VMEM] * (TILES + 2 + len(more)),
        [*tiles, half, means, *more],
        "image_terms",
        scratch=[pltpu.VMEM((WIDTH, MARKS), B16), pltpu.VMEM((16, MARKS), B16)],
        flops=2 * ROWS * MARKS * WIDTH,
    )[0]


def owner_kernel(last, *refs):
    if not last:
        refs = refs[TILES:]
    terms_ref, weight_ref, out_ref, *more = refs
    image = terms_ref[0].astype(F32)
    for member in range(1, EIGHT):
        image = image + terms_ref[member].astype(F32)
    weight = jnp.transpose(jnp.broadcast_to(weight_ref[0:1, :], (WIDTH, OWN)))
    image = weight * image
    squares = jnp.sum(image * image, axis=0, keepdims=True)
    if last:
        out_ref[...] = image
        more[0][...] = jnp.broadcast_to(squares, (8, WIDTH))
    else:
        product = weight * image
        totals = jnp.sum(product, axis=0, keepdims=True)
        body = (product * DOWN).astype(B16).astype(F32)
        rounded = jnp.sum(body, axis=0, keepdims=True)
        body = jnp.transpose(body).astype(B16)
        first = jnp.concatenate([totals, squares], axis=1)
        second = jnp.concatenate([rounded, jnp.zeros((1, OWN - WIDTH), F32)], axis=1)
        tail = tails_in_kernel([first, second])
        for member in range(EIGHT):
            out_ref[member, :WIDTH, :] = body
            out_ref[member, WIDTH:, :] = tail


def owner(last, tiles, terms, weight):
    if last:
        shapes = [jax.ShapeDtypeStruct((OWN, WIDTH), F32), jax.ShapeDtypeStruct((8, WIDTH), F32)]
        tiles = []
    else:
        shapes = [jax.ShapeDtypeStruct((EIGHT, WIDTH + 16, OWN), B16)]
    return call(
        lambda *refs: owner_kernel(last, *refs),
        shapes,
        [VMEM] * (len(tiles) + 2),
        [*tiles, terms, weight],
        "owner",
        flops=10**9,
    )


def exchange(payload, axes):
    return lax.all_to_all(payload, axes, 0, 0)


def swap_core(values):
    return lax.ppermute(values, "core", [(0, 1), (1, 0)])


def swap_z(values):
    return lax.ppermute(values, "zl", [(0, 1), (1, 0)])


def from_below(values):
    return lax.ppermute(values, "x", [(at, (at + 1) % 4) for at in range(4)])


def from_above(values):
    return lax.ppermute(values, "x", [(at, (at + 3) % 4) for at in range(4)])


def pack_kernel(rows_hbm, start_hbm, weight_hbm, out_ref, line_ref, rows_ref, start_ref, weight_ref, sems):
    copies = [
        pltpu.make_async_copy(rows_hbm, rows_ref, sems.at[0]),
        pltpu.make_async_copy(start_hbm, start_ref, sems.at[1]),
        pltpu.make_async_copy(weight_hbm, weight_ref, sems.at[2]),
    ]
    for copy in copies:
        copy.start()
    copies[0].wait()
    values = rows_ref[...].astype(F32)
    scale = lax.rsqrt(jnp.sum(values * values, axis=1, keepdims=True) + 1e-06)
    out_ref[:OWN, :] = (values * scale).astype(B16)
    copies[1].wait()
    copies[2].wait()
    weight = weight_ref[...]
    wide = jnp.transpose(jnp.broadcast_to(weight, (WIDTH, OWN)))
    line_ref[...] = jnp.broadcast_to(weight, (8, OWN))
    product = wide * start_ref[...]
    totals = jnp.sum(product, axis=0, keepdims=True)
    vectors = jnp.transpose(product).astype(B16)
    half = WIDTH // 2
    out_ref[OWN : OWN + half, :OWN] = vectors[:half]
    out_ref[OWN : OWN + half, OWN:] = vectors[half:]
    rounded = jnp.sum(product.astype(B16).astype(F32), axis=0, keepdims=True)
    out_ref[OWN + half :, :] = tail_in_kernel(jnp.concatenate([weight, totals, rounded], axis=1))


def pack(rows, start, weight):
    shapes = [pltpu.VMEM((PACK, rows.shape[1]), B16), jax.ShapeDtypeStruct((8, OWN), F32)]
    scratch = [
        pltpu.VMEM(rows.shape, B16),
        pltpu.VMEM(start.shape, F32),
        pltpu.VMEM(weight.shape, F32),
        pltpu.SemaphoreType.DMA((3,)),
    ]
    specs = [pl.BlockSpec(memory_space=pl.ANY)] * 3
    return call(pack_kernel, shapes, specs, [rows, start, weight], "pack", scratch=scratch, mib=54)


def slot_owner(slot):
    dx, dz = MOVES[slot]
    return (lax.axis_index("x") + dx) % 4 * 2 + (lax.axis_index("zl") + dz) % 2


def local(embeddings, landmarks, start_vectors, row_weight, spread):
    total_rows = embeddings.shape[0] * lax.axis_size(AXES)
    packed, weight = pack(embeddings, start_vectors, row_weight[None, :])
    below, above, across = from_below(packed), from_above(packed), swap_z(packed)
    near = unit(landmarks)
    far = unit(swap_core(landmarks))
    zero, sums_zero = build((1,), 2048, spread, [[packed]], near, far)
    below, above, across, sums_zero = lax.optimization_barrier((below, above, across, sums_zero))
    opposite, across_above, across_below = from_below(below), from_above(across), swap_z(below)
    one, sums_one = build((3,), 2048, spread, [[below], [above], [across]], near, far)
    opposite, across_above, across_below, sums_one = lax.optimization_barrier(
        (opposite, across_above, across_below, sums_one)
    )
    last = [swap_z(opposite[:SPLIT]), from_above(across_above[SPLIT:])]
    two, sums_two = build((3,), 2048, spread, [[opposite], [across_above], [across_below]], near, far)
    *last, sums_two = lax.optimization_barrier((*last, sums_two))
    three, sums_three = build((1,), 2048, spread, [last], near, far)
    packs = [packed, below, above, across, opposite, across_above, across_below, *last]
    tiles = (zero, one, two, three)
    first = [*packs, sums_zero, sums_one, sums_two, sums_three]
    for step in range(ITERS):
        more = first if step == 0 else [vectors]
        other = swap_core(side_terms(step == 0, MARKS, tiles, more))
        own = side_terms(step == 0, 0, tiles, more)
        if step == 0:
            payload, pair_means = pair(True, tiles, own, other)
            sides, means = centre(True, total_rows, tiles, exchange(payload, MARK_AXES))
        else:
            (payload,) = pair(False, tiles, own, other, pair_means)
            (sides,) = centre(False, total_rows, tiles, exchange(payload, MARK_AXES), means)
        sides = exchange(sides, MARK_AXES)
        across_core = swap_core(sides)
        if step == 0:
            tails = (sides, across_core)
        parts = image_terms(tiles, sides, tails[0])
        parts = image_terms(tiles, across_core, tails[1], parts)
        parts = exchange(parts, ROW_AXES)
        if step + 1 < ITERS:
            (vectors,) = owner(False, tiles, parts, weight)
            vectors = exchange(vectors, ROW_AXES)
    image, squares = owner(True, tiles, parts, weight)
    count = lax.axis_size(AXES)
    every = exchange(jnp.broadcast_to(squares[:1][None], (count, 1, WIDTH)), AXES)
    scale = jnp.sqrt(jnp.sum(every[:, 0], axis=0) / total_rows + 1e-06)
    return image / scale[None, :]


def solution(mesh):
    fine = Mesh(mesh.devices.reshape(4, 2, 4, 2, 2), AXES)
    rows = P(AXES, None)
    in_specs = (rows, P(("x", "zl", "core"), None), rows, P(AXES), P())
    return jax.shard_map(local, mesh=fine, in_specs=in_specs, out_specs=rows, check_vma=False)
```

```python
import jax
import jax.numpy as jnp
from jax import lax
from jax.experimental import pallas as pl
from jax.experimental.pallas import tpu as pltpu
from jax.sharding import Mesh
from jax.sharding import PartitionSpec as P

ITERS = 2
AXES = ("y", "zh", "x", "zl", "core")
ROW_AXES = ("x", "zl")
MARK_AXES = ("y", "zh")
F32, B16 = jnp.float32, jnp.bfloat16
DOWN = 2.0**-20
UP = 2.0**20
LOG2E = 1.4426950408889634
VMEM = pl.BlockSpec(memory_space=pltpu.VMEM)
SMEM = pl.BlockSpec(memory_space=pltpu.SMEM)
OWN = 256
PIECE = 256
WIDTH = 128
MARKS = 2048
EIGHT = 8
ROWS = EIGHT * OWN
PACK = OWN + WIDTH // 2 + 16
BLOCK = 8 * PIECE
SPLIT = 160
TILES = 4
MOVES = [(0, 0), (3, 0), (1, 0), (0, 1), (2, 0), (1, 1), (3, 1), (2, 1)]


def params(mib):
    return pltpu.CompilerParams(vmem_limit_bytes=int(mib * 2**20))


def dot(left, right, left_dim, right_dim):
    dims = (((left_dim,), (right_dim,)), ((), ()))
    return lax.dot_general(left, right, dims, preferred_element_type=F32)


def parts_in_kernel(values):
    high = values.astype(B16)
    rest = values - high.astype(F32)
    mid = rest.astype(B16)
    low = (rest - mid.astype(F32)).astype(B16)
    return high.astype(F32), mid.astype(F32), low.astype(F32)


def tail_in_kernel(row):
    at = lax.broadcasted_iota(jnp.int32, (16, row.shape[1]), 0)
    high, mid, low = parts_in_kernel(row)
    zero = jnp.zeros((16, row.shape[1]), F32)
    block = jnp.where(at == 0, high, jnp.where(at == 1, mid, jnp.where(at == 2, low, zero)))
    return block.astype(B16)


def join_tail(block):
    block = block.astype(F32)
    return (block[2:3] + block[1:2]) + block[0:1]


def stat_rows(first, second, third):
    at = lax.broadcasted_iota(jnp.int32, (8, PIECE), 0)
    zero = jnp.zeros((8, PIECE), F32)
    return jnp.where(at == 0, first, jnp.where(at == 1, second, jnp.where(at == 2, third, zero)))


def tails_in_kernel(rows):
    at = lax.broadcasted_iota(jnp.int32, (16, rows[0].shape[1]), 0)
    block = jnp.zeros(at.shape, F32)
    for index, row in enumerate(rows):
        for part, value in enumerate(parts_in_kernel(row)):
            block = jnp.where(at == 3 * index + part, value, block)
    return block.astype(B16)


def join_at(block, index):
    block = block[3 * index : 3 * index + 3].astype(F32)
    return (block[2:3] + block[1:2]) + block[0:1]


def columns_of(rows):
    at = lax.broadcasted_iota(jnp.int32, (WIDTH, WIDTH), 0)
    block = jnp.zeros((WIDTH, WIDTH), F32)
    for index, row in enumerate(rows):
        block = jnp.where(at == index, row, block)
    return jnp.transpose(block)


def call(kernel, shapes, specs, args, name, scratch=(), flops=0, mib=24):
    cost = pl.CostEstimate(flops=flops, bytes_accessed=0, transcendentals=0)
    return pl.pallas_call(
        kernel,
        out_shape=shapes,
        in_specs=specs,
        out_specs=[VMEM] * len(shapes),
        scratch_shapes=list(scratch),
        compiler_params=params(mib),
        cost_estimate=cost,
        name=name,
    )(*args)


def rows_of(refs):
    if len(refs) == 1:
        return refs[0][:OWN, :]
    return jnp.concatenate([refs[0][...], refs[1][: OWN - SPLIT, :]], axis=0)


def rest_of(refs, start, stop, lanes=slice(None)):
    skip = 0 if len(refs) == 1 else SPLIT
    return refs[-1][start - skip : stop - skip, lanes]


def take(refs, counts):
    taken = []
    for count in counts:
        taken.append(refs[:count])
        refs = refs[count:]
    return taken, refs


def unit_kernel(in_ref, out_ref):
    block = 2 * OWN

    def body(index, _):
        rows = pl.ds(pl.multiple_of(index * block, block), block)
        values = in_ref[rows, :].astype(F32)
        scale = lax.rsqrt(jnp.sum(values * values, axis=1, keepdims=True) + 1e-06)
        out_ref[rows, :] = (values * scale).astype(B16)
        return 0

    lax.fori_loop(0, MARKS // block, body, 0)


def unit(values):
    shape = jax.ShapeDtypeStruct(values.shape, B16)
    return call(unit_kernel, [shape], [VMEM], [values], "unit", flops=2 * 10**9)[0]


def build_kernel(counts, groups, block, *refs):
    spread_ref = refs[0]
    packed, refs = take(refs[1:], counts)
    near_ref, far_ref, tile_ref, sums_ref, wide_ref = refs
    gamma = spread_ref[0] * LOG2E
    for source, parts in enumerate(packed):
        weight = join_tail(rest_of(parts, PACK - 16, PACK))[:, :OWN]
        column = jnp.transpose(jnp.broadcast_to(weight, (WIDTH, OWN)))
        wide_ref[source * OWN : (source + 1) * OWN, :] = column

    def half_of(marks_ref, base):
        def body(index, _):
            start = pl.multiple_of(index * block, block)
            marks = marks_ref[pl.ds(start, block), :]
            lanes = pl.ds(pl.multiple_of(base + start, block), block)
            sums = [jnp.zeros((8, WIDTH), F32) for _ in range(block // WIDTH)]
            first = 0
            for size in groups:
                rows = jnp.concatenate([rows_of(parts) for parts in packed[first : first + size]], axis=0)
                values = jnp.exp2(dot(rows, marks, 1, 1) * gamma)
                at = slice(first * OWN, (first + size) * OWN)
                tile_ref[at, lanes] = values.astype(B16)
                wide = wide_ref[at, :]
                for lane in range(block // WIDTH):
                    term = values[:, lane * WIDTH : (lane + 1) * WIDTH] * wide
                    sums[lane] = sums[lane] + jnp.sum(term.reshape(-1, 8, WIDTH), axis=0)
                first += size
            sums_ref[:, lanes] = jnp.concatenate(sums, axis=1)
            return 0

        lax.fori_loop(0, MARKS // block, body, 0)

    half_of(near_ref, 0)
    half_of(far_ref, MARKS)


def build(groups, block, spread, packed, near, far):
    rows = sum(groups) * OWN
    counts = [len(parts) for parts in packed]
    flat = [part for parts in packed for part in parts]
    return call(
        lambda *refs: build_kernel(counts, groups, block, *refs),
        [pltpu.VMEM((rows, 2 * MARKS), B16), jax.ShapeDtypeStruct((8, 2 * MARKS), F32)],
        [SMEM] + [VMEM] * (len(flat) + 2),
        [spread, *flat, near, far],
        "build",
        scratch=[pltpu.VMEM((rows, WIDTH), F32)],
        flops=4 * rows * 2 * MARKS * 512,
    )


def side_kernel(first, base, *refs):
    tiles, refs = refs[:TILES], refs[TILES:]
    half = WIDTH // 2
    if first:
        packed, refs = take(refs, [1] * 7 + [2])
        sums, (out_ref, wt_ref) = refs[:TILES], refs[TILES:]
        tails = [rest_of(parts, OWN + half, PACK) for parts in packed]
        for slot, parts in enumerate(packed):
            lanes = slice(slot * OWN, (slot + 1) * OWN)
            wt_ref[:half, lanes] = rest_of(parts, OWN, OWN + half, slice(0, OWN))
            wt_ref[half:, lanes] = rest_of(parts, OWN, OWN + half, slice(OWN, 2 * OWN))
    else:
        packed_ref, out_ref, wt_ref = refs
        for slot in range(EIGHT):
            wt_ref[:, slot * OWN : (slot + 1) * OWN] = packed_ref[slot_owner(slot), :WIDTH, :]
        tails = [packed_ref[source, WIDTH:, :] for source in range(EIGHT)]
    tail = tails[0].astype(F32)
    for more in tails[1:]:
        tail = tail + more.astype(F32)
    if first:
        tail = join_at(tail, 0)
        second = tail[:, OWN:]
        third = jnp.broadcast_to(jnp.sum(tail[:, :OWN], axis=1, keepdims=True), (1, PIECE))
    else:
        one, two = join_at(tail, 0), join_at(tail, 1)
        second = jnp.concatenate([one[:, :WIDTH], two[:, :WIDTH]], axis=1)
        third = jnp.concatenate([one[:, WIDTH:], two[:, WIDTH:]], axis=1)

    def body(index, _):
        lanes = pl.ds(pl.multiple_of(base + index * BLOCK, BLOCK), BLOCK)
        product, start = None, 0
        for tile in tiles:
            stop = start + tile.shape[0]
            term = dot(wt_ref[:, start:stop], tile[:, lanes], 1, 0)
            product, start = (term if product is None else product + term), stop
        if first:
            column = sums[0][:, lanes]
            for more in sums[1:]:
                column = column + more[:, lanes]
            column = jnp.sum(column, axis=0, keepdims=True)
        else:
            column = jnp.zeros((1, BLOCK), F32)
        for at in range(BLOCK // PIECE):
            lane = slice(at * PIECE, (at + 1) * PIECE)
            out_ref[BLOCK // PIECE * index + at, :WIDTH, :] = product[:, lane]
            out_ref[BLOCK // PIECE * index + at, WIDTH:, :] = stat_rows(column[:, lane], second, third)
        return 0

    lax.fori_loop(0, MARKS // BLOCK, body, 0)


def side_terms(first, base, tiles, more):
    return call(
        lambda *refs: side_kernel(first, base, *refs),
        [jax.ShapeDtypeStruct((EIGHT, WIDTH + 8, PIECE), F32)],
        [VMEM] * (TILES + len(more)),
        [*tiles, *more],
        "side_terms",
        scratch=[pltpu.VMEM((WIDTH, ROWS), B16)],
        flops=2 * ROWS * MARKS * WIDTH,
    )[0]


def pair_kernel(first, *refs):
    refs = refs[TILES:]
    if first:
        own_ref, other_ref, out_ref, pair_ref = refs
    else:
        own_ref, other_ref, before_ref, out_ref = refs
    stats = own_ref[0, WIDTH:, :] + other_ref[0, WIDTH:, :]
    second, third = stats[1:2], stats[2:3]
    rounded = columns_of([second[:, WIDTH:]])[:, 0:1]
    for piece in range(EIGHT):
        if first:
            column = own_ref[piece, WIDTH : WIDTH + 8, :] + other_ref[piece, WIDTH : WIDTH + 8, :]
            means = column[0:1] / third[:, 0:1]
            pair_ref[piece : piece + 1, :] = means
        else:
            means = before_ref[piece : piece + 1, :]
        side = own_ref[piece, :WIDTH, :] + other_ref[piece, :WIDTH, :]
        out_ref[piece, :WIDTH, :] = (side - rounded * means).astype(B16)
        out_ref[piece, WIDTH:, :] = tails_in_kernel([means, second, third])


def pair(first, tiles, *args):
    shapes = [jax.ShapeDtypeStruct((EIGHT, WIDTH + 16, PIECE), B16)]
    if first:
        shapes.append(jax.ShapeDtypeStruct((EIGHT, PIECE), F32))
    return call(
        lambda *refs: pair_kernel(first, *refs),
        shapes,
        [VMEM] * (TILES + len(args)),
        [*tiles, *args],
        "pair",
        flops=10**9,
    )


def centre_kernel(first, total_rows, *refs):
    refs = refs[TILES:]
    if first:
        terms_ref, out_ref, means_ref = refs
    else:
        terms_ref, before_ref, out_ref = refs
    tails = [terms_ref[group, WIDTH:, :] for group in range(EIGHT)]
    pairs = [join_at(tail, 0) for tail in tails]
    second = [join_at(tail, 1) for tail in tails]
    third = [join_at(tail, 2) for tail in tails]
    total, every = second[0], third[0]
    for group in range(1, EIGHT):
        total, every = total + second[group], every + third[group]
    columns = columns_of([row[:, WIDTH:] for row in second] + [total[:, :WIDTH], every[:, :WIDTH]])
    if first:
        means = third[0][:, 0:1] * pairs[0]
        for group in range(1, EIGHT):
            means = means + third[group][:, 0:1] * pairs[group]
        means = means / every[:, 0:1]
        means_ref[...] = jnp.broadcast_to(means, (8, PIECE))
    else:
        means = before_ref[0:1]
    side = terms_ref[0, :WIDTH, :].astype(F32) + columns[:, 0:1] * pairs[0]
    for group in range(1, EIGHT):
        side = side + (terms_ref[group, :WIDTH, :].astype(F32) + columns[:, group : group + 1] * pairs[group])
    totals = columns[:, EIGHT : EIGHT + 1]
    if first:
        side = side - totals * means
    else:
        squares = columns[:, EIGHT + 1 : EIGHT + 2]
        side = (side * UP - totals * means) / jnp.sqrt(squares / total_rows + 1e-06)
    side = side.astype(B16)
    for group in range(EIGHT):
        out_ref[group, :WIDTH, :] = side
        if first:
            out_ref[group, WIDTH:, :] = tail_in_kernel(means)


def centre(first, total_rows, tiles, *args):
    shapes = [jax.ShapeDtypeStruct((EIGHT, WIDTH + 16 * first, PIECE), B16)]
    if first:
        shapes.append(jax.ShapeDtypeStruct((8, PIECE), F32))
    return call(
        lambda *refs: centre_kernel(first, total_rows, *refs),
        shapes,
        [VMEM] * (TILES + len(args)),
        [*tiles, *args],
        "centre",
        flops=10**9,
    )


def image_kernel(base, *refs):
    tiles, (half_ref, means_ref), refs = refs[:TILES], refs[TILES : TILES + 2], refs[TILES + 2 :]
    if base:
        before_ref, out_ref, side_ref, tail_ref = refs
    else:
        out_ref, side_ref, tail_ref = refs
    for piece in range(EIGHT):
        lanes = slice(piece * PIECE, (piece + 1) * PIECE)
        side_ref[:, lanes] = half_ref[piece, :WIDTH, :]
        tail_ref[:, lanes] = means_ref[piece, WIDTH:, :]
    shift = dot(tail_ref[...], side_ref[...], 1, 1)
    shift = (shift[2:3] + shift[1:2]) + shift[0:1]
    slot = 0
    for tile in tiles:
        count = tile.shape[0] // OWN
        term = dot(tile[:, base : base + MARKS], side_ref[...], 1, 1) - shift
        if base:
            term = term + before_ref[slot * OWN : (slot + count) * OWN, :]
            for at in range(count):
                out_ref[slot_owner(slot + at)] = term[at * OWN : (at + 1) * OWN].astype(B16)
        else:
            out_ref[slot * OWN : (slot + count) * OWN, :] = term
        slot += count


def image_terms(tiles, half, means, before=None):
    if before is None:
        base, more, shape = 0, [], jax.ShapeDtypeStruct((ROWS, WIDTH), F32)
    else:
        base, more, shape = MARKS, [before], jax.ShapeDtypeStruct((EIGHT, OWN, WIDTH), B16)
    return call(
        lambda *refs: image_kernel(base, *refs),
        [shape],
        [VMEM] * (TILES + 2 + len(more)),
        [*tiles, half, means, *more],
        "image_terms",
        scratch=[pltpu.VMEM((WIDTH, MARKS), B16), pltpu.VMEM((16, MARKS), B16)],
        flops=2 * ROWS * MARKS * WIDTH,
    )[0]


def owner_kernel(last, *refs):
    if not last:
        refs = refs[TILES:]
    terms_ref, weight_ref, out_ref, *more = refs
    image = terms_ref[0].astype(F32)
    for member in range(1, EIGHT):
        image = image + terms_ref[member].astype(F32)
    weight = jnp.transpose(jnp.broadcast_to(weight_ref[0:1, :], (WIDTH, OWN)))
    image = weight * image
    squares = jnp.sum(image * image, axis=0, keepdims=True)
    if last:
        out_ref[...] = image
        more[0][...] = jnp.broadcast_to(squares, (8, WIDTH))
    else:
        product = weight * image
        totals = jnp.sum(product, axis=0, keepdims=True)
        body = (product * DOWN).astype(B16).astype(F32)
        rounded = jnp.sum(body, axis=0, keepdims=True)
        body = jnp.transpose(body).astype(B16)
        first = jnp.concatenate([totals, squares], axis=1)
        second = jnp.concatenate([rounded, jnp.zeros((1, OWN - WIDTH), F32)], axis=1)
        tail = tails_in_kernel([first, second])
        for member in range(EIGHT):
            out_ref[member, :WIDTH, :] = body
            out_ref[member, WIDTH:, :] = tail


def owner(last, tiles, terms, weight):
    if last:
        shapes = [jax.ShapeDtypeStruct((OWN, WIDTH), F32), jax.ShapeDtypeStruct((8, WIDTH), F32)]
        tiles = []
    else:
        shapes = [jax.ShapeDtypeStruct((EIGHT, WIDTH + 16, OWN), B16)]
    return call(
        lambda *refs: owner_kernel(last, *refs),
        shapes,
        [VMEM] * (len(tiles) + 2),
        [*tiles, terms, weight],
        "owner",
        flops=10**9,
    )


def exchange(payload, axes):
    return lax.all_to_all(payload, axes, 0, 0)


def swap_core(values):
    return lax.ppermute(values, "core", [(0, 1), (1, 0)])


def swap_z(values):
    return lax.ppermute(values, "zl", [(0, 1), (1, 0)])


def from_below(values):
    return lax.ppermute(values, "x", [(at, (at + 1) % 4) for at in range(4)])


def from_above(values):
    return lax.ppermute(values, "x", [(at, (at + 3) % 4) for at in range(4)])


def pack_kernel(rows_hbm, start_hbm, weight_hbm, out_ref, line_ref, rows_ref, start_ref, weight_ref, sems):
    copies = [
        pltpu.make_async_copy(rows_hbm, rows_ref, sems.at[0]),
        pltpu.make_async_copy(start_hbm, start_ref, sems.at[1]),
        pltpu.make_async_copy(weight_hbm, weight_ref, sems.at[2]),
    ]
    for copy in copies:
        copy.start()
    copies[0].wait()
    values = rows_ref[...].astype(F32)
    scale = lax.rsqrt(jnp.sum(values * values, axis=1, keepdims=True) + 1e-06)
    out_ref[:OWN, :] = (values * scale).astype(B16)
    copies[1].wait()
    copies[2].wait()
    weight = weight_ref[...]
    wide = jnp.transpose(jnp.broadcast_to(weight, (WIDTH, OWN)))
    line_ref[...] = jnp.broadcast_to(weight, (8, OWN))
    product = wide * start_ref[...]
    totals = jnp.sum(product, axis=0, keepdims=True)
    vectors = jnp.transpose(product).astype(B16)
    half = WIDTH // 2
    out_ref[OWN : OWN + half, :OWN] = vectors[:half]
    out_ref[OWN : OWN + half, OWN:] = vectors[half:]
    rounded = jnp.sum(product.astype(B16).astype(F32), axis=0, keepdims=True)
    out_ref[OWN + half :, :] = tail_in_kernel(jnp.concatenate([weight, totals, rounded], axis=1))


def pack(rows, start, weight):
    shapes = [pltpu.VMEM((PACK, rows.shape[1]), B16), jax.ShapeDtypeStruct((8, OWN), F32)]
    scratch = [
        pltpu.VMEM(rows.shape, B16),
        pltpu.VMEM(start.shape, F32),
        pltpu.VMEM(weight.shape, F32),
        pltpu.SemaphoreType.DMA((3,)),
    ]
    specs = [pl.BlockSpec(memory_space=pl.ANY)] * 3
    return call(pack_kernel, shapes, specs, [rows, start, weight], "pack", scratch=scratch, mib=54)


def slot_owner(slot):
    dx, dz = MOVES[slot]
    return (lax.axis_index("x") + dx) % 4 * 2 + (lax.axis_index("zl") + dz) % 2


def local(embeddings, landmarks, start_vectors, row_weight, spread):
    total_rows = embeddings.shape[0] * lax.axis_size(AXES)
    packed, weight = pack(embeddings, start_vectors, row_weight[None, :])
    below, above, across = from_below(packed), from_above(packed), swap_z(packed)
    near = unit(landmarks)
    far = unit(swap_core(landmarks))
    zero, sums_zero = build((1,), 2048, spread, [[packed]], near, far)
    sums_zero, across, above, below = lax.optimization_barrier((sums_zero, across, above, below))
    opposite, across_above, across_below = from_below(below), from_above(across), swap_z(below)
    one, sums_one = build((3,), 2048, spread, [[below], [above], [across]], near, far)
    sums_one, across_above, across_below, opposite = lax.optimization_barrier(
        (sums_one, across_above, across_below, opposite)
    )
    last = [swap_z(opposite[:SPLIT]), from_above(across_above[SPLIT:])]
    two, sums_two = build((3,), 2048, spread, [[opposite], [across_above], [across_below]], near, far)
    sums_two, *last = lax.optimization_barrier((sums_two, *last[::-1]))
    last = last[::-1]
    three, sums_three = build((1,), 2048, spread, [last], near, far)
    packs = [packed, below, above, across, opposite, across_above, across_below, *last]
    tiles = (zero, one, two, three)
    first = [*packs, sums_zero, sums_one, sums_two, sums_three]
    for step in range(ITERS):
        more = first if step == 0 else [vectors]
        other = swap_core(side_terms(step == 0, MARKS, tiles, more))
        own = side_terms(step == 0, 0, tiles, more)
        if step == 0:
            payload, pair_means = pair(True, tiles, own, other)
            sides, means = centre(True, total_rows, tiles, exchange(payload, MARK_AXES))
        else:
            (payload,) = pair(False, tiles, own, other, pair_means)
            (sides,) = centre(False, total_rows, tiles, exchange(payload, MARK_AXES), means)
        sides = exchange(sides, MARK_AXES)
        across_core = swap_core(sides)
        if step == 0:
            tails = (sides, across_core)
        parts = image_terms(tiles, sides, tails[0])
        parts = image_terms(tiles, across_core, tails[1], parts)
        parts = exchange(parts, ROW_AXES)
        if step + 1 < ITERS:
            (vectors,) = owner(False, tiles, parts, weight)
            vectors = exchange(vectors, ROW_AXES)
    image, squares = owner(True, tiles, parts, weight)
    count = lax.axis_size(AXES)
    every = exchange(jnp.broadcast_to(squares[:1][None], (count, 1, WIDTH)), AXES)
    scale = jnp.sqrt(jnp.sum(every[:, 0], axis=0) / total_rows + 1e-06)
    return image / scale[None, :]


def solution(mesh):
    fine = Mesh(mesh.devices.reshape(4, 2, 4, 2, 2), AXES)
    rows = P(AXES, None)
    in_specs = (rows, P(("x", "zl", "core"), None), rows, P(AXES), P())
    return jax.shard_map(local, mesh=fine, in_specs=in_specs, out_specs=rows, check_vma=False)
```

```python
import jax
import jax.numpy as jnp
from jax import lax
from jax.experimental import pallas as pl
from jax.experimental.pallas import tpu as pltpu
from jax.sharding import Mesh
from jax.sharding import PartitionSpec as P

ITERS = 2
AXES = ("y", "zh", "x", "zl", "core")
ROW_AXES = ("x", "zl")
MARK_AXES = ("y", "zh")
F32, B16 = jnp.float32, jnp.bfloat16
DOWN = 2.0**-20
UP = 2.0**20
LOG2E = 1.4426950408889634
VMEM = pl.BlockSpec(memory_space=pltpu.VMEM)
SMEM = pl.BlockSpec(memory_space=pltpu.SMEM)
OWN = 256
PIECE = 256
WIDTH = 128
MARKS = 2048
EIGHT = 8
ROWS = EIGHT * OWN
PACK = OWN + WIDTH // 2 + 16
BLOCK = 8 * PIECE
SPLIT = 160
TILES = 4
MOVES = [(0, 0), (3, 0), (1, 0), (0, 1), (2, 0), (1, 1), (3, 1), (2, 1)]


def params(mib):
    return pltpu.CompilerParams(vmem_limit_bytes=int(mib * 2**20))


def dot(left, right, left_dim, right_dim):
    dims = (((left_dim,), (right_dim,)), ((), ()))
    return lax.dot_general(left, right, dims, preferred_element_type=F32)


def parts_in_kernel(values):
    high = values.astype(B16)
    rest = values - high.astype(F32)
    mid = rest.astype(B16)
    low = (rest - mid.astype(F32)).astype(B16)
    return high.astype(F32), mid.astype(F32), low.astype(F32)


def tail_in_kernel(row):
    at = lax.broadcasted_iota(jnp.int32, (16, row.shape[1]), 0)
    high, mid, low = parts_in_kernel(row)
    zero = jnp.zeros((16, row.shape[1]), F32)
    block = jnp.where(at == 0, high, jnp.where(at == 1, mid, jnp.where(at == 2, low, zero)))
    return block.astype(B16)


def join_tail(block):
    block = block.astype(F32)
    return (block[2:3] + block[1:2]) + block[0:1]


def stat_rows(first, second, third):
    at = lax.broadcasted_iota(jnp.int32, (8, PIECE), 0)
    zero = jnp.zeros((8, PIECE), F32)
    return jnp.where(at == 0, first, jnp.where(at == 1, second, jnp.where(at == 2, third, zero)))


def tails_in_kernel(rows):
    at = lax.broadcasted_iota(jnp.int32, (16, rows[0].shape[1]), 0)
    block = jnp.zeros(at.shape, F32)
    for index, row in enumerate(rows):
        for part, value in enumerate(parts_in_kernel(row)):
            block = jnp.where(at == 3 * index + part, value, block)
    return block.astype(B16)


def join_at(block, index):
    block = block[3 * index : 3 * index + 3].astype(F32)
    return (block[2:3] + block[1:2]) + block[0:1]


def columns_of(rows):
    at = lax.broadcasted_iota(jnp.int32, (WIDTH, WIDTH), 0)
    block = jnp.zeros((WIDTH, WIDTH), F32)
    for index, row in enumerate(rows):
        block = jnp.where(at == index, row, block)
    return jnp.transpose(block)


def call(kernel, shapes, specs, args, name, scratch=(), flops=0, mib=24):
    cost = pl.CostEstimate(flops=flops, bytes_accessed=0, transcendentals=0)
    return pl.pallas_call(
        kernel,
        out_shape=shapes,
        in_specs=specs,
        out_specs=[VMEM] * len(shapes),
        scratch_shapes=list(scratch),
        compiler_params=params(mib),
        cost_estimate=cost,
        name=name,
    )(*args)


def rows_of(refs):
    if len(refs) == 1:
        return refs[0][:OWN, :]
    return jnp.concatenate([refs[0][...], refs[1][: OWN - SPLIT, :]], axis=0)


def rest_of(refs, start, stop, lanes=slice(None)):
    skip = 0 if len(refs) == 1 else SPLIT
    return refs[-1][start - skip : stop - skip, lanes]


def take(refs, counts):
    taken = []
    for count in counts:
        taken.append(refs[:count])
        refs = refs[count:]
    return taken, refs


def unit_kernel(in_ref, out_ref):
    block = 2 * OWN

    def body(index, _):
        rows = pl.ds(pl.multiple_of(index * block, block), block)
        values = in_ref[rows, :].astype(F32)
        scale = lax.rsqrt(jnp.sum(values * values, axis=1, keepdims=True) + 1e-06)
        out_ref[rows, :] = (values * scale).astype(B16)
        return 0

    lax.fori_loop(0, MARKS // block, body, 0)


def unit(values):
    shape = jax.ShapeDtypeStruct(values.shape, B16)
    return call(unit_kernel, [shape], [VMEM], [values], "unit", flops=2 * 10**9)[0]


def build_kernel(counts, groups, block, *refs):
    spread_ref = refs[0]
    packed, refs = take(refs[1:], counts)
    near_ref, far_ref, tile_ref, sums_ref, wide_ref = refs
    gamma = spread_ref[0] * LOG2E
    for source, parts in enumerate(packed):
        weight = join_tail(rest_of(parts, PACK - 16, PACK))[:, :OWN]
        column = jnp.transpose(jnp.broadcast_to(weight, (WIDTH, OWN)))
        wide_ref[source * OWN : (source + 1) * OWN, :] = column

    def half_of(marks_ref, base):
        def body(index, _):
            start = pl.multiple_of(index * block, block)
            marks = marks_ref[pl.ds(start, block), :]
            lanes = pl.ds(pl.multiple_of(base + start, block), block)
            sums = [jnp.zeros((8, WIDTH), F32) for _ in range(block // WIDTH)]
            first = 0
            for size in groups:
                rows = jnp.concatenate([rows_of(parts) for parts in packed[first : first + size]], axis=0)
                values = jnp.exp2(dot(rows, marks, 1, 1) * gamma)
                at = slice(first * OWN, (first + size) * OWN)
                tile_ref[at, lanes] = values.astype(B16)
                wide = wide_ref[at, :]
                for lane in range(block // WIDTH):
                    term = values[:, lane * WIDTH : (lane + 1) * WIDTH] * wide
                    sums[lane] = sums[lane] + jnp.sum(term.reshape(-1, 8, WIDTH), axis=0)
                first += size
            sums_ref[:, lanes] = jnp.concatenate(sums, axis=1)
            return 0

        lax.fori_loop(0, MARKS // block, body, 0)

    half_of(near_ref, 0)
    half_of(far_ref, MARKS)


def build(groups, block, spread, packed, near, far):
    rows = sum(groups) * OWN
    counts = [len(parts) for parts in packed]
    flat = [part for parts in packed for part in parts]
    return call(
        lambda *refs: build_kernel(counts, groups, block, *refs),
        [pltpu.VMEM((rows, 2 * MARKS), B16), jax.ShapeDtypeStruct((8, 2 * MARKS), F32)],
        [SMEM] + [VMEM] * (len(flat) + 2),
        [spread, *flat, near, far],
        "build",
        scratch=[pltpu.VMEM((rows, WIDTH), F32)],
        flops=4 * rows * 2 * MARKS * 512,
    )


def side_kernel(first, base, *refs):
    tiles, refs = refs[:TILES], refs[TILES:]
    half = WIDTH // 2
    if first:
        packed, refs = take(refs, [1] * 7 + [2])
        sums, (out_ref, wt_ref) = refs[:TILES], refs[TILES:]
        tails = [rest_of(parts, OWN + half, PACK) for parts in packed]
        for slot, parts in enumerate(packed):
            lanes = slice(slot * OWN, (slot + 1) * OWN)
            wt_ref[:half, lanes] = rest_of(parts, OWN, OWN + half, slice(0, OWN))
            wt_ref[half:, lanes] = rest_of(parts, OWN, OWN + half, slice(OWN, 2 * OWN))
    else:
        packed_ref, out_ref, wt_ref = refs
        for slot in range(EIGHT):
            wt_ref[:, slot * OWN : (slot + 1) * OWN] = packed_ref[slot_owner(slot), :WIDTH, :]
        tails = [packed_ref[source, WIDTH:, :] for source in range(EIGHT)]
    tail = tails[0].astype(F32)
    for more in tails[1:]:
        tail = tail + more.astype(F32)
    if first:
        tail = join_at(tail, 0)
        second = tail[:, OWN:]
        third = jnp.broadcast_to(jnp.sum(tail[:, :OWN], axis=1, keepdims=True), (1, PIECE))
    else:
        one, two = join_at(tail, 0), join_at(tail, 1)
        second = jnp.concatenate([one[:, :WIDTH], two[:, :WIDTH]], axis=1)
        third = jnp.concatenate([one[:, WIDTH:], two[:, WIDTH:]], axis=1)

    def body(index, _):
        lanes = pl.ds(pl.multiple_of(base + index * BLOCK, BLOCK), BLOCK)
        product, start = None, 0
        for tile in tiles:
            stop = start + tile.shape[0]
            term = dot(wt_ref[:, start:stop], tile[:, lanes], 1, 0)
            product, start = (term if product is None else product + term), stop
        if first:
            column = sums[0][:, lanes]
            for more in sums[1:]:
                column = column + more[:, lanes]
            column = jnp.sum(column, axis=0, keepdims=True)
        else:
            column = jnp.zeros((1, BLOCK), F32)
        for at in range(BLOCK // PIECE):
            lane = slice(at * PIECE, (at + 1) * PIECE)
            out_ref[BLOCK // PIECE * index + at, :WIDTH, :] = product[:, lane]
            out_ref[BLOCK // PIECE * index + at, WIDTH:, :] = stat_rows(column[:, lane], second, third)
        return 0

    lax.fori_loop(0, MARKS // BLOCK, body, 0)


def side_terms(first, base, tiles, more):
    return call(
        lambda *refs: side_kernel(first, base, *refs),
        [jax.ShapeDtypeStruct((EIGHT, WIDTH + 8, PIECE), F32)],
        [VMEM] * (TILES + len(more)),
        [*tiles, *more],
        "side_terms",
        scratch=[pltpu.VMEM((WIDTH, ROWS), B16)],
        flops=2 * ROWS * MARKS * WIDTH,
    )[0]


def pair_kernel(first, *refs):
    refs = refs[TILES:]
    if first:
        own_ref, other_ref, out_ref, pair_ref = refs
    else:
        own_ref, other_ref, before_ref, out_ref = refs
    stats = own_ref[0, WIDTH:, :] + other_ref[0, WIDTH:, :]
    second, third = stats[1:2], stats[2:3]
    rounded = columns_of([second[:, WIDTH:]])[:, 0:1]
    for piece in range(EIGHT):
        if first:
            column = own_ref[piece, WIDTH : WIDTH + 8, :] + other_ref[piece, WIDTH : WIDTH + 8, :]
            means = column[0:1] / third[:, 0:1]
            pair_ref[piece : piece + 1, :] = means
        else:
            means = before_ref[piece : piece + 1, :]
        side = own_ref[piece, :WIDTH, :] + other_ref[piece, :WIDTH, :]
        out_ref[piece, :WIDTH, :] = (side - rounded * means).astype(B16)
        out_ref[piece, WIDTH:, :] = tails_in_kernel([means, second, third])


def pair(first, tiles, *args):
    shapes = [jax.ShapeDtypeStruct((EIGHT, WIDTH + 16, PIECE), B16)]
    if first:
        shapes.append(jax.ShapeDtypeStruct((EIGHT, PIECE), F32))
    return call(
        lambda *refs: pair_kernel(first, *refs),
        shapes,
        [VMEM] * (TILES + len(args)),
        [*tiles, *args],
        "pair",
        flops=10**9,
    )


def centre_kernel(first, total_rows, *refs):
    refs = refs[TILES:]
    if first:
        terms_ref, out_ref, means_ref = refs
    else:
        terms_ref, before_ref, out_ref = refs
    tails = [terms_ref[group, WIDTH:, :] for group in range(EIGHT)]
    pairs = [join_at(tail, 0) for tail in tails]
    second = [join_at(tail, 1) for tail in tails]
    third = [join_at(tail, 2) for tail in tails]
    total, every = second[0], third[0]
    for group in range(1, EIGHT):
        total, every = total + second[group], every + third[group]
    columns = columns_of([row[:, WIDTH:] for row in second] + [total[:, :WIDTH], every[:, :WIDTH]])
    if first:
        means = third[0][:, 0:1] * pairs[0]
        for group in range(1, EIGHT):
            means = means + third[group][:, 0:1] * pairs[group]
        means = means / every[:, 0:1]
        means_ref[...] = jnp.broadcast_to(means, (8, PIECE))
    else:
        means = before_ref[0:1]
    side = terms_ref[0, :WIDTH, :].astype(F32) + columns[:, 0:1] * pairs[0]
    for group in range(1, EIGHT):
        side = side + (terms_ref[group, :WIDTH, :].astype(F32) + columns[:, group : group + 1] * pairs[group])
    totals = columns[:, EIGHT : EIGHT + 1]
    if first:
        side = side - totals * means
    else:
        squares = columns[:, EIGHT + 1 : EIGHT + 2]
        side = (side * UP - totals * means) / jnp.sqrt(squares / total_rows + 1e-06)
    side = side.astype(B16)
    for group in range(EIGHT):
        out_ref[group, :WIDTH, :] = side
        if first:
            out_ref[group, WIDTH:, :] = tail_in_kernel(means)


def centre(first, total_rows, tiles, *args):
    shapes = [jax.ShapeDtypeStruct((EIGHT, WIDTH + 16 * first, PIECE), B16)]
    if first:
        shapes.append(jax.ShapeDtypeStruct((8, PIECE), F32))
    return call(
        lambda *refs: centre_kernel(first, total_rows, *refs),
        shapes,
        [VMEM] * (TILES + len(args)),
        [*tiles, *args],
        "centre",
        flops=10**9,
    )


def image_kernel(base, *refs):
    tiles, (half_ref, means_ref), refs = refs[:TILES], refs[TILES : TILES + 2], refs[TILES + 2 :]
    if base:
        before_ref, out_ref, side_ref, tail_ref = refs
    else:
        out_ref, side_ref, tail_ref = refs
    for piece in range(EIGHT):
        lanes = slice(piece * PIECE, (piece + 1) * PIECE)
        side_ref[:, lanes] = half_ref[piece, :WIDTH, :]
        tail_ref[:, lanes] = means_ref[piece, WIDTH:, :]
    shift = dot(tail_ref[...], side_ref[...], 1, 1)
    shift = (shift[2:3] + shift[1:2]) + shift[0:1]
    slot = 0
    for tile in tiles:
        count = tile.shape[0] // OWN
        term = dot(tile[:, base : base + MARKS], side_ref[...], 1, 1) - shift
        if base:
            term = term + before_ref[slot * OWN : (slot + count) * OWN, :]
            for at in range(count):
                out_ref[slot_owner(slot + at)] = term[at * OWN : (at + 1) * OWN].astype(B16)
        else:
            out_ref[slot * OWN : (slot + count) * OWN, :] = term
        slot += count


def image_terms(tiles, half, means, before=None):
    if before is None:
        base, more, shape = 0, [], jax.ShapeDtypeStruct((ROWS, WIDTH), F32)
    else:
        base, more, shape = MARKS, [before], jax.ShapeDtypeStruct((EIGHT, OWN, WIDTH), B16)
    return call(
        lambda *refs: image_kernel(base, *refs),
        [shape],
        [VMEM] * (TILES + 2 + len(more)),
        [*tiles, half, means, *more],
        "image_terms",
        scratch=[pltpu.VMEM((WIDTH, MARKS), B16), pltpu.VMEM((16, MARKS), B16)],
        flops=2 * ROWS * MARKS * WIDTH,
    )[0]


def owner_kernel(last, *refs):
    if not last:
        refs = refs[TILES:]
    terms_ref, weight_ref, out_ref, *more = refs
    image = terms_ref[0].astype(F32)
    for member in range(1, EIGHT):
        image = image + terms_ref[member].astype(F32)
    weight = jnp.transpose(jnp.broadcast_to(weight_ref[0:1, :], (WIDTH, OWN)))
    image = weight * image
    squares = jnp.sum(image * image, axis=0, keepdims=True)
    if last:
        out_ref[...] = image
        more[0][...] = jnp.broadcast_to(squares, (8, WIDTH))
    else:
        product = weight * image
        totals = jnp.sum(product, axis=0, keepdims=True)
        body = (product * DOWN).astype(B16).astype(F32)
        rounded = jnp.sum(body, axis=0, keepdims=True)
        body = jnp.transpose(body).astype(B16)
        first = jnp.concatenate([totals, squares], axis=1)
        second = jnp.concatenate([rounded, jnp.zeros((1, OWN - WIDTH), F32)], axis=1)
        tail = tails_in_kernel([first, second])
        for member in range(EIGHT):
            out_ref[member, :WIDTH, :] = body
            out_ref[member, WIDTH:, :] = tail


def owner(last, tiles, terms, weight):
    if last:
        shapes = [jax.ShapeDtypeStruct((OWN, WIDTH), F32), jax.ShapeDtypeStruct((8, WIDTH), F32)]
        tiles = []
    else:
        shapes = [jax.ShapeDtypeStruct((EIGHT, WIDTH + 16, OWN), B16)]
    return call(
        lambda *refs: owner_kernel(last, *refs),
        shapes,
        [VMEM] * (len(tiles) + 2),
        [*tiles, terms, weight],
        "owner",
        flops=10**9,
    )


def exchange(payload, axes):
    return lax.all_to_all(payload, axes, 0, 0)


def swap_core(values):
    return lax.ppermute(values, "core", [(0, 1), (1, 0)])


def swap_z(values):
    return lax.ppermute(values, "zl", [(0, 1), (1, 0)])


def from_below(values):
    return lax.ppermute(values, "x", [(at, (at + 1) % 4) for at in range(4)])


def from_above(values):
    return lax.ppermute(values, "x", [(at, (at + 3) % 4) for at in range(4)])


def pack_kernel(rows_hbm, start_hbm, weight_hbm, out_ref, line_ref, rows_ref, start_ref, weight_ref, sems):
    copies = [
        pltpu.make_async_copy(rows_hbm, rows_ref, sems.at[0]),
        pltpu.make_async_copy(start_hbm, start_ref, sems.at[1]),
        pltpu.make_async_copy(weight_hbm, weight_ref, sems.at[2]),
    ]
    for copy in copies:
        copy.start()
    copies[0].wait()
    values = rows_ref[...].astype(F32)
    scale = lax.rsqrt(jnp.sum(values * values, axis=1, keepdims=True) + 1e-06)
    out_ref[:OWN, :] = (values * scale).astype(B16)
    copies[1].wait()
    copies[2].wait()
    weight = weight_ref[...]
    wide = jnp.transpose(jnp.broadcast_to(weight, (WIDTH, OWN)))
    line_ref[...] = jnp.broadcast_to(weight, (8, OWN))
    product = wide * start_ref[...]
    totals = jnp.sum(product, axis=0, keepdims=True)
    vectors = jnp.transpose(product).astype(B16)
    half = WIDTH // 2
    out_ref[OWN : OWN + half, :OWN] = vectors[:half]
    out_ref[OWN : OWN + half, OWN:] = vectors[half:]
    rounded = jnp.sum(product.astype(B16).astype(F32), axis=0, keepdims=True)
    out_ref[OWN + half :, :] = tail_in_kernel(jnp.concatenate([weight, totals, rounded], axis=1))


def pack(rows, start, weight):
    shapes = [pltpu.VMEM((PACK, rows.shape[1]), B16), jax.ShapeDtypeStruct((8, OWN), F32)]
    scratch = [
        pltpu.VMEM(rows.shape, B16),
        pltpu.VMEM(start.shape, F32),
        pltpu.VMEM(weight.shape, F32),
        pltpu.SemaphoreType.DMA((3,)),
    ]
    specs = [pl.BlockSpec(memory_space=pl.ANY)] * 3
    return call(pack_kernel, shapes, specs, [rows, start, weight], "pack", scratch=scratch, mib=54)


def slot_owner(slot):
    dx, dz = MOVES[slot]
    return (lax.axis_index("x") + dx) % 4 * 2 + (lax.axis_index("zl") + dz) % 2


def local(embeddings, landmarks, start_vectors, row_weight, spread):
    total_rows = embeddings.shape[0] * lax.axis_size(AXES)
    packed, weight = pack(embeddings, start_vectors, row_weight[None, :])
    below, above, across = from_below(packed), from_above(packed), swap_z(packed)
    near = unit(landmarks)
    far = unit(swap_core(landmarks))
    zero, sums_zero = build((1,), 2048, spread, [[packed]], near, far)
    sums_zero, across, above, below = lax.optimization_barrier((sums_zero, across, above, below))
    opposite, across_above, across_below = from_below(below), from_above(across), swap_z(below)
    one, sums_one = build((3,), 2048, spread, [[below], [above], [across]], near, far)
    sums_one, across_above, across_below, opposite = lax.optimization_barrier(
        (sums_one, across_above, across_below, opposite)
    )
    last = [from_above(across_above[:SPLIT]), swap_z(opposite[SPLIT:])]
    two, sums_two = build((3,), 2048, spread, [[opposite], [across_above], [across_below]], near, far)
    sums_two, *last = lax.optimization_barrier((sums_two, *last[::-1]))
    last = last[::-1]
    three, sums_three = build((1,), 2048, spread, [last], near, far)
    packs = [packed, below, above, across, opposite, across_above, across_below, *last]
    tiles = (zero, one, two, three)
    first = [*packs, sums_zero, sums_one, sums_two, sums_three]
    for step in range(ITERS):
        more = first if step == 0 else [vectors]
        other = swap_core(side_terms(step == 0, MARKS, tiles, more))
        own = side_terms(step == 0, 0, tiles, more)
        if step == 0:
            payload, pair_means = pair(True, tiles, own, other)
            sides, means = centre(True, total_rows, tiles, exchange(payload, MARK_AXES))
        else:
            (payload,) = pair(False, tiles, own, other, pair_means)
            (sides,) = centre(False, total_rows, tiles, exchange(payload, MARK_AXES), means)
        sides = exchange(sides, MARK_AXES)
        across_core = swap_core(sides)
        if step == 0:
            tails = (sides, across_core)
        parts = image_terms(tiles, sides, tails[0])
        parts = image_terms(tiles, across_core, tails[1], parts)
        parts = exchange(parts, ROW_AXES)
        if step + 1 < ITERS:
            (vectors,) = owner(False, tiles, parts, weight)
            vectors = exchange(vectors, ROW_AXES)
    image, squares = owner(True, tiles, parts, weight)
    count = lax.axis_size(AXES)
    every = exchange(jnp.broadcast_to(squares[:1][None], (count, 1, WIDTH)), AXES)
    scale = jnp.sqrt(jnp.sum(every[:, 0], axis=0) / total_rows + 1e-06)
    return image / scale[None, :]


def solution(mesh):
    fine = Mesh(mesh.devices.reshape(4, 2, 4, 2, 2), AXES)
    rows = P(AXES, None)
    in_specs = (rows, P(("x", "zl", "core"), None), rows, P(AXES), P())
    return jax.shard_map(local, mesh=fine, in_specs=in_specs, out_specs=rows, check_vma=False)
```

```python
import jax
import jax.numpy as jnp
from jax import lax
from jax.experimental import pallas as pl
from jax.experimental.pallas import tpu as pltpu
from jax.sharding import Mesh
from jax.sharding import PartitionSpec as P

ITERS = 2
AXES = ("y", "zh", "x", "zl", "core")
ROW_AXES = ("x", "zl")
MARK_AXES = ("y", "zh")
F32, B16 = jnp.float32, jnp.bfloat16
DOWN = 2.0**-20
UP = 2.0**20
LOG2E = 1.4426950408889634
VMEM = pl.BlockSpec(memory_space=pltpu.VMEM)
SMEM = pl.BlockSpec(memory_space=pltpu.SMEM)
OWN = 256
PIECE = 256
WIDTH = 128
MARKS = 2048
EIGHT = 8
ROWS = EIGHT * OWN
PACK = OWN + WIDTH // 2 + 16
BLOCK = 8 * PIECE
SPLIT = 192
TILES = 4
MOVES = [(0, 0), (3, 0), (1, 0), (0, 1), (2, 0), (1, 1), (3, 1), (2, 1)]


def params(mib):
    return pltpu.CompilerParams(vmem_limit_bytes=int(mib * 2**20))


def dot(left, right, left_dim, right_dim):
    dims = (((left_dim,), (right_dim,)), ((), ()))
    return lax.dot_general(left, right, dims, preferred_element_type=F32)


def parts_in_kernel(values):
    high = values.astype(B16)
    rest = values - high.astype(F32)
    mid = rest.astype(B16)
    low = (rest - mid.astype(F32)).astype(B16)
    return high.astype(F32), mid.astype(F32), low.astype(F32)


def tail_in_kernel(row):
    at = lax.broadcasted_iota(jnp.int32, (16, row.shape[1]), 0)
    high, mid, low = parts_in_kernel(row)
    zero = jnp.zeros((16, row.shape[1]), F32)
    block = jnp.where(at == 0, high, jnp.where(at == 1, mid, jnp.where(at == 2, low, zero)))
    return block.astype(B16)


def join_tail(block):
    block = block.astype(F32)
    return (block[2:3] + block[1:2]) + block[0:1]


def stat_rows(first, second, third):
    at = lax.broadcasted_iota(jnp.int32, (8, PIECE), 0)
    zero = jnp.zeros((8, PIECE), F32)
    return jnp.where(at == 0, first, jnp.where(at == 1, second, jnp.where(at == 2, third, zero)))


def tails_in_kernel(rows):
    at = lax.broadcasted_iota(jnp.int32, (16, rows[0].shape[1]), 0)
    block = jnp.zeros(at.shape, F32)
    for index, row in enumerate(rows):
        for part, value in enumerate(parts_in_kernel(row)):
            block = jnp.where(at == 3 * index + part, value, block)
    return block.astype(B16)


def join_at(block, index):
    block = block[3 * index : 3 * index + 3].astype(F32)
    return (block[2:3] + block[1:2]) + block[0:1]


def columns_of(rows):
    at = lax.broadcasted_iota(jnp.int32, (WIDTH, WIDTH), 0)
    block = jnp.zeros((WIDTH, WIDTH), F32)
    for index, row in enumerate(rows):
        block = jnp.where(at == index, row, block)
    return jnp.transpose(block)


def call(kernel, shapes, specs, args, name, scratch=(), flops=0, mib=24):
    cost = pl.CostEstimate(flops=flops, bytes_accessed=0, transcendentals=0)
    return pl.pallas_call(
        kernel,
        out_shape=shapes,
        in_specs=specs,
        out_specs=[VMEM] * len(shapes),
        scratch_shapes=list(scratch),
        compiler_params=params(mib),
        cost_estimate=cost,
        name=name,
    )(*args)


def rows_of(refs):
    if len(refs) == 1:
        return refs[0][:OWN, :]
    return jnp.concatenate([refs[0][...], refs[1][: OWN - SPLIT, :]], axis=0)


def rest_of(refs, start, stop, lanes=slice(None)):
    skip = 0 if len(refs) == 1 else SPLIT
    return refs[-1][start - skip : stop - skip, lanes]


def take(refs, counts):
    taken = []
    for count in counts:
        taken.append(refs[:count])
        refs = refs[count:]
    return taken, refs


def unit_kernel(in_ref, out_ref):
    block = 2 * OWN

    def body(index, _):
        rows = pl.ds(pl.multiple_of(index * block, block), block)
        values = in_ref[rows, :].astype(F32)
        scale = lax.rsqrt(jnp.sum(values * values, axis=1, keepdims=True) + 1e-06)
        out_ref[rows, :] = (values * scale).astype(B16)
        return 0

    lax.fori_loop(0, MARKS // block, body, 0)


def unit(values):
    shape = jax.ShapeDtypeStruct(values.shape, B16)
    return call(unit_kernel, [shape], [VMEM], [values], "unit", flops=2 * 10**9)[0]


def build_kernel(counts, groups, block, *refs):
    spread_ref = refs[0]
    packed, refs = take(refs[1:], counts)
    near_ref, far_ref, tile_ref, sums_ref, wide_ref = refs
    gamma = spread_ref[0] * LOG2E
    for source, parts in enumerate(packed):
        weight = join_tail(rest_of(parts, PACK - 16, PACK))[:, :OWN]
        column = jnp.transpose(jnp.broadcast_to(weight, (WIDTH, OWN)))
        wide_ref[source * OWN : (source + 1) * OWN, :] = column

    def half_of(marks_ref, base):
        def body(index, _):
            start = pl.multiple_of(index * block, block)
            marks = marks_ref[pl.ds(start, block), :]
            lanes = pl.ds(pl.multiple_of(base + start, block), block)
            sums = [jnp.zeros((8, WIDTH), F32) for _ in range(block // WIDTH)]
            first = 0
            for size in groups:
                rows = jnp.concatenate([rows_of(parts) for parts in packed[first : first + size]], axis=0)
                values = jnp.exp2(dot(rows, marks, 1, 1) * gamma)
                at = slice(first * OWN, (first + size) * OWN)
                tile_ref[at, lanes] = values.astype(B16)
                wide = wide_ref[at, :]
                for lane in range(block // WIDTH):
                    term = values[:, lane * WIDTH : (lane + 1) * WIDTH] * wide
                    sums[lane] = sums[lane] + jnp.sum(term.reshape(-1, 8, WIDTH), axis=0)
                first += size
            sums_ref[:, lanes] = jnp.concatenate(sums, axis=1)
            return 0

        lax.fori_loop(0, MARKS // block, body, 0)

    half_of(near_ref, 0)
    half_of(far_ref, MARKS)


def build(groups, block, spread, packed, near, far):
    rows = sum(groups) * OWN
    counts = [len(parts) for parts in packed]
    flat = [part for parts in packed for part in parts]
    return call(
        lambda *refs: build_kernel(counts, groups, block, *refs),
        [pltpu.VMEM((rows, 2 * MARKS), B16), jax.ShapeDtypeStruct((8, 2 * MARKS), F32)],
        [SMEM] + [VMEM] * (len(flat) + 2),
        [spread, *flat, near, far],
        "build",
        scratch=[pltpu.VMEM((rows, WIDTH), F32)],
        flops=4 * rows * 2 * MARKS * 512,
    )


def side_kernel(first, base, *refs):
    tiles, refs = refs[:TILES], refs[TILES:]
    half = WIDTH // 2
    if first:
        packed, refs = take(refs, [1] * 7 + [2])
        sums, (out_ref, wt_ref) = refs[:TILES], refs[TILES:]
        tails = [rest_of(parts, OWN + half, PACK) for parts in packed]
        for slot, parts in enumerate(packed):
            lanes = slice(slot * OWN, (slot + 1) * OWN)
            wt_ref[:half, lanes] = rest_of(parts, OWN, OWN + half, slice(0, OWN))
            wt_ref[half:, lanes] = rest_of(parts, OWN, OWN + half, slice(OWN, 2 * OWN))
    else:
        packed_ref, out_ref, wt_ref = refs
        for slot in range(EIGHT):
            wt_ref[:, slot * OWN : (slot + 1) * OWN] = packed_ref[slot_owner(slot), :WIDTH, :]
        tails = [packed_ref[source, WIDTH:, :] for source in range(EIGHT)]
    tail = tails[0].astype(F32)
    for more in tails[1:]:
        tail = tail + more.astype(F32)
    if first:
        tail = join_at(tail, 0)
        second = tail[:, OWN:]
        third = jnp.broadcast_to(jnp.sum(tail[:, :OWN], axis=1, keepdims=True), (1, PIECE))
    else:
        one, two = join_at(tail, 0), join_at(tail, 1)
        second = jnp.concatenate([one[:, :WIDTH], two[:, :WIDTH]], axis=1)
        third = jnp.concatenate([one[:, WIDTH:], two[:, WIDTH:]], axis=1)

    def body(index, _):
        lanes = pl.ds(pl.multiple_of(base + index * BLOCK, BLOCK), BLOCK)
        product, start = None, 0
        for tile in tiles:
            stop = start + tile.shape[0]
            term = dot(wt_ref[:, start:stop], tile[:, lanes], 1, 0)
            product, start = (term if product is None else product + term), stop
        if first:
            column = sums[0][:, lanes]
            for more in sums[1:]:
                column = column + more[:, lanes]
            column = jnp.sum(column, axis=0, keepdims=True)
        else:
            column = jnp.zeros((1, BLOCK), F32)
        for at in range(BLOCK // PIECE):
            lane = slice(at * PIECE, (at + 1) * PIECE)
            out_ref[BLOCK // PIECE * index + at, :WIDTH, :] = product[:, lane]
            out_ref[BLOCK // PIECE * index + at, WIDTH:, :] = stat_rows(column[:, lane], second, third)
        return 0

    lax.fori_loop(0, MARKS // BLOCK, body, 0)


def side_terms(first, base, tiles, more):
    return call(
        lambda *refs: side_kernel(first, base, *refs),
        [jax.ShapeDtypeStruct((EIGHT, WIDTH + 8, PIECE), F32)],
        [VMEM] * (TILES + len(more)),
        [*tiles, *more],
        "side_terms",
        scratch=[pltpu.VMEM((WIDTH, ROWS), B16)],
        flops=2 * ROWS * MARKS * WIDTH,
    )[0]


def pair_kernel(first, *refs):
    refs = refs[TILES:]
    if first:
        own_ref, other_ref, out_ref, pair_ref = refs
    else:
        own_ref, other_ref, before_ref, out_ref = refs
    stats = own_ref[0, WIDTH:, :] + other_ref[0, WIDTH:, :]
    second, third = stats[1:2], stats[2:3]
    rounded = columns_of([second[:, WIDTH:]])[:, 0:1]
    for piece in range(EIGHT):
        if first:
            column = own_ref[piece, WIDTH : WIDTH + 8, :] + other_ref[piece, WIDTH : WIDTH + 8, :]
            means = column[0:1] / third[:, 0:1]
            pair_ref[piece : piece + 1, :] = means
        else:
            means = before_ref[piece : piece + 1, :]
        side = own_ref[piece, :WIDTH, :] + other_ref[piece, :WIDTH, :]
        out_ref[piece, :WIDTH, :] = (side - rounded * means).astype(B16)
        out_ref[piece, WIDTH:, :] = tails_in_kernel([means, second, third])


def pair(first, tiles, *args):
    shapes = [jax.ShapeDtypeStruct((EIGHT, WIDTH + 16, PIECE), B16)]
    if first:
        shapes.append(jax.ShapeDtypeStruct((EIGHT, PIECE), F32))
    return call(
        lambda *refs: pair_kernel(first, *refs),
        shapes,
        [VMEM] * (TILES + len(args)),
        [*tiles, *args],
        "pair",
        flops=10**9,
    )


def centre_kernel(first, total_rows, *refs):
    refs = refs[TILES:]
    if first:
        terms_ref, out_ref, means_ref = refs
    else:
        terms_ref, before_ref, out_ref = refs
    tails = [terms_ref[group, WIDTH:, :] for group in range(EIGHT)]
    pairs = [join_at(tail, 0) for tail in tails]
    second = [join_at(tail, 1) for tail in tails]
    third = [join_at(tail, 2) for tail in tails]
    total, every = second[0], third[0]
    for group in range(1, EIGHT):
        total, every = total + second[group], every + third[group]
    columns = columns_of([row[:, WIDTH:] for row in second] + [total[:, :WIDTH], every[:, :WIDTH]])
    if first:
        means = third[0][:, 0:1] * pairs[0]
        for group in range(1, EIGHT):
            means = means + third[group][:, 0:1] * pairs[group]
        means = means / every[:, 0:1]
        means_ref[...] = jnp.broadcast_to(means, (8, PIECE))
    else:
        means = before_ref[0:1]
    side = terms_ref[0, :WIDTH, :].astype(F32) + columns[:, 0:1] * pairs[0]
    for group in range(1, EIGHT):
        side = side + (terms_ref[group, :WIDTH, :].astype(F32) + columns[:, group : group + 1] * pairs[group])
    totals = columns[:, EIGHT : EIGHT + 1]
    if first:
        side = side - totals * means
    else:
        squares = columns[:, EIGHT + 1 : EIGHT + 2]
        side = (side * UP - totals * means) / jnp.sqrt(squares / total_rows + 1e-06)
    side = side.astype(B16)
    for group in range(EIGHT):
        out_ref[group, :WIDTH, :] = side
        if first:
            out_ref[group, WIDTH:, :] = tail_in_kernel(means)


def centre(first, total_rows, tiles, *args):
    shapes = [jax.ShapeDtypeStruct((EIGHT, WIDTH + 16 * first, PIECE), B16)]
    if first:
        shapes.append(jax.ShapeDtypeStruct((8, PIECE), F32))
    return call(
        lambda *refs: centre_kernel(first, total_rows, *refs),
        shapes,
        [VMEM] * (TILES + len(args)),
        [*tiles, *args],
        "centre",
        flops=10**9,
    )


def image_kernel(base, *refs):
    tiles, (half_ref, means_ref), refs = refs[:TILES], refs[TILES : TILES + 2], refs[TILES + 2 :]
    if base:
        before_ref, out_ref, side_ref, tail_ref = refs
    else:
        out_ref, side_ref, tail_ref = refs
    for piece in range(EIGHT):
        lanes = slice(piece * PIECE, (piece + 1) * PIECE)
        side_ref[:, lanes] = half_ref[piece, :WIDTH, :]
        tail_ref[:, lanes] = means_ref[piece, WIDTH:, :]
    shift = dot(tail_ref[...], side_ref[...], 1, 1)
    shift = (shift[2:3] + shift[1:2]) + shift[0:1]
    slot = 0
    for tile in tiles:
        count = tile.shape[0] // OWN
        term = dot(tile[:, base : base + MARKS], side_ref[...], 1, 1) - shift
        if base:
            term = term + before_ref[slot * OWN : (slot + count) * OWN, :]
            for at in range(count):
                out_ref[slot_owner(slot + at)] = term[at * OWN : (at + 1) * OWN].astype(B16)
        else:
            out_ref[slot * OWN : (slot + count) * OWN, :] = term
        slot += count


def image_terms(tiles, half, means, before=None):
    if before is None:
        base, more, shape = 0, [], jax.ShapeDtypeStruct((ROWS, WIDTH), F32)
    else:
        base, more, shape = MARKS, [before], jax.ShapeDtypeStruct((EIGHT, OWN, WIDTH), B16)
    return call(
        lambda *refs: image_kernel(base, *refs),
        [shape],
        [VMEM] * (TILES + 2 + len(more)),
        [*tiles, half, means, *more],
        "image_terms",
        scratch=[pltpu.VMEM((WIDTH, MARKS), B16), pltpu.VMEM((16, MARKS), B16)],
        flops=2 * ROWS * MARKS * WIDTH,
    )[0]


def owner_kernel(last, *refs):
    if not last:
        refs = refs[TILES:]
    terms_ref, weight_ref, out_ref, *more = refs
    image = terms_ref[0].astype(F32)
    for member in range(1, EIGHT):
        image = image + terms_ref[member].astype(F32)
    weight = jnp.transpose(jnp.broadcast_to(weight_ref[0:1, :], (WIDTH, OWN)))
    image = weight * image
    squares = jnp.sum(image * image, axis=0, keepdims=True)
    if last:
        out_ref[...] = image
        more[0][...] = jnp.broadcast_to(squares, (8, WIDTH))
    else:
        product = weight * image
        totals = jnp.sum(product, axis=0, keepdims=True)
        body = (product * DOWN).astype(B16).astype(F32)
        rounded = jnp.sum(body, axis=0, keepdims=True)
        body = jnp.transpose(body).astype(B16)
        first = jnp.concatenate([totals, squares], axis=1)
        second = jnp.concatenate([rounded, jnp.zeros((1, OWN - WIDTH), F32)], axis=1)
        tail = tails_in_kernel([first, second])
        for member in range(EIGHT):
            out_ref[member, :WIDTH, :] = body
            out_ref[member, WIDTH:, :] = tail


def owner(last, tiles, terms, weight):
    if last:
        shapes = [jax.ShapeDtypeStruct((OWN, WIDTH), F32), jax.ShapeDtypeStruct((8, WIDTH), F32)]
        tiles = []
    else:
        shapes = [jax.ShapeDtypeStruct((EIGHT, WIDTH + 16, OWN), B16)]
    return call(
        lambda *refs: owner_kernel(last, *refs),
        shapes,
        [VMEM] * (len(tiles) + 2),
        [*tiles, terms, weight],
        "owner",
        flops=10**9,
    )


def exchange(payload, axes):
    return lax.all_to_all(payload, axes, 0, 0)


def swap_core(values):
    return lax.ppermute(values, "core", [(0, 1), (1, 0)])


def swap_z(values):
    return lax.ppermute(values, "zl", [(0, 1), (1, 0)])


def from_below(values):
    return lax.ppermute(values, "x", [(at, (at + 1) % 4) for at in range(4)])


def from_above(values):
    return lax.ppermute(values, "x", [(at, (at + 3) % 4) for at in range(4)])


def pack_kernel(rows_hbm, start_hbm, weight_hbm, out_ref, line_ref, rows_ref, start_ref, weight_ref, sems):
    copies = [
        pltpu.make_async_copy(rows_hbm, rows_ref, sems.at[0]),
        pltpu.make_async_copy(start_hbm, start_ref, sems.at[1]),
        pltpu.make_async_copy(weight_hbm, weight_ref, sems.at[2]),
    ]
    for copy in copies:
        copy.start()
    copies[0].wait()
    values = rows_ref[...].astype(F32)
    scale = lax.rsqrt(jnp.sum(values * values, axis=1, keepdims=True) + 1e-06)
    out_ref[:OWN, :] = (values * scale).astype(B16)
    copies[1].wait()
    copies[2].wait()
    weight = weight_ref[...]
    wide = jnp.transpose(jnp.broadcast_to(weight, (WIDTH, OWN)))
    line_ref[...] = jnp.broadcast_to(weight, (8, OWN))
    product = wide * start_ref[...]
    totals = jnp.sum(product, axis=0, keepdims=True)
    vectors = jnp.transpose(product).astype(B16)
    half = WIDTH // 2
    out_ref[OWN : OWN + half, :OWN] = vectors[:half]
    out_ref[OWN : OWN + half, OWN:] = vectors[half:]
    rounded = jnp.sum(product.astype(B16).astype(F32), axis=0, keepdims=True)
    out_ref[OWN + half :, :] = tail_in_kernel(jnp.concatenate([weight, totals, rounded], axis=1))


def pack(rows, start, weight):
    shapes = [pltpu.VMEM((PACK, rows.shape[1]), B16), jax.ShapeDtypeStruct((8, OWN), F32)]
    scratch = [
        pltpu.VMEM(rows.shape, B16),
        pltpu.VMEM(start.shape, F32),
        pltpu.VMEM(weight.shape, F32),
        pltpu.SemaphoreType.DMA((3,)),
    ]
    specs = [pl.BlockSpec(memory_space=pl.ANY)] * 3
    return call(pack_kernel, shapes, specs, [rows, start, weight], "pack", scratch=scratch, mib=54)


def slot_owner(slot):
    dx, dz = MOVES[slot]
    return (lax.axis_index("x") + dx) % 4 * 2 + (lax.axis_index("zl") + dz) % 2


def local(embeddings, landmarks, start_vectors, row_weight, spread):
    total_rows = embeddings.shape[0] * lax.axis_size(AXES)
    packed, weight = pack(embeddings, start_vectors, row_weight[None, :])
    below, above, across = from_below(packed), from_above(packed), swap_z(packed)
    near = unit(landmarks)
    far = unit(swap_core(landmarks))
    zero, sums_zero = build((1,), 2048, spread, [[packed]], near, far)
    sums_zero, across, above, below = lax.optimization_barrier((sums_zero, across, above, below))
    opposite, across_above, across_below = from_below(below), from_above(across), swap_z(below)
    one, sums_one = build((3,), 2048, spread, [[below], [above], [across]], near, far)
    sums_one, across_above, across_below, opposite = lax.optimization_barrier(
        (sums_one, across_above, across_below, opposite)
    )
    last = [from_above(across_above[:SPLIT]), swap_z(opposite[SPLIT:])]
    two, sums_two = build((3,), 2048, spread, [[opposite], [across_above], [across_below]], near, far)
    sums_two, *last = lax.optimization_barrier((sums_two, *last[::-1]))
    last = last[::-1]
    three, sums_three = build((1,), 2048, spread, [last], near, far)
    packs = [packed, below, above, across, opposite, across_above, across_below, *last]
    tiles = (zero, one, two, three)
    first = [*packs, sums_zero, sums_one, sums_two, sums_three]
    for step in range(ITERS):
        more = first if step == 0 else [vectors]
        other = swap_core(side_terms(step == 0, MARKS, tiles, more))
        own = side_terms(step == 0, 0, tiles, more)
        if step == 0:
            payload, pair_means = pair(True, tiles, own, other)
            sides, means = centre(True, total_rows, tiles, exchange(payload, MARK_AXES))
        else:
            (payload,) = pair(False, tiles, own, other, pair_means)
            (sides,) = centre(False, total_rows, tiles, exchange(payload, MARK_AXES), means)
        sides = exchange(sides, MARK_AXES)
        across_core = swap_core(sides)
        if step == 0:
            tails = (sides, across_core)
        parts = image_terms(tiles, sides, tails[0])
        parts = image_terms(tiles, across_core, tails[1], parts)
        parts = exchange(parts, ROW_AXES)
        if step + 1 < ITERS:
            (vectors,) = owner(False, tiles, parts, weight)
            vectors = exchange(vectors, ROW_AXES)
    image, squares = owner(True, tiles, parts, weight)
    count = lax.axis_size(AXES)
    every = exchange(jnp.broadcast_to(squares[:1][None], (count, 1, WIDTH)), AXES)
    scale = jnp.sqrt(jnp.sum(every[:, 0], axis=0) / total_rows + 1e-06)
    return image / scale[None, :]


def solution(mesh):
    fine = Mesh(mesh.devices.reshape(4, 2, 4, 2, 2), AXES)
    rows = P(AXES, None)
    in_specs = (rows, P(("x", "zl", "core"), None), rows, P(AXES), P())
    return jax.shard_map(local, mesh=fine, in_specs=in_specs, out_specs=rows, check_vma=False)
```

```python
import jax
import jax.numpy as jnp
from jax import lax
from jax.experimental import pallas as pl
from jax.experimental.pallas import tpu as pltpu
from jax.sharding import Mesh
from jax.sharding import PartitionSpec as P

ITERS = 2
AXES = ("y", "zh", "x", "zl", "core")
ROW_AXES = ("x", "zl")
MARK_AXES = ("y", "zh")
F32, B16 = jnp.float32, jnp.bfloat16
DOWN = 2.0**-20
UP = 2.0**20
LOG2E = 1.4426950408889634
VMEM = pl.BlockSpec(memory_space=pltpu.VMEM)
SMEM = pl.BlockSpec(memory_space=pltpu.SMEM)
OWN = 256
PIECE = 256
WIDTH = 128
MARKS = 2048
EIGHT = 8
ROWS = EIGHT * OWN
PACK = OWN + WIDTH // 2 + 16
BLOCK = 8 * PIECE
SPLIT = 128
TILES = 4
MOVES = [(0, 0), (3, 0), (1, 0), (0, 1), (2, 0), (1, 1), (3, 1), (2, 1)]


def params(mib):
    return pltpu.CompilerParams(vmem_limit_bytes=int(mib * 2**20))


def dot(left, right, left_dim, right_dim):
    dims = (((left_dim,), (right_dim,)), ((), ()))
    return lax.dot_general(left, right, dims, preferred_element_type=F32)


def parts_in_kernel(values):
    high = values.astype(B16)
    rest = values - high.astype(F32)
    mid = rest.astype(B16)
    low = (rest - mid.astype(F32)).astype(B16)
    return high.astype(F32), mid.astype(F32), low.astype(F32)


def tail_in_kernel(row):
    at = lax.broadcasted_iota(jnp.int32, (16, row.shape[1]), 0)
    high, mid, low = parts_in_kernel(row)
    zero = jnp.zeros((16, row.shape[1]), F32)
    block = jnp.where(at == 0, high, jnp.where(at == 1, mid, jnp.where(at == 2, low, zero)))
    return block.astype(B16)


def join_tail(block):
    block = block.astype(F32)
    return (block[2:3] + block[1:2]) + block[0:1]


def stat_rows(first, second, third):
    at = lax.broadcasted_iota(jnp.int32, (8, PIECE), 0)
    zero = jnp.zeros((8, PIECE), F32)
    return jnp.where(at == 0, first, jnp.where(at == 1, second, jnp.where(at == 2, third, zero)))


def tails_in_kernel(rows):
    at = lax.broadcasted_iota(jnp.int32, (16, rows[0].shape[1]), 0)
    block = jnp.zeros(at.shape, F32)
    for index, row in enumerate(rows):
        for part, value in enumerate(parts_in_kernel(row)):
            block = jnp.where(at == 3 * index + part, value, block)
    return block.astype(B16)


def join_at(block, index):
    block = block[3 * index : 3 * index + 3].astype(F32)
    return (block[2:3] + block[1:2]) + block[0:1]


def columns_of(rows):
    at = lax.broadcasted_iota(jnp.int32, (WIDTH, WIDTH), 0)
    block = jnp.zeros((WIDTH, WIDTH), F32)
    for index, row in enumerate(rows):
        block = jnp.where(at == index, row, block)
    return jnp.transpose(block)


def call(kernel, shapes, specs, args, name, scratch=(), flops=0, mib=24):
    cost = pl.CostEstimate(flops=flops, bytes_accessed=0, transcendentals=0)
    return pl.pallas_call(
        kernel,
        out_shape=shapes,
        in_specs=specs,
        out_specs=[VMEM] * len(shapes),
        scratch_shapes=list(scratch),
        compiler_params=params(mib),
        cost_estimate=cost,
        name=name,
    )(*args)


def rows_of(refs):
    if len(refs) == 1:
        return refs[0][:OWN, :]
    return jnp.concatenate([refs[0][...], refs[1][: OWN - SPLIT, :]], axis=0)


def rest_of(refs, start, stop, lanes=slice(None)):
    skip = 0 if len(refs) == 1 else SPLIT
    return refs[-1][start - skip : stop - skip, lanes]


def take(refs, counts):
    taken = []
    for count in counts:
        taken.append(refs[:count])
        refs = refs[count:]
    return taken, refs


def unit_kernel(in_ref, out_ref):
    block = 2 * OWN

    def body(index, _):
        rows = pl.ds(pl.multiple_of(index * block, block), block)
        values = in_ref[rows, :].astype(F32)
        scale = lax.rsqrt(jnp.sum(values * values, axis=1, keepdims=True) + 1e-06)
        out_ref[rows, :] = (values * scale).astype(B16)
        return 0

    lax.fori_loop(0, MARKS // block, body, 0)


def unit(values):
    shape = jax.ShapeDtypeStruct(values.shape, B16)
    return call(unit_kernel, [shape], [VMEM], [values], "unit", flops=2 * 10**9)[0]


def build_kernel(counts, groups, block, *refs):
    spread_ref = refs[0]
    packed, refs = take(refs[1:], counts)
    near_ref, far_ref, tile_ref, sums_ref, wide_ref = refs
    gamma = spread_ref[0] * LOG2E
    for source, parts in enumerate(packed):
        weight = join_tail(rest_of(parts, PACK - 16, PACK))[:, :OWN]
        column = jnp.transpose(jnp.broadcast_to(weight, (WIDTH, OWN)))
        wide_ref[source * OWN : (source + 1) * OWN, :] = column

    def half_of(marks_ref, base):
        def body(index, _):
            start = pl.multiple_of(index * block, block)
            marks = marks_ref[pl.ds(start, block), :]
            lanes = pl.ds(pl.multiple_of(base + start, block), block)
            sums = [jnp.zeros((8, WIDTH), F32) for _ in range(block // WIDTH)]
            first = 0
            for size in groups:
                rows = jnp.concatenate([rows_of(parts) for parts in packed[first : first + size]], axis=0)
                values = jnp.exp2(dot(rows, marks, 1, 1) * gamma)
                at = slice(first * OWN, (first + size) * OWN)
                tile_ref[at, lanes] = values.astype(B16)
                wide = wide_ref[at, :]
                for lane in range(block // WIDTH):
                    term = values[:, lane * WIDTH : (lane + 1) * WIDTH] * wide
                    sums[lane] = sums[lane] + jnp.sum(term.reshape(-1, 8, WIDTH), axis=0)
                first += size
            sums_ref[:, lanes] = jnp.concatenate(sums, axis=1)
            return 0

        lax.fori_loop(0, MARKS // block, body, 0)

    half_of(near_ref, 0)
    half_of(far_ref, MARKS)


def build(groups, block, spread, packed, near, far):
    rows = sum(groups) * OWN
    counts = [len(parts) for parts in packed]
    flat = [part for parts in packed for part in parts]
    return call(
        lambda *refs: build_kernel(counts, groups, block, *refs),
        [pltpu.VMEM((rows, 2 * MARKS), B16), jax.ShapeDtypeStruct((8, 2 * MARKS), F32)],
        [SMEM] + [VMEM] * (len(flat) + 2),
        [spread, *flat, near, far],
        "build",
        scratch=[pltpu.VMEM((rows, WIDTH), F32)],
        flops=4 * rows * 2 * MARKS * 512,
    )


def side_kernel(first, base, *refs):
    tiles, refs = refs[:TILES], refs[TILES:]
    half = WIDTH // 2
    if first:
        packed, refs = take(refs, [1] * 7 + [2])
        sums, (out_ref, wt_ref) = refs[:TILES], refs[TILES:]
        tails = [rest_of(parts, OWN + half, PACK) for parts in packed]
        for slot, parts in enumerate(packed):
            lanes = slice(slot * OWN, (slot + 1) * OWN)
            wt_ref[:half, lanes] = rest_of(parts, OWN, OWN + half, slice(0, OWN))
            wt_ref[half:, lanes] = rest_of(parts, OWN, OWN + half, slice(OWN, 2 * OWN))
    else:
        packed_ref, out_ref, wt_ref = refs
        for slot in range(EIGHT):
            wt_ref[:, slot * OWN : (slot + 1) * OWN] = packed_ref[slot_owner(slot), :WIDTH, :]
        tails = [packed_ref[source, WIDTH:, :] for source in range(EIGHT)]
    tail = tails[0].astype(F32)
    for more in tails[1:]:
        tail = tail + more.astype(F32)
    if first:
        tail = join_at(tail, 0)
        second = tail[:, OWN:]
        third = jnp.broadcast_to(jnp.sum(tail[:, :OWN], axis=1, keepdims=True), (1, PIECE))
    else:
        one, two = join_at(tail, 0), join_at(tail, 1)
        second = jnp.concatenate([one[:, :WIDTH], two[:, :WIDTH]], axis=1)
        third = jnp.concatenate([one[:, WIDTH:], two[:, WIDTH:]], axis=1)

    def body(index, _):
        lanes = pl.ds(pl.multiple_of(base + index * BLOCK, BLOCK), BLOCK)
        product, start = None, 0
        for tile in tiles:
            stop = start + tile.shape[0]
            term = dot(wt_ref[:, start:stop], tile[:, lanes], 1, 0)
            product, start = (term if product is None else product + term), stop
        if first:
            column = sums[0][:, lanes]
            for more in sums[1:]:
                column = column + more[:, lanes]
            column = jnp.sum(column, axis=0, keepdims=True)
        else:
            column = jnp.zeros((1, BLOCK), F32)
        for at in range(BLOCK // PIECE):
            lane = slice(at * PIECE, (at + 1) * PIECE)
            out_ref[BLOCK // PIECE * index + at, :WIDTH, :] = product[:, lane]
            out_ref[BLOCK // PIECE * index + at, WIDTH:, :] = stat_rows(column[:, lane], second, third)
        return 0

    lax.fori_loop(0, MARKS // BLOCK, body, 0)


def side_terms(first, base, tiles, more):
    return call(
        lambda *refs: side_kernel(first, base, *refs),
        [jax.ShapeDtypeStruct((EIGHT, WIDTH + 8, PIECE), F32)],
        [VMEM] * (TILES + len(more)),
        [*tiles, *more],
        "side_terms",
        scratch=[pltpu.VMEM((WIDTH, ROWS), B16)],
        flops=2 * ROWS * MARKS * WIDTH,
    )[0]


def pair_kernel(first, *refs):
    refs = refs[TILES:]
    if first:
        own_ref, other_ref, out_ref, pair_ref = refs
    else:
        own_ref, other_ref, before_ref, out_ref = refs
    stats = own_ref[0, WIDTH:, :] + other_ref[0, WIDTH:, :]
    second, third = stats[1:2], stats[2:3]
    rounded = columns_of([second[:, WIDTH:]])[:, 0:1]
    for piece in range(EIGHT):
        if first:
            column = own_ref[piece, WIDTH : WIDTH + 8, :] + other_ref[piece, WIDTH : WIDTH + 8, :]
            means = column[0:1] / third[:, 0:1]
            pair_ref[piece : piece + 1, :] = means
        else:
            means = before_ref[piece : piece + 1, :]
        side = own_ref[piece, :WIDTH, :] + other_ref[piece, :WIDTH, :]
        out_ref[piece, :WIDTH, :] = (side - rounded * means).astype(B16)
        out_ref[piece, WIDTH:, :] = tails_in_kernel([means, second, third])


def pair(first, tiles, *args):
    shapes = [jax.ShapeDtypeStruct((EIGHT, WIDTH + 16, PIECE), B16)]
    if first:
        shapes.append(jax.ShapeDtypeStruct((EIGHT, PIECE), F32))
    return call(
        lambda *refs: pair_kernel(first, *refs),
        shapes,
        [VMEM] * (TILES + len(args)),
        [*tiles, *args],
        "pair",
        flops=10**9,
    )


def centre_kernel(first, total_rows, *refs):
    refs = refs[TILES:]
    if first:
        terms_ref, out_ref, means_ref = refs
    else:
        terms_ref, before_ref, out_ref = refs
    tails = [terms_ref[group, WIDTH:, :] for group in range(EIGHT)]
    pairs = [join_at(tail, 0) for tail in tails]
    second = [join_at(tail, 1) for tail in tails]
    third = [join_at(tail, 2) for tail in tails]
    total, every = second[0], third[0]
    for group in range(1, EIGHT):
        total, every = total + second[group], every + third[group]
    columns = columns_of([row[:, WIDTH:] for row in second] + [total[:, :WIDTH], every[:, :WIDTH]])
    if first:
        means = third[0][:, 0:1] * pairs[0]
        for group in range(1, EIGHT):
            means = means + third[group][:, 0:1] * pairs[group]
        means = means / every[:, 0:1]
        means_ref[...] = jnp.broadcast_to(means, (8, PIECE))
    else:
        means = before_ref[0:1]
    side = terms_ref[0, :WIDTH, :].astype(F32) + columns[:, 0:1] * pairs[0]
    for group in range(1, EIGHT):
        side = side + (terms_ref[group, :WIDTH, :].astype(F32) + columns[:, group : group + 1] * pairs[group])
    totals = columns[:, EIGHT : EIGHT + 1]
    if first:
        side = side - totals * means
    else:
        squares = columns[:, EIGHT + 1 : EIGHT + 2]
        side = (side * UP - totals * means) / jnp.sqrt(squares / total_rows + 1e-06)
    side = side.astype(B16)
    for group in range(EIGHT):
        out_ref[group, :WIDTH, :] = side
        if first:
            out_ref[group, WIDTH:, :] = tail_in_kernel(means)


def centre(first, total_rows, tiles, *args):
    shapes = [jax.ShapeDtypeStruct((EIGHT, WIDTH + 16 * first, PIECE), B16)]
    if first:
        shapes.append(jax.ShapeDtypeStruct((8, PIECE), F32))
    return call(
        lambda *refs: centre_kernel(first, total_rows, *refs),
        shapes,
        [VMEM] * (TILES + len(args)),
        [*tiles, *args],
        "centre",
        flops=10**9,
    )


def image_kernel(base, *refs):
    tiles, (half_ref, means_ref), refs = refs[:TILES], refs[TILES : TILES + 2], refs[TILES + 2 :]
    if base:
        before_ref, out_ref, side_ref, tail_ref = refs
    else:
        out_ref, side_ref, tail_ref = refs
    for piece in range(EIGHT):
        lanes = slice(piece * PIECE, (piece + 1) * PIECE)
        side_ref[:, lanes] = half_ref[piece, :WIDTH, :]
        tail_ref[:, lanes] = means_ref[piece, WIDTH:, :]
    shift = dot(tail_ref[...], side_ref[...], 1, 1)
    shift = (shift[2:3] + shift[1:2]) + shift[0:1]
    slot = 0
    for tile in tiles:
        count = tile.shape[0] // OWN
        term = dot(tile[:, base : base + MARKS], side_ref[...], 1, 1) - shift
        if base:
            term = term + before_ref[slot * OWN : (slot + count) * OWN, :]
            for at in range(count):
                out_ref[slot_owner(slot + at)] = term[at * OWN : (at + 1) * OWN].astype(B16)
        else:
            out_ref[slot * OWN : (slot + count) * OWN, :] = term
        slot += count


def image_terms(tiles, half, means, before=None):
    if before is None:
        base, more, shape = 0, [], jax.ShapeDtypeStruct((ROWS, WIDTH), F32)
    else:
        base, more, shape = MARKS, [before], jax.ShapeDtypeStruct((EIGHT, OWN, WIDTH), B16)
    return call(
        lambda *refs: image_kernel(base, *refs),
        [shape],
        [VMEM] * (TILES + 2 + len(more)),
        [*tiles, half, means, *more],
        "image_terms",
        scratch=[pltpu.VMEM((WIDTH, MARKS), B16), pltpu.VMEM((16, MARKS), B16)],
        flops=2 * ROWS * MARKS * WIDTH,
    )[0]


def owner_kernel(last, *refs):
    if not last:
        refs = refs[TILES:]
    terms_ref, weight_ref, out_ref, *more = refs
    image = terms_ref[0].astype(F32)
    for member in range(1, EIGHT):
        image = image + terms_ref[member].astype(F32)
    weight = jnp.transpose(jnp.broadcast_to(weight_ref[0:1, :], (WIDTH, OWN)))
    image = weight * image
    squares = jnp.sum(image * image, axis=0, keepdims=True)
    if last:
        out_ref[...] = image
        more[0][...] = jnp.broadcast_to(squares, (8, WIDTH))
    else:
        product = weight * image
        totals = jnp.sum(product, axis=0, keepdims=True)
        body = (product * DOWN).astype(B16).astype(F32)
        rounded = jnp.sum(body, axis=0, keepdims=True)
        body = jnp.transpose(body).astype(B16)
        first = jnp.concatenate([totals, squares], axis=1)
        second = jnp.concatenate([rounded, jnp.zeros((1, OWN - WIDTH), F32)], axis=1)
        tail = tails_in_kernel([first, second])
        for member in range(EIGHT):
            out_ref[member, :WIDTH, :] = body
            out_ref[member, WIDTH:, :] = tail


def owner(last, tiles, terms, weight):
    if last:
        shapes = [jax.ShapeDtypeStruct((OWN, WIDTH), F32), jax.ShapeDtypeStruct((8, WIDTH), F32)]
        tiles = []
    else:
        shapes = [jax.ShapeDtypeStruct((EIGHT, WIDTH + 16, OWN), B16)]
    return call(
        lambda *refs: owner_kernel(last, *refs),
        shapes,
        [VMEM] * (len(tiles) + 2),
        [*tiles, terms, weight],
        "owner",
        flops=10**9,
    )


def exchange(payload, axes):
    return lax.all_to_all(payload, axes, 0, 0)


def swap_core(values):
    return lax.ppermute(values, "core", [(0, 1), (1, 0)])


def swap_z(values):
    return lax.ppermute(values, "zl", [(0, 1), (1, 0)])


def from_below(values):
    return lax.ppermute(values, "x", [(at, (at + 1) % 4) for at in range(4)])


def from_above(values):
    return lax.ppermute(values, "x", [(at, (at + 3) % 4) for at in range(4)])


def pack_kernel(rows_hbm, start_hbm, weight_hbm, out_ref, line_ref, rows_ref, start_ref, weight_ref, sems):
    copies = [
        pltpu.make_async_copy(rows_hbm, rows_ref, sems.at[0]),
        pltpu.make_async_copy(start_hbm, start_ref, sems.at[1]),
        pltpu.make_async_copy(weight_hbm, weight_ref, sems.at[2]),
    ]
    for copy in copies:
        copy.start()
    copies[0].wait()
    values = rows_ref[...].astype(F32)
    scale = lax.rsqrt(jnp.sum(values * values, axis=1, keepdims=True) + 1e-06)
    out_ref[:OWN, :] = (values * scale).astype(B16)
    copies[1].wait()
    copies[2].wait()
    weight = weight_ref[...]
    wide = jnp.transpose(jnp.broadcast_to(weight, (WIDTH, OWN)))
    line_ref[...] = jnp.broadcast_to(weight, (8, OWN))
    product = wide * start_ref[...]
    totals = jnp.sum(product, axis=0, keepdims=True)
    vectors = jnp.transpose(product).astype(B16)
    half = WIDTH // 2
    out_ref[OWN : OWN + half, :OWN] = vectors[:half]
    out_ref[OWN : OWN + half, OWN:] = vectors[half:]
    rounded = jnp.sum(product.astype(B16).astype(F32), axis=0, keepdims=True)
    out_ref[OWN + half :, :] = tail_in_kernel(jnp.concatenate([weight, totals, rounded], axis=1))


def pack(rows, start, weight):
    shapes = [pltpu.VMEM((PACK, rows.shape[1]), B16), jax.ShapeDtypeStruct((8, OWN), F32)]
    scratch = [
        pltpu.VMEM(rows.shape, B16),
        pltpu.VMEM(start.shape, F32),
        pltpu.VMEM(weight.shape, F32),
        pltpu.SemaphoreType.DMA((3,)),
    ]
    specs = [pl.BlockSpec(memory_space=pl.ANY)] * 3
    return call(pack_kernel, shapes, specs, [rows, start, weight], "pack", scratch=scratch, mib=54)


def slot_owner(slot):
    dx, dz = MOVES[slot]
    return (lax.axis_index("x") + dx) % 4 * 2 + (lax.axis_index("zl") + dz) % 2


def local(embeddings, landmarks, start_vectors, row_weight, spread):
    total_rows = embeddings.shape[0] * lax.axis_size(AXES)
    packed, weight = pack(embeddings, start_vectors, row_weight[None, :])
    below, above, across = from_below(packed), from_above(packed), swap_z(packed)
    near = unit(landmarks)
    far = unit(swap_core(landmarks))
    zero, sums_zero = build((1,), 2048, spread, [[packed]], near, far)
    sums_zero, across, above, below = lax.optimization_barrier((sums_zero, across, above, below))
    opposite, across_above, across_below = from_below(below), from_above(across), swap_z(below)
    one, sums_one = build((3,), 2048, spread, [[below], [above], [across]], near, far)
    sums_one, across_above, across_below, opposite = lax.optimization_barrier(
        (sums_one, across_above, across_below, opposite)
    )
    last = [from_above(across_above[:SPLIT]), swap_z(opposite[SPLIT:])]
    two, sums_two = build((3,), 2048, spread, [[opposite], [across_above], [across_below]], near, far)
    sums_two, *last = lax.optimization_barrier((sums_two, *last[::-1]))
    last = last[::-1]
    three, sums_three = build((1,), 2048, spread, [last], near, far)
    packs = [packed, below, above, across, opposite, across_above, across_below, *last]
    tiles = (zero, one, two, three)
    first = [*packs, sums_zero, sums_one, sums_two, sums_three]
    for step in range(ITERS):
        more = first if step == 0 else [vectors]
        other = swap_core(side_terms(step == 0, MARKS, tiles, more))
        own = side_terms(step == 0, 0, tiles, more)
        if step == 0:
            payload, pair_means = pair(True, tiles, own, other)
            sides, means = centre(True, total_rows, tiles, exchange(payload, MARK_AXES))
        else:
            (payload,) = pair(False, tiles, own, other, pair_means)
            (sides,) = centre(False, total_rows, tiles, exchange(payload, MARK_AXES), means)
        sides = exchange(sides, MARK_AXES)
        across_core = swap_core(sides)
        if step == 0:
            tails = (sides, across_core)
        parts = image_terms(tiles, sides, tails[0])
        parts = image_terms(tiles, across_core, tails[1], parts)
        parts = exchange(parts, ROW_AXES)
        if step + 1 < ITERS:
            (vectors,) = owner(False, tiles, parts, weight)
            vectors = exchange(vectors, ROW_AXES)
    image, squares = owner(True, tiles, parts, weight)
    count = lax.axis_size(AXES)
    every = exchange(jnp.broadcast_to(squares[:1][None], (count, 1, WIDTH)), AXES)
    scale = jnp.sqrt(jnp.sum(every[:, 0], axis=0) / total_rows + 1e-06)
    return image / scale[None, :]


def solution(mesh):
    fine = Mesh(mesh.devices.reshape(4, 2, 4, 2, 2), AXES)
    rows = P(AXES, None)
    in_specs = (rows, P(("x", "zl", "core"), None), rows, P(AXES), P())
    return jax.shard_map(local, mesh=fine, in_specs=in_specs, out_specs=rows, check_vma=False)
```

```python
import jax
import jax.numpy as jnp
from jax import lax
from jax.experimental import pallas as pl
from jax.experimental.pallas import tpu as pltpu
from jax.sharding import Mesh
from jax.sharding import PartitionSpec as P

ITERS = 2
AXES = ("y", "zh", "x", "zl", "core")
ROW_AXES = ("x", "zl")
MARK_AXES = ("y", "zh")
F32, B16 = jnp.float32, jnp.bfloat16
DOWN = 2.0**-20
UP = 2.0**20
LOG2E = 1.4426950408889634
VMEM = pl.BlockSpec(memory_space=pltpu.VMEM)
SMEM = pl.BlockSpec(memory_space=pltpu.SMEM)
OWN = 256
PIECE = 256
WIDTH = 128
MARKS = 2048
EIGHT = 8
ROWS = EIGHT * OWN
PACK = OWN + WIDTH // 2 + 16
BLOCK = 8 * PIECE
SPLIT = 160
TILES = 4
MOVES = [(0, 0), (3, 0), (1, 0), (0, 1), (2, 0), (1, 1), (3, 1), (2, 1)]


def params(mib):
    return pltpu.CompilerParams(vmem_limit_bytes=int(mib * 2**20))


def dot(left, right, left_dim, right_dim):
    dims = (((left_dim,), (right_dim,)), ((), ()))
    return lax.dot_general(left, right, dims, preferred_element_type=F32)


def parts_in_kernel(values):
    high = values.astype(B16)
    rest = values - high.astype(F32)
    mid = rest.astype(B16)
    low = (rest - mid.astype(F32)).astype(B16)
    return high.astype(F32), mid.astype(F32), low.astype(F32)


def tail_in_kernel(row):
    at = lax.broadcasted_iota(jnp.int32, (16, row.shape[1]), 0)
    high, mid, low = parts_in_kernel(row)
    zero = jnp.zeros((16, row.shape[1]), F32)
    block = jnp.where(at == 0, high, jnp.where(at == 1, mid, jnp.where(at == 2, low, zero)))
    return block.astype(B16)


def join_tail(block):
    block = block.astype(F32)
    return (block[2:3] + block[1:2]) + block[0:1]


def stat_rows(first, second, third):
    at = lax.broadcasted_iota(jnp.int32, (8, PIECE), 0)
    zero = jnp.zeros((8, PIECE), F32)
    return jnp.where(at == 0, first, jnp.where(at == 1, second, jnp.where(at == 2, third, zero)))


def tails_in_kernel(rows):
    at = lax.broadcasted_iota(jnp.int32, (16, rows[0].shape[1]), 0)
    block = jnp.zeros(at.shape, F32)
    for index, row in enumerate(rows):
        for part, value in enumerate(parts_in_kernel(row)):
            block = jnp.where(at == 3 * index + part, value, block)
    return block.astype(B16)


def join_at(block, index):
    block = block[3 * index : 3 * index + 3].astype(F32)
    return (block[2:3] + block[1:2]) + block[0:1]


def columns_of(rows):
    at = lax.broadcasted_iota(jnp.int32, (WIDTH, WIDTH), 0)
    block = jnp.zeros((WIDTH, WIDTH), F32)
    for index, row in enumerate(rows):
        block = jnp.where(at == index, row, block)
    return jnp.transpose(block)


def call(kernel, shapes, specs, args, name, scratch=(), flops=0, mib=24):
    cost = pl.CostEstimate(flops=flops, bytes_accessed=0, transcendentals=0)
    return pl.pallas_call(
        kernel,
        out_shape=shapes,
        in_specs=specs,
        out_specs=[VMEM] * len(shapes),
        scratch_shapes=list(scratch),
        compiler_params=params(mib),
        cost_estimate=cost,
        name=name,
    )(*args)


def rows_of(refs):
    if len(refs) == 1:
        return refs[0][:OWN, :]
    return jnp.concatenate([refs[0][...], refs[1][: OWN - SPLIT, :]], axis=0)


def rest_of(refs, start, stop, lanes=slice(None)):
    skip = 0 if len(refs) == 1 else SPLIT
    return refs[-1][start - skip : stop - skip, lanes]


def take(refs, counts):
    taken = []
    for count in counts:
        taken.append(refs[:count])
        refs = refs[count:]
    return taken, refs


def unit_kernel(in_ref, out_ref):
    block = 2 * OWN

    def body(index, _):
        rows = pl.ds(pl.multiple_of(index * block, block), block)
        values = in_ref[rows, :].astype(F32)
        scale = lax.rsqrt(jnp.sum(values * values, axis=1, keepdims=True) + 1e-06)
        out_ref[rows, :] = (values * scale).astype(B16)
        return 0

    lax.fori_loop(0, MARKS // block, body, 0)


def unit(values):
    shape = jax.ShapeDtypeStruct(values.shape, B16)
    return call(unit_kernel, [shape], [VMEM], [values], "unit", flops=2 * 10**9)[0]


def build_kernel(counts, groups, block, *refs):
    spread_ref = refs[0]
    packed, refs = take(refs[1:], counts)
    near_ref, far_ref, tile_ref, sums_ref, wide_ref = refs
    gamma = spread_ref[0] * LOG2E
    for source, parts in enumerate(packed):
        weight = join_tail(rest_of(parts, PACK - 16, PACK))[:, :OWN]
        column = jnp.transpose(jnp.broadcast_to(weight, (WIDTH, OWN)))
        wide_ref[source * OWN : (source + 1) * OWN, :] = column

    def half_of(marks_ref, base):
        def body(index, _):
            start = pl.multiple_of(index * block, block)
            marks = marks_ref[pl.ds(start, block), :]
            lanes = pl.ds(pl.multiple_of(base + start, block), block)
            sums = [jnp.zeros((8, WIDTH), F32) for _ in range(block // WIDTH)]
            first = 0
            for size in groups:
                rows = jnp.concatenate([rows_of(parts) for parts in packed[first : first + size]], axis=0)
                values = jnp.exp2(dot(rows, marks, 1, 1) * gamma)
                at = slice(first * OWN, (first + size) * OWN)
                tile_ref[at, lanes] = values.astype(B16)
                wide = wide_ref[at, :]
                for lane in range(block // WIDTH):
                    term = values[:, lane * WIDTH : (lane + 1) * WIDTH] * wide
                    sums[lane] = sums[lane] + jnp.sum(term.reshape(-1, 8, WIDTH), axis=0)
                first += size
            sums_ref[:, lanes] = jnp.concatenate(sums, axis=1)
            return 0

        lax.fori_loop(0, MARKS // block, body, 0)

    half_of(near_ref, 0)
    half_of(far_ref, MARKS)


def build(groups, block, spread, packed, near, far):
    rows = sum(groups) * OWN
    counts = [len(parts) for parts in packed]
    flat = [part for parts in packed for part in parts]
    return call(
        lambda *refs: build_kernel(counts, groups, block, *refs),
        [pltpu.VMEM((rows, 2 * MARKS), B16), jax.ShapeDtypeStruct((8, 2 * MARKS), F32)],
        [SMEM] + [VMEM] * (len(flat) + 2),
        [spread, *flat, near, far],
        "build",
        scratch=[pltpu.VMEM((rows, WIDTH), F32)],
        flops=4 * rows * 2 * MARKS * 512,
    )


def side_kernel(first, base, *refs):
    tiles, refs = refs[:TILES], refs[TILES:]
    half = WIDTH // 2
    if first:
        packed, refs = take(refs, [1] * 7 + [2])
        sums, (out_ref, wt_ref) = refs[:TILES], refs[TILES:]
        tails = [rest_of(parts, OWN + half, PACK) for parts in packed]
        for slot, parts in enumerate(packed):
            lanes = slice(slot * OWN, (slot + 1) * OWN)
            wt_ref[:half, lanes] = rest_of(parts, OWN, OWN + half, slice(0, OWN))
            wt_ref[half:, lanes] = rest_of(parts, OWN, OWN + half, slice(OWN, 2 * OWN))
    else:
        packed_ref, out_ref, wt_ref = refs
        for slot in range(EIGHT):
            wt_ref[:, slot * OWN : (slot + 1) * OWN] = packed_ref[slot_owner(slot), :WIDTH, :]
        tails = [packed_ref[source, WIDTH:, :] for source in range(EIGHT)]
    tail = tails[0].astype(F32)
    for more in tails[1:]:
        tail = tail + more.astype(F32)
    if first:
        tail = join_at(tail, 0)
        second = tail[:, OWN:]
        third = jnp.broadcast_to(jnp.sum(tail[:, :OWN], axis=1, keepdims=True), (1, PIECE))
    else:
        one, two = join_at(tail, 0), join_at(tail, 1)
        second = jnp.concatenate([one[:, :WIDTH], two[:, :WIDTH]], axis=1)
        third = jnp.concatenate([one[:, WIDTH:], two[:, WIDTH:]], axis=1)

    def body(index, _):
        lanes = pl.ds(pl.multiple_of(base + index * BLOCK, BLOCK), BLOCK)
        product, start = None, 0
        for tile in tiles:
            stop = start + tile.shape[0]
            term = dot(wt_ref[:, start:stop], tile[:, lanes], 1, 0)
            product, start = (term if product is None else product + term), stop
        if first:
            column = sums[0][:, lanes]
            for more in sums[1:]:
                column = column + more[:, lanes]
            column = jnp.sum(column, axis=0, keepdims=True)
        else:
            column = jnp.zeros((1, BLOCK), F32)
        for at in range(BLOCK // PIECE):
            lane = slice(at * PIECE, (at + 1) * PIECE)
            out_ref[BLOCK // PIECE * index + at, :WIDTH, :] = product[:, lane]
            out_ref[BLOCK // PIECE * index + at, WIDTH:, :] = stat_rows(column[:, lane], second, third)
        return 0

    lax.fori_loop(0, MARKS // BLOCK, body, 0)


def side_terms(first, base, tiles, more):
    return call(
        lambda *refs: side_kernel(first, base, *refs),
        [jax.ShapeDtypeStruct((EIGHT, WIDTH + 8, PIECE), F32)],
        [VMEM] * (TILES + len(more)),
        [*tiles, *more],
        "side_terms",
        scratch=[pltpu.VMEM((WIDTH, ROWS), B16)],
        flops=2 * ROWS * MARKS * WIDTH,
    )[0]


def pair_kernel(first, *refs):
    refs = refs[TILES:]
    if first:
        own_ref, other_ref, out_ref, pair_ref = refs
    else:
        own_ref, other_ref, before_ref, out_ref = refs
    stats = own_ref[0, WIDTH:, :] + other_ref[0, WIDTH:, :]
    second, third = stats[1:2], stats[2:3]
    rounded = columns_of([second[:, WIDTH:]])[:, 0:1]
    for piece in range(EIGHT):
        if first:
            column = own_ref[piece, WIDTH : WIDTH + 8, :] + other_ref[piece, WIDTH : WIDTH + 8, :]
            means = column[0:1] / third[:, 0:1]
            pair_ref[piece : piece + 1, :] = means
        else:
            means = before_ref[piece : piece + 1, :]
        side = own_ref[piece, :WIDTH, :] + other_ref[piece, :WIDTH, :]
        out_ref[piece, :WIDTH, :] = (side - rounded * means).astype(B16)
        out_ref[piece, WIDTH:, :] = tails_in_kernel([means, second, third])


def pair(first, tiles, *args):
    shapes = [jax.ShapeDtypeStruct((EIGHT, WIDTH + 16, PIECE), B16)]
    if first:
        shapes.append(jax.ShapeDtypeStruct((EIGHT, PIECE), F32))
    return call(
        lambda *refs: pair_kernel(first, *refs),
        shapes,
        [VMEM] * (TILES + len(args)),
        [*tiles, *args],
        "pair",
        flops=10**9,
    )


def centre_kernel(first, total_rows, *refs):
    refs = refs[TILES:]
    if first:
        terms_ref, out_ref, means_ref = refs
    else:
        terms_ref, before_ref, out_ref = refs
    tails = [terms_ref[group, WIDTH:, :] for group in range(EIGHT)]
    pairs = [join_at(tail, 0) for tail in tails]
    second = [join_at(tail, 1) for tail in tails]
    third = [join_at(tail, 2) for tail in tails]
    total, every = second[0], third[0]
    for group in range(1, EIGHT):
        total, every = total + second[group], every + third[group]
    columns = columns_of([row[:, WIDTH:] for row in second] + [total[:, :WIDTH], every[:, :WIDTH]])
    if first:
        means = third[0][:, 0:1] * pairs[0]
        for group in range(1, EIGHT):
            means = means + third[group][:, 0:1] * pairs[group]
        means = means / every[:, 0:1]
        means_ref[...] = jnp.broadcast_to(means, (8, PIECE))
    else:
        means = before_ref[0:1]
    side = terms_ref[0, :WIDTH, :].astype(F32) + columns[:, 0:1] * pairs[0]
    for group in range(1, EIGHT):
        side = side + (terms_ref[group, :WIDTH, :].astype(F32) + columns[:, group : group + 1] * pairs[group])
    totals = columns[:, EIGHT : EIGHT + 1]
    if first:
        side = side - totals * means
    else:
        squares = columns[:, EIGHT + 1 : EIGHT + 2]
        side = (side * UP - totals * means) / jnp.sqrt(squares / total_rows + 1e-06)
    side = side.astype(B16)
    for group in range(EIGHT):
        out_ref[group, :WIDTH, :] = side
        if first:
            out_ref[group, WIDTH:, :] = tail_in_kernel(means)


def centre(first, total_rows, tiles, *args):
    shapes = [jax.ShapeDtypeStruct((EIGHT, WIDTH + 16 * first, PIECE), B16)]
    if first:
        shapes.append(jax.ShapeDtypeStruct((8, PIECE), F32))
    return call(
        lambda *refs: centre_kernel(first, total_rows, *refs),
        shapes,
        [VMEM] * (TILES + len(args)),
        [*tiles, *args],
        "centre",
        flops=10**9,
    )


def image_kernel(base, *refs):
    tiles, (half_ref, means_ref), refs = refs[:TILES], refs[TILES : TILES + 2], refs[TILES + 2 :]
    if base:
        before_ref, out_ref, side_ref, tail_ref = refs
    else:
        out_ref, side_ref, tail_ref = refs
    for piece in range(EIGHT):
        lanes = slice(piece * PIECE, (piece + 1) * PIECE)
        side_ref[:, lanes] = half_ref[piece, :WIDTH, :]
        tail_ref[:, lanes] = means_ref[piece, WIDTH:, :]
    shift = dot(tail_ref[...], side_ref[...], 1, 1)
    shift = (shift[2:3] + shift[1:2]) + shift[0:1]
    slot = 0
    for tile in tiles:
        count = tile.shape[0] // OWN
        term = dot(tile[:, base : base + MARKS], side_ref[...], 1, 1) - shift
        if base:
            term = term + before_ref[slot * OWN : (slot + count) * OWN, :]
            for at in range(count):
                out_ref[slot_owner(slot + at)] = term[at * OWN : (at + 1) * OWN].astype(B16)
        else:
            out_ref[slot * OWN : (slot + count) * OWN, :] = term
        slot += count


def image_terms(tiles, half, means, before=None):
    if before is None:
        base, more, shape = 0, [], jax.ShapeDtypeStruct((ROWS, WIDTH), F32)
    else:
        base, more, shape = MARKS, [before], jax.ShapeDtypeStruct((EIGHT, OWN, WIDTH), B16)
    return call(
        lambda *refs: image_kernel(base, *refs),
        [shape],
        [VMEM] * (TILES + 2 + len(more)),
        [*tiles, half, means, *more],
        "image_terms",
        scratch=[pltpu.VMEM((WIDTH, MARKS), B16), pltpu.VMEM((16, MARKS), B16)],
        flops=2 * ROWS * MARKS * WIDTH,
    )[0]


def owner_kernel(last, *refs):
    if not last:
        refs = refs[TILES:]
    terms_ref, weight_ref, out_ref, *more = refs
    image = terms_ref[0].astype(F32)
    for member in range(1, EIGHT):
        image = image + terms_ref[member].astype(F32)
    weight = jnp.transpose(jnp.broadcast_to(weight_ref[0:1, :], (WIDTH, OWN)))
    image = weight * image
    squares = jnp.sum(image * image, axis=0, keepdims=True)
    if last:
        out_ref[...] = image
        more[0][...] = jnp.broadcast_to(squares, (8, WIDTH))
    else:
        product = weight * image
        totals = jnp.sum(product, axis=0, keepdims=True)
        body = (product * DOWN).astype(B16).astype(F32)
        rounded = jnp.sum(body, axis=0, keepdims=True)
        body = jnp.transpose(body).astype(B16)
        first = jnp.concatenate([totals, squares], axis=1)
        second = jnp.concatenate([rounded, jnp.zeros((1, OWN - WIDTH), F32)], axis=1)
        tail = tails_in_kernel([first, second])
        for member in range(EIGHT):
            out_ref[member, :WIDTH, :] = body
            out_ref[member, WIDTH:, :] = tail


def owner(last, tiles, terms, weight):
    if last:
        shapes = [jax.ShapeDtypeStruct((OWN, WIDTH), F32), jax.ShapeDtypeStruct((8, WIDTH), F32)]
        tiles = []
    else:
        shapes = [jax.ShapeDtypeStruct((EIGHT, WIDTH + 16, OWN), B16)]
    return call(
        lambda *refs: owner_kernel(last, *refs),
        shapes,
        [VMEM] * (len(tiles) + 2),
        [*tiles, terms, weight],
        "owner",
        flops=10**9,
    )


def exchange(payload, axes):
    return lax.all_to_all(payload, axes, 0, 0)


def swap_core(values):
    return lax.ppermute(values, "core", [(0, 1), (1, 0)])


def swap_z(values):
    return lax.ppermute(values, "zl", [(0, 1), (1, 0)])


def from_below(values):
    return lax.ppermute(values, "x", [(at, (at + 1) % 4) for at in range(4)])


def from_above(values):
    return lax.ppermute(values, "x", [(at, (at + 3) % 4) for at in range(4)])


def pack_kernel(rows_hbm, start_hbm, weight_hbm, out_ref, line_ref, rows_ref, start_ref, weight_ref, sems):
    copies = [
        pltpu.make_async_copy(rows_hbm, rows_ref, sems.at[0]),
        pltpu.make_async_copy(start_hbm, start_ref, sems.at[1]),
        pltpu.make_async_copy(weight_hbm, weight_ref, sems.at[2]),
    ]
    for copy in copies:
        copy.start()
    copies[0].wait()
    values = rows_ref[...].astype(F32)
    scale = lax.rsqrt(jnp.sum(values * values, axis=1, keepdims=True) + 1e-06)
    out_ref[:OWN, :] = (values * scale).astype(B16)
    copies[1].wait()
    copies[2].wait()
    weight = weight_ref[...]
    wide = jnp.transpose(jnp.broadcast_to(weight, (WIDTH, OWN)))
    line_ref[...] = jnp.broadcast_to(weight, (8, OWN))
    product = wide * start_ref[...]
    totals = jnp.sum(product, axis=0, keepdims=True)
    vectors = jnp.transpose(product).astype(B16)
    half = WIDTH // 2
    out_ref[OWN : OWN + half, :OWN] = vectors[:half]
    out_ref[OWN : OWN + half, OWN:] = vectors[half:]
    rounded = jnp.sum(product.astype(B16).astype(F32), axis=0, keepdims=True)
    out_ref[OWN + half :, :] = tail_in_kernel(jnp.concatenate([weight, totals, rounded], axis=1))


def pack(rows, start, weight):
    shapes = [pltpu.VMEM((PACK, rows.shape[1]), B16), jax.ShapeDtypeStruct((8, OWN), F32)]
    scratch = [
        pltpu.VMEM(rows.shape, B16),
        pltpu.VMEM(start.shape, F32),
        pltpu.VMEM(weight.shape, F32),
        pltpu.SemaphoreType.DMA((3,)),
    ]
    specs = [pl.BlockSpec(memory_space=pl.ANY)] * 3
    return call(pack_kernel, shapes, specs, [rows, start, weight], "pack", scratch=scratch, mib=54)


def slot_owner(slot):
    dx, dz = MOVES[slot]
    return (lax.axis_index("x") + dx) % 4 * 2 + (lax.axis_index("zl") + dz) % 2


def local(embeddings, landmarks, start_vectors, row_weight, spread):
    total_rows = embeddings.shape[0] * lax.axis_size(AXES)
    packed, weight = pack(embeddings, start_vectors, row_weight[None, :])
    below, above, across = from_below(packed), from_above(packed), swap_z(packed)
    near = unit(landmarks)
    far = unit(swap_core(landmarks))
    zero, sums_zero = build((1,), 2048, spread, [[packed]], near, far)
    sums_zero, across, above, below = lax.optimization_barrier((sums_zero, across, above, below))
    opposite, across_above, across_below = from_below(below), from_above(across), swap_z(below)
    one, sums_one = build((3,), 2048, spread, [[below], [above], [across]], near, far)
    sums_one, across_above, across_below, opposite = lax.optimization_barrier(
        (sums_one, across_above, across_below, opposite)
    )
    last = [from_above(across_above[:SPLIT]), swap_z(opposite[SPLIT:])]
    two, sums_two = build((3,), 2048, spread, [[opposite], [across_above], [across_below]], near, far)
    sums_two, *last = lax.optimization_barrier((sums_two, *last[::-1]))
    last = last[::-1]
    three, sums_three = build((1,), 2048, spread, [last], near, far)
    packs = [packed, below, above, across, opposite, across_above, across_below, *last]
    tiles = (zero, one, two, three)
    first = [*packs, sums_zero, sums_one, sums_two, sums_three]
    for step in range(ITERS):
        more = first if step == 0 else [vectors]
        other = swap_core(side_terms(step == 0, MARKS, tiles, more))
        own = side_terms(step == 0, 0, tiles, more)
        if step == 0:
            payload, pair_means = pair(True, tiles, own, other)
            sides, means = centre(True, total_rows, tiles, exchange(payload, MARK_AXES))
        else:
            (payload,) = pair(False, tiles, own, other, pair_means)
            (sides,) = centre(False, total_rows, tiles, exchange(payload, MARK_AXES), means)
        sides = exchange(sides, MARK_AXES)
        across_core = swap_core(sides)
        if step == 0:
            tails = (sides, across_core)
        parts = image_terms(tiles, sides, tails[0])
        parts = image_terms(tiles, across_core, tails[1], parts)
        parts = exchange(parts, ROW_AXES)
        if step + 1 < ITERS:
            (vectors,) = owner(False, tiles, parts, weight)
            vectors = exchange(vectors, ROW_AXES)
    image, squares = owner(True, tiles, parts, weight)
    count = lax.axis_size(AXES)
    every = exchange(jnp.broadcast_to(squares[:1][None], (count, 1, WIDTH)), AXES[::-1])
    scale = jnp.sqrt(jnp.sum(every[:, 0], axis=0) / total_rows + 1e-06)
    return image / scale[None, :]


def solution(mesh):
    fine = Mesh(mesh.devices.reshape(4, 2, 4, 2, 2), AXES)
    rows = P(AXES, None)
    in_specs = (rows, P(("x", "zl", "core"), None), rows, P(AXES), P())
    return jax.shard_map(local, mesh=fine, in_specs=in_specs, out_specs=rows, check_vma=False)
```
